32 devices in a mesh: group: 8 (over z, x), narrow: 4 (over y, core).
Axes of the slice: x: 2, y: 2, z: 4, core: 2. Of those that a mesh axis runs over, the one named last changes fastest.
Arguments:
- series_values: float32 [128, 1024], P(('group', 'narrow')), may hold values from -60 to 60, as said below
- observed: int32 [128, 1024], P(('group', 'narrow')), may hold values 0 or 1
- lag_steps: int32 [84], replicated, may hold values from 1 to 511
- lag_flags: int32 [84], replicated, may hold values 0 or 1
- dataset_ids: int32 [128], P(('group', 'narrow')), may hold values from 0 to 3
- in_proj: float32 [86, 144], replicated, may hold values from -0.625 to 0.625
- gain_attn: float32 [144], replicated, may hold values from 0.5 to 1.5
- query_proj: float32 [144, 144], replicated, may hold values from -0.5 to 0.5
- key_proj: float32 [144, 144], replicated, may hold values from -0.5 to 0.5
- value_proj: float32 [144, 144], replicated, may hold values from -0.5 to 0.5
- out_proj: float32 [144, 144], replicated, may hold values from -1 to 1
- gain_ffn: float32 [144], replicated, may hold values from 0.5 to 1.5
- gate_proj: float32 [144, 384], replicated, may hold values from -0.5 to 0.5
- up_proj: float32 [144, 384], replicated, may hold values from -0.5 to 0.5
- down_proj: float32 [384, 144], replicated, may hold values from -0.625 to 0.625
- cotangent: float32 [128, 1024, 144], P(('group', 'narrow')), may hold values from -6 to 6
Outputs:
- activations: float32 [128, 1024, 144], P(('group', 'narrow'))
- input_grad: float32 [128, 1024, 144], P(('group', 'narrow'))
- grad_in_proj: float32 [86, 144], P(None, 'narrow')
- grad_gain_attn: float32 [144], P('narrow')
- grad_query_proj: float32 [144, 144], P('narrow')
- grad_key_proj: float32 [144, 144], P('narrow')
- grad_value_proj: float32 [144, 144], P('narrow')
- grad_out_proj: float32 [144, 144], P('narrow')
- grad_gain_ffn: float32 [144], P('narrow')
- grad_gate_proj: float32 [144, 384], P(None, 'narrow')
- grad_up_proj: float32 [144, 384], P(None, 'narrow')
- grad_down_proj: float32 [384, 144], P('narrow')
The draws below stay inside these ranges and needn't reach their ends.
Inputs may be any that keep to these rules, and one draw needn't show every extreme that they name: `series_values`: raw series values; each series has its own magnitude.
All inputs are finite; a program needn't handle non-finite values. No bound on the sum of `observed` on one device may be relied on, other than what follows from the above.
Results may differ from the reference program's by a relative error of at most 0.0003.
Values sent between devices are 32-bit elements; how exact they have to be, the bound alone decides.
A program may use at most 640 MiB of HBM per device.

```python
import math
import jax
import jax.numpy as jnp
from jax import lax

D = 144
HEADS = 9
HD = 16
FF = 384
NLAG = 84
DSETS = 4
STEPS = 1024
NF = 86
SERIES = 128
N_GROUP = 8


def draw_series_values(key, part):
    key = jax.random.fold_in(key, 11)
    key_scale, key_noise, key_level = jax.random.split(key, 3)
    row_scale = jnp.exp(jax.random.uniform(key_scale, (SERIES, 1), jnp.float32, 0.0, math.log(10.0)))
    level = jax.random.uniform(key_level, (SERIES, 1), jnp.float32, -1.0, 1.0)
    noise = jnp.clip(jax.random.normal(key_noise, (SERIES, STEPS), jnp.float32), -4.0, 4.0)
    return (row_scale * (noise + 0.5 * level)).astype(jnp.float32)


def set_ends(drawn, key, smallest, largest):
    longest = drawn.shape.index(max(drawn.shape))
    spots = []
    for shift in (0, 1):
        where = [jax.random.randint(jax.random.fold_in(key, axis), (), 0, length) for axis, length in enumerate(drawn.shape)]
        where[longest] = (where[longest] + shift) % drawn.shape[longest]
        spots.append(tuple(where))
    return drawn.at[spots[0]].set(smallest).at[spots[1]].set(largest)


def level_of(key, shape, cuts, low, top_value):
    def one(axis_at, blocks):
        draws = jax.random.uniform(jax.random.fold_in(jax.random.fold_in(key, 6), axis_at), (blocks,), jnp.float32, low / len(cuts), top_value / len(cuts))
        return jnp.repeat(jnp.exp(draws), shape[axis_at] // blocks).reshape((-1,) + (1,) * (len(shape) - axis_at - 1))

    loudness = one(*cuts[0])
    for cut in cuts[1:]:
        loudness = loudness * one(*cut)
    return loudness


def bell_draw(stream_key, dims, width, most, cuts=(), kind=jnp.bfloat16):
    drawn = width * jax.random.normal(stream_key, dims, jnp.float32)
    if cuts:
        drawn = drawn * level_of(stream_key, dims, cuts, -0.22, 0.18)
    return jnp.clip(drawn, -most, most).astype(kind)


def setup_inputs(seed: int = 0) -> dict:
    streams_of = jax.random.split(jax.random.key(seed), 17)
    return {
        "series_values": draw_series_values(jax.random.fold_in(streams_of[16], 71), 0),
        "observed": set_ends((jax.random.randint(streams_of[1], (SERIES, STEPS), 0, 5) < 4).astype(jnp.int32), jax.random.fold_in(streams_of[1], 1), 0, 1),
        "lag_steps": set_ends(jax.random.randint(streams_of[2], (NLAG,), 1, STEPS // 2), jax.random.fold_in(streams_of[2], 1), 1, (STEPS // 2) - 1).astype(jnp.int32),
        "lag_flags": set_ends((jax.random.randint(streams_of[3], (NLAG,), 0, 2) < 1).astype(jnp.int32), jax.random.fold_in(streams_of[3], 1), 0, 1),
        "dataset_ids": set_ends(jax.random.randint(streams_of[4], (SERIES,), 0, DSETS), jax.random.fold_in(streams_of[4], 1), 0, DSETS - 1).astype(jnp.int32),
        "in_proj": bell_draw(streams_of[5], (NF, D), NF ** -0.5, 0.625, (), jnp.float32),
        "gain_attn": jnp.clip(1.0 + 0.1 * jax.random.normal(streams_of[6], (D,), jnp.float32), 0.5, 1.5),
        "query_proj": bell_draw(streams_of[7], (D, D), D ** -0.5, 0.5, (), jnp.float32),
        "key_proj": bell_draw(streams_of[8], (D, D), D ** -0.5, 0.5, (), jnp.float32),
        "value_proj": bell_draw(streams_of[9], (D, D), D ** -0.5, 0.5, (), jnp.float32),
        "out_proj": bell_draw(streams_of[10], (D, D), (D // 4) ** -0.5, 1.0, (), jnp.float32),
        "gain_ffn": jnp.clip(1.0 + 0.1 * jax.random.normal(streams_of[11], (D,), jnp.float32), 0.5, 1.5),
        "gate_proj": bell_draw(streams_of[12], (D, FF), D ** -0.5, 0.5, (), jnp.float32),
        "up_proj": bell_draw(streams_of[13], (D, FF), D ** -0.5, 0.5, (), jnp.float32),
        "down_proj": bell_draw(streams_of[14], (FF, D), (FF // 4) ** -0.5, 0.625, (), jnp.float32),
        "cotangent": bell_draw(streams_of[15], (SERIES, STEPS, D), 1.0, 6.0, ((0, 32),), jnp.float32),
    }


@jax.custom_vjp
def low(v):
    return lax.optimization_barrier(v.astype(jnp.bfloat16)).astype(jnp.float32)

@jax.custom_vjp
def low_back(v):
    return v

def low_keep(v):
    return (low(v), None)

def low_pass(kept, grad):
    return (grad,)

def back_keep(v):
    return (v, None)

def back_low(kept, grad):
    return (low(grad),)
low.defvjp(low_keep, low_pass)
low_back.defvjp(back_keep, back_low)
NORM_EPS = 1e-05
SCALE_EPS = 1e-05

def matmul_high(left, right):
    return jnp.dot(left, right, precision=lax.Precision.HIGHEST, preferred_element_type=jnp.float32)

def rms_scale(hidden, gain):
    return hidden * lax.rsqrt(lax.optimization_barrier(jnp.mean(hidden * hidden, axis=-1, keepdims=True)) + NORM_EPS) * gain

def rotate_pairs(tensor, cosine, sine):
    half_width = tensor.shape[-1] // 2
    first_half = tensor[..., :half_width]
    second_half = tensor[..., half_width:]
    return jnp.concatenate([first_half * cosine - second_half * sine, first_half * sine + second_half * cosine], axis=-1)

def head_attention(query_head, key_head, value_head):
    length = query_head.shape[0]
    scores = matmul_high(query_head, key_head.T) * query_head.shape[1] ** (-0.5)
    rows_idx = lax.broadcasted_iota(jnp.int32, (length, length), 0)
    cols_idx = lax.broadcasted_iota(jnp.int32, (length, length), 1)
    scores = jnp.where(rows_idx >= cols_idx, scores, -1e+30)
    highest = lax.optimization_barrier(jnp.max(scores, axis=1, keepdims=True))
    weights = jnp.exp(scores - highest)
    denominator = lax.optimization_barrier(jnp.sum(weights, axis=1, keepdims=True))
    return matmul_high(weights / denominator, value_head)

def series_forward(params, features, offset):
    in_proj, gain_attn, query_proj, key_proj, value_proj, out_proj, gain_ffn, gate_proj, up_proj, down_proj = params
    length = features.shape[0]
    block_input = matmul_high(features, in_proj) + offset
    normed = rms_scale(block_input, gain_attn)
    queries = matmul_high(normed, query_proj).reshape(length, HEADS, HD)
    key_rows = matmul_high(normed, key_proj).reshape(length, HEADS, HD)
    value_rows = matmul_high(normed, value_proj).reshape(length, HEADS, HD)
    positions = jnp.arange(length).astype(jnp.float32)
    freqs = 10000.0 ** (-jnp.arange(HD // 2).astype(jnp.float32) * 2.0 / HD)
    angles = positions[:, None] * freqs[None, :]
    cosine = jnp.cos(angles)[:, None, :]
    sine = jnp.sin(angles)[:, None, :]
    queries = rotate_pairs(queries, cosine, sine)
    key_rows = rotate_pairs(key_rows, cosine, sine)
    attend = jax.checkpoint(head_attention)
    mixed = lax.map(lambda triple: attend(triple[0], triple[1], triple[2]), (jnp.transpose(queries, (1, 0, 2)), jnp.transpose(key_rows, (1, 0, 2)), jnp.transpose(value_rows, (1, 0, 2))))
    mixed = jnp.transpose(mixed, (1, 0, 2)).reshape(length, HEADS * HD)
    attended = block_input + matmul_high(mixed, out_proj)
    normed_two = rms_scale(attended, gain_ffn)
    gate = matmul_high(normed_two, gate_proj)
    upward = matmul_high(normed_two, up_proj)
    return attended + matmul_high(jax.nn.silu(gate) * upward, down_proj)

def build_features(values, observed, series_scale, lag_steps, lag_flags):
    steps_count = values.shape[1]
    positions = jnp.arange(steps_count).astype(jnp.int32)
    source = positions[:, None] - lag_steps[None, :]
    inside = (source >= 0).astype(jnp.int32)
    clipped = jnp.maximum(source, 0).astype(jnp.int32)
    scaled = values / series_scale[:, None]
    lagged = jnp.take(scaled, clipped, axis=1)
    seen = (jnp.take(observed, clipped, axis=1) * inside[None, :, :]).astype(jnp.float32)
    lag_part = lagged * seen
    missing = lax.optimization_barrier(jnp.sum((1.0 - seen) * lag_flags.astype(jnp.float32)[None, None, :], axis=2, keepdims=True)) * lag_steps.shape[0] ** (-0.5)
    log_scale = jnp.broadcast_to(jnp.log(series_scale)[:, None, None], missing.shape)
    return jnp.concatenate([lag_part, log_scale, missing], axis=2)

def reference(series_values, observed, lag_steps, lag_flags, dataset_ids, in_proj, gain_attn, query_proj, key_proj, value_proj, out_proj, gain_ffn, gate_proj, up_proj, down_proj, cotangent):
    observed_f = observed.astype(jnp.float32)
    magnitude = lax.optimization_barrier(jnp.sum(jnp.abs(series_values) * observed_f, axis=1))
    counted = lax.optimization_barrier(jnp.sum(observed_f, axis=1))
    onehot = (dataset_ids[:, None] == jnp.arange(DSETS).astype(jnp.int32)[None, :]).astype(jnp.float32)
    grouped = onehot.reshape(N_GROUP, SERIES // N_GROUP, DSETS)
    magnitude_sets = lax.optimization_barrier(jnp.sum(grouped * magnitude.reshape(N_GROUP, SERIES // N_GROUP, 1), axis=1))
    count_sets = lax.optimization_barrier(jnp.sum(grouped * counted.reshape(N_GROUP, SERIES // N_GROUP, 1), axis=1))
    set_scale = magnitude_sets / jnp.maximum(count_sets, 1.0) + SCALE_EPS
    series_scale = lax.optimization_barrier(jnp.sum(grouped * set_scale[:, None, :], axis=2)).reshape(SERIES)
    features = build_features(series_values, observed, series_scale, lag_steps, lag_flags)
    params = (in_proj, gain_attn, query_proj, key_proj, value_proj, out_proj, gain_ffn, gate_proj, up_proj, down_proj)

    def one_series(running, series_item):
        feature_rows, cot_rows = series_item
        offset = jnp.zeros((feature_rows.shape[0], in_proj.shape[1]), jnp.float32)
        outputs, pullback = jax.vjp(lambda weights, shift: series_forward(weights, feature_rows, shift), params, offset)
        grad_params, grad_input = pullback(cot_rows)
        running = jax.tree.map(lambda accum, extra: accum + extra, running, grad_params)
        return (running, (outputs, grad_input))
    zeros = jax.tree.map(jnp.zeros_like, params)
    totals, (activations, input_grad) = lax.scan(one_series, zeros, (features, cotangent))
    return (activations, input_grad, totals[0], totals[1], totals[2], totals[3], totals[4], totals[5], totals[6], totals[7], totals[8], totals[9])
```

```python
import functools

import jax
import jax.numpy as jnp
import numpy as np
from jax import lax
from jax.experimental import pallas as pl
from jax.experimental.pallas import tpu as pltpu
from jax.sharding import PartitionSpec as P

HEADS = 9
HD = 16
DSETS = 4
FPAD = 96
QB = 256

NORM_EPS = 1e-05
SCALE_EPS = 1e-05
LOG2E = 1.4426950408889634
LN2 = 0.6931471805599453

F32 = jnp.float32
BF16 = jnp.bfloat16


def nn(left, right):
    return lax.dot_general(left, right, (((1,), (0,)), ((), ())), preferred_element_type=F32)


def nt(left, right):
    return lax.dot_general(left, right, (((1,), (1,)), ((), ())), preferred_element_type=F32)


def split(x):
    hi = x.astype(BF16)
    return hi, (x - hi.astype(F32)).astype(BF16)


def split3(x):
    hi = x.astype(BF16)
    rest = x - hi.astype(F32)
    mid = rest.astype(BF16)
    return hi, mid, (rest - mid.astype(F32)).astype(BF16)


def cat3(x):
    hi, lo = split(x)
    return jnp.concatenate([hi, hi, lo], axis=0)


def weight_cat(w):
    hi, lo = split(w)
    hi, lo = hi.astype(F32), lo.astype(F32)
    return jnp.concatenate([hi, lo, hi], axis=0).T.astype(BF16)


def weight_stack(w):
    hi, lo = split(w)
    return jnp.concatenate([hi, lo], axis=0)


def mm_stack(stack, x):
    m = stack.shape[0] // 2
    hi, lo = split(x)
    both = nn(stack, hi)
    return both[:m] + both[m:] + nn(stack[:m], lo)


def outer_sum(left, right):
    m = left.shape[0]
    lh, ll = split(left)
    rh, rl = split(right)
    both = nt(jnp.concatenate([lh, ll], axis=0), rh)
    return both[:m] + both[m:] + nt(lh, rl)


def column(row):
    n = row.shape[0]
    return jnp.broadcast_to(row[None, :], (8, n)).T[:, :1]


def lane_fold(x):
    total = x[:, :128]
    for i in range(1, x.shape[1] // 128):
        total = total + x[:, i * 128 : (i + 1) * 128]
    return total


def rotate(x, cos, sin):
    t = x.shape[1]
    pairs = x.reshape(HEADS, 2, HD // 2, t)
    a, b = pairs[:, 0], pairs[:, 1]
    first = a * cos - b * sin
    second = a * sin + b * cos
    return jnp.stack([first, second], axis=1).reshape(HEADS * HD, t)


def accumulate(step, ref, value):
    @pl.when(step == 0)
    def _():
        ref[...] = value

    @pl.when(step != 0)
    def _():
        ref[...] += value


def forward_kernel(
    lag_ref, flag_ref, scale_ref, vals_ref, obs_ref, in_ref, ga_ref, wq_ref, wk_ref, wv_ref, wo_ref, gf_ref,
    wg_ref, wu_ref, wd_ref, cos_ref, sin_ref, cot_ref,
    act_ref, q_ref, k_ref, v_ref, dm_ref, st_ref, da_ref, x_ref, f_ref, b1_ref,
    feat, w_in, w_qkv, w_out, w_gu, w_down, w_dh, w_dn, w_dm, gains, g_gu, g_down, g_out, g_gf,
):
    step = pl.program_id(0)
    t = vals_ref.shape[1]
    d = cot_ref.shape[1]
    nlag = lag_ref.shape[0]
    ff = wg_ref.shape[1]
    n_series = vals_ref.shape[0]

    @pl.when(step == 0)
    def _():
        nf = in_ref.shape[1]
        w_in_rows = jnp.concatenate([in_ref[...].T, jnp.zeros((FPAD - nf, d), F32)], axis=0)
        w_in[...] = weight_cat(w_in_rows)
        for i, ref in enumerate((wq_ref, wk_ref, wv_ref)):
            w_qkv[i * d : (i + 1) * d, :] = weight_cat(ref[...])
        w_out[...] = weight_cat(wo_ref[...])
        w_gu[:ff, :] = weight_cat(wg_ref[...])
        w_gu[ff:, :] = weight_cat(wu_ref[...])
        w_down[...] = weight_stack(wd_ref[...])
        w_dh[...] = weight_cat(wd_ref[...])
        w_dn[:, :ff] = weight_stack(wg_ref[...])
        w_dn[:, ff:] = weight_stack(wu_ref[...])
        w_dm[...] = weight_cat(wo_ref[...].T)
        gains[:, :1] = column(ga_ref[...])
        gains[:, 1:2] = column(gf_ref[...])

        obs = obs_ref[...].astype(F32)
        both = jnp.concatenate([vals_ref[...] * obs, obs], axis=0)
        lanes = lax.broadcasted_iota(jnp.int32, both.shape, 1)
        feat[...] = jnp.zeros_like(feat)

        def one_lag(j, missing):
            lag = lag_ref[j]
            moved = jnp.where(lanes >= lag, pltpu.roll(both, lag, 1), 0.0)
            for s in range(n_series):
                feat[s, pl.ds(j, 1), :] = moved[s : s + 1] / scale_ref[s]
            return missing + flag_ref[j].astype(F32) * (1.0 - moved[n_series:])

        missing = lax.fori_loop(0, nlag, one_lag, jnp.zeros((n_series, t), F32))
        for s in range(n_series):
            feat[s, nlag : nlag + 1, :] = jnp.log(jnp.full((1, t), scale_ref[s], F32))
            feat[s, nlag + 1 : nlag + 2, :] = missing[s : s + 1] * nlag**-0.5

    cos, sin = cos_ref[...], sin_ref[...]
    gain_attn, gain_ffn = gains[:, :1], gains[:, 1:2]
    feats = feat[step]
    f_ref[0] = feats
    x = nn(w_in[...], cat3(feats))
    x_ref[0] = x
    normed = x * lax.rsqrt(jnp.mean(x * x, axis=0, keepdims=True) + NORM_EPS) * gain_attn
    qkv = nn(w_qkv[...], cat3(normed))
    q = rotate(qkv[:d], cos, sin) * (HD**-0.5 * LOG2E)
    k = rotate(qkv[d : 2 * d], cos, sin)
    v = qkv[2 * d :]
    q_ref[0] = q
    k_ref[0] = k
    v_ref[0] = v

    st_ref[0] = jnp.zeros(st_ref.shape[1:], F32)
    causal = lax.broadcasted_iota(jnp.int32, (QB, QB), 0) <= lax.broadcasted_iota(jnp.int32, (QB, QB), 1)
    mixed_rows = []
    for h in range(HEADS):
        rows = slice(h * HD, (h + 1) * HD)
        qh, ql = split(q[rows])
        qc = jnp.concatenate([qh, ql, qh], axis=0)
        kh, kl = split(k[rows])
        kh, kl = kh.astype(F32), kl.astype(F32)
        kc = jnp.concatenate([kh, kh, kl], axis=0).T.astype(BF16)
        vh, vl = split(v[rows])
        vs = jnp.concatenate([vh, vl], axis=0)
        parts = []
        for block in range(t // QB):
            lo, top = block * QB, (block + 1) * QB
            s = nn(kc[:top], qc[:, lo:top])
            last = jnp.where(causal, s[lo:], -1e30)
            s = jnp.concatenate([s[:lo], last], axis=0) if block else last
            m = jnp.max(s, axis=0, keepdims=True)
            p = jnp.exp2(s - m)
            total = jnp.sum(p, axis=0, keepdims=True)
            ph, pl_ = split(p)
            both = nn(vs[:, :top], ph)
            out = both[:HD] + both[HD:] + nn(vh[:, :top], pl_)
            parts.append(out / total)
            st_ref[0, h : h + 1, lo:top] = m + jnp.log2(total)
        mixed_rows.append(jnp.concatenate(parts, axis=1))
    mixed = jnp.concatenate(mixed_rows, axis=0)

    attended = x + nn(w_out[...], cat3(mixed))
    r2 = lax.rsqrt(jnp.mean(attended * attended, axis=0, keepdims=True) + NORM_EPS)
    normed2 = attended * r2 * gain_ffn
    gu = nn(w_gu[...], cat3(normed2))
    gate, up = gu[:ff], gu[ff:]
    sig = 1.0 / (1.0 + jnp.exp(-gate))
    silu = gate * sig
    hidden = silu * up
    act_ref[0] = attended + mm_stack(w_down[...], hidden)

    g = cot_ref[0]
    dh = nn(w_dh[...], cat3(g))
    dgate = dh * up * (sig + silu * (1.0 - sig))
    dup = dh * silu
    dgu = jnp.concatenate([dgate, dup], axis=0)
    dn2 = mm_stack(w_dn[...], dgu)
    accumulate(step, g_down, outer_sum(hidden, g))
    accumulate(step, g_gu, outer_sum(dgu, normed2))
    weighted = dn2 * gain_ffn
    inner = jnp.mean(weighted * attended, axis=0, keepdims=True)
    da = g + r2 * weighted - attended * (r2 * r2 * r2 * inner)
    da_ref[0] = da
    accumulate(step, g_gf, lane_fold(dn2 * attended * r2))
    accumulate(step, g_out, outer_sum(mixed, da))
    dm = nn(w_dm[...], cat3(da))
    dm_ref[0] = dm
    prod = (dm * mixed).reshape(HEADS, HD, t)
    for h in range(HEADS):
        st_ref[0, 16 + h : 17 + h, :] = jnp.sum(prod[h], axis=0, keepdims=True)

    @pl.when(step == pl.num_programs(0) - 1)
    def _():
        parts = b1_ref.shape[0]
        b1_ref[...] = jnp.zeros_like(b1_ref)
        fs, ds = ff // parts, d // parts
        g_gu_t = g_gu[...].T
        g_down_t = g_down[...].T
        g_out_t = g_out[...].T
        gf = jnp.sum(g_gf[...], axis=1, keepdims=True)
        for n in range(parts):
            b1_ref[n, :, :fs] = g_gu_t[:, n * fs : (n + 1) * fs]
            b1_ref[n, :, fs : 2 * fs] = g_gu_t[:, ff + n * fs : ff + (n + 1) * fs]
            b1_ref[n, :, 2 * fs : 3 * fs] = g_down_t[:, n * fs : (n + 1) * fs]
            b1_ref[n, :, 3 * fs : 3 * fs + ds] = g_out_t[:, n * ds : (n + 1) * ds]
            b1_ref[n, :ds, 3 * fs + ds : 3 * fs + ds + 1] = gf[n * ds : (n + 1) * ds]


def backward_kernel(
    q_ref, k_ref, v_ref, dm_ref, st_ref, da_ref, x_ref, f_ref, ga_ref, wq_ref, wk_ref, wv_ref, cos_ref, sin_ref,
    dx_ref, b2_ref,
    w_dn, gains, g_qkv, g_in, g_ga,
):
    step = pl.program_id(0)
    d, t = q_ref.shape[1], q_ref.shape[2]

    @pl.when(step == 0)
    def _():
        for i, ref in enumerate((wq_ref, wk_ref, wv_ref)):
            w_dn[:, i * d : (i + 1) * d] = weight_stack(ref[...])
        gains[:, :1] = column(ga_ref[...])

    nb = t // QB
    causal = lax.broadcasted_iota(jnp.int32, (QB, QB), 0) >= lax.broadcasted_iota(jnp.int32, (QB, QB), 1)
    ones = (lax.broadcasted_iota(jnp.int32, (HD, t), 0) < 3).astype(BF16)
    blank = jnp.zeros((HD - 3, t), BF16)
    dq_rows, dk_rows, dv_rows = [], [], []
    for h in range(HEADS):
        rows = slice(h * HD, (h + 1) * HD)

        def extras(row):
            a, b, c = split3(row)
            pieces = jnp.concatenate([a.astype(F32), b.astype(F32), c.astype(F32)], axis=0)
            return jnp.concatenate([pieces, jnp.zeros((HD - 3, t), F32)], axis=0)

        def sides(block, row):
            hi, lo = split(block)
            hf, lf = hi.astype(F32), lo.astype(F32)
            tall = jnp.concatenate([hf, lf, hf, extras(-row)], axis=0).T.astype(BF16)
            return tall, jnp.concatenate([hi, lo], axis=0), hi

        qc, qs, qh = sides(q_ref[0, rows, :], st_ref[0, h : h + 1, :])
        mc, ms, mh = sides(dm_ref[0, rows, :], st_ref[0, 16 + h : 17 + h, :])
        kh, kl = split(k_ref[0, rows, :])
        kc = jnp.concatenate([kh, kh, kl, ones], axis=0)
        ks = jnp.concatenate([kh, kl], axis=0)
        vh, vl = split(v_ref[0, rows, :])
        vc = jnp.concatenate([vh, vh, vl, ones], axis=0)

        def scores(block):
            lo = block * QB
            cols = slice(lo, lo + QB)
            return nn(qc[lo:], kc[:, cols]), nn(mc[lo:], vc[:, cols])

        dq_blocks = [None] * nb
        dk_blocks, dv_blocks = [], []
        ahead = scores(0)
        for block in range(nb):
            lo = block * QB
            s, dp = ahead
            if block + 1 < nb:
                ahead = scores(block + 1)
            p = jnp.exp2(s)
            first = jnp.where(causal, p[:QB], 0.0)
            p = jnp.concatenate([first, p[QB:]], axis=0) if block + 1 < nb else first
            ds = p * dp
            ph, pl_ = split(p)
            dh, dl = split(ds)
            both = nn(ms[:, lo:], ph)
            dv_blocks.append(both[:HD] + both[HD:] + nn(mh[:, lo:], pl_))
            both = nn(qs[:, lo:], dh)
            dk_blocks.append(both[:HD] + both[HD:] + nn(qh[:, lo:], dl))
            th, tl = split(ds.T)
            both = nn(ks[:, lo : lo + QB], th)
            part = both[:HD] + both[HD:] + nn(kh[:, lo : lo + QB], tl)
            for i in range(block, nb):
                piece = part[:, (i - block) * QB : (i - block + 1) * QB]
                dq_blocks[i] = piece if dq_blocks[i] is None else dq_blocks[i] + piece
        dq_rows.append(jnp.concatenate(dq_blocks, axis=1))
        dk_rows.append(jnp.concatenate(dk_blocks, axis=1))
        dv_rows.append(jnp.concatenate(dv_blocks, axis=1))

    cos, sin = cos_ref[...], -sin_ref[...]
    dq = rotate(jnp.concatenate(dq_rows, axis=0), cos, sin) * HD**-0.5
    dk = rotate(jnp.concatenate(dk_rows, axis=0), cos, sin) * LN2
    dqkv = jnp.concatenate([dq, dk] + dv_rows, axis=0)

    gain = gains[:, :1]
    x = x_ref[0]
    r = lax.rsqrt(jnp.mean(x * x, axis=0, keepdims=True) + NORM_EPS)
    xr = x * r
    dn = mm_stack(w_dn[...], dqkv)
    accumulate(step, g_qkv, outer_sum(dqkv, xr * gain))
    weighted = dn * gain
    inner = jnp.mean(weighted * x, axis=0, keepdims=True)
    dx = da_ref[0] + r * weighted - x * (r * r * r * inner)
    dx_ref[0] = dx
    accumulate(step, g_ga, lane_fold(dn * xr))
    accumulate(step, g_in, outer_sum(dx, f_ref[0]))

    @pl.when(step == pl.num_programs(0) - 1)
    def _():
        parts = b2_ref.shape[0]
        ds = d // parts
        b2_ref[...] = jnp.zeros_like(b2_ref)
        g_qkv_t = g_qkv[...].T
        ga = jnp.sum(g_ga[...], axis=1, keepdims=True)
        for n in range(parts):
            own = slice(n * ds, (n + 1) * ds)
            b2_ref[n, :ds, : 3 * d] = g_qkv_t[own]
            b2_ref[n, :ds, 3 * d : 3 * d + FPAD] = g_in[own, :]
            b2_ref[n, :ds, 3 * d + FPAD : 3 * d + FPAD + 1] = ga[own]


def rotation_tables(t):
    freqs = 10000.0 ** (-np.arange(HD // 2, dtype=np.float64) * 2.0 / HD)
    angles = freqs[:, None] * np.arange(t, dtype=np.float64)[None, :]
    return np.cos(angles).astype(np.float32), np.sin(angles).astype(np.float32)


def round_up(n, m):
    return (n + m - 1) // m * m


def on_device(
    parts, series_values, observed, lag_steps, lag_flags, dataset_ids, in_proj, gain_attn, query_proj, key_proj,
    value_proj, out_proj, gain_ffn, gate_proj, up_proj, down_proj, cotangent,
):
    n_series, t = series_values.shape
    nf, d = in_proj.shape
    ff = gate_proj.shape[1]
    observed_f = observed.astype(F32)
    magnitude = jnp.sum(jnp.abs(series_values) * observed_f, axis=1)
    counted = jnp.sum(observed_f, axis=1)
    onehot = (dataset_ids[:, None] == jnp.arange(DSETS)[None, :]).astype(F32)
    sums = jnp.sum(onehot[None] * jnp.stack([magnitude, counted])[:, :, None], axis=1)
    sums = lax.psum(sums, "narrow")
    set_scale = sums[0] / jnp.maximum(sums[1], 1.0) + SCALE_EPS
    series_scale = jnp.sum(onehot * set_scale[None, :], axis=1)

    cos, sin = rotation_tables(t)
    cos, sin = jnp.asarray(cos), jnp.asarray(sin)
    smem = pl.BlockSpec(memory_space=pltpu.SMEM)

    def whole(a):
        return pl.BlockSpec(a.shape, lambda i: (0,) * a.ndim)

    def each(rows):
        return pl.BlockSpec((1, rows, t), lambda i: (i, 0, 0))

    def rows_of(rows):
        return jax.ShapeDtypeStruct((n_series, rows, t), F32)

    params = pltpu.CompilerParams(dimension_semantics=("arbitrary",), vmem_limit_bytes=62 * 2**20)
    in_t, down_t = in_proj.T, down_proj.T
    full = [series_values, observed, in_t, gain_attn, query_proj, key_proj, value_proj, out_proj, gain_ffn, gate_proj,
            up_proj, down_t, cos, sin]
    b1 = jax.ShapeDtypeStruct((parts, d, round_up(3 * (ff // parts) + d // parts + 1, 128)), F32)
    outs = [rows_of(d)] * 5 + [rows_of(32)] + [rows_of(d)] * 2 + [rows_of(FPAD), b1]
    act, q, k, v, dm, st, da, x, feats, b1 = pl.pallas_call(
        forward_kernel,
        grid=(n_series,),
        in_specs=[smem] * 3 + [whole(a) for a in full] + [each(d)],
        out_specs=[each(d)] * 5 + [each(32)] + [each(d)] * 2 + [each(FPAD), whole(b1)],
        out_shape=outs,
        scratch_shapes=[
            pltpu.VMEM((n_series, FPAD, t), F32),
            pltpu.VMEM((d, 3 * FPAD), BF16),
            pltpu.VMEM((3 * d, 3 * d), BF16),
            pltpu.VMEM((d, 3 * d), BF16),
            pltpu.VMEM((2 * ff, 3 * d), BF16),
            pltpu.VMEM((2 * d, ff), BF16),
            pltpu.VMEM((ff, 3 * d), BF16),
            pltpu.VMEM((2 * d, 2 * ff), BF16),
            pltpu.VMEM((d, 3 * d), BF16),
            pltpu.VMEM((d, 128), F32),
            pltpu.VMEM((2 * ff, d), F32),
            pltpu.VMEM((ff, d), F32),
            pltpu.VMEM((d, d), F32),
            pltpu.VMEM((d, 128), F32),
        ],
        compiler_params=params,
        name="forward_and_ffn",
    )(lag_steps, lag_flags, series_scale, *full, jnp.transpose(cotangent, (0, 2, 1)))

    share1 = lax.psum_scatter(b1, "narrow", scatter_dimension=0, tiled=True)
    total1 = lax.psum(share1, "group")[0]

    b2 = jax.ShapeDtypeStruct((parts, round_up(d // parts, 8), round_up(3 * d + FPAD + 1, 128)), F32)
    full = [gain_attn, query_proj, key_proj, value_proj, cos, sin]
    dx, b2 = pl.pallas_call(
        backward_kernel,
        grid=(n_series,),
        in_specs=[each(d)] * 4 + [each(32)] + [each(d)] * 2 + [each(FPAD)] + [whole(a) for a in full],
        out_specs=[each(d), whole(b2)],
        out_shape=[rows_of(d), b2],
        scratch_shapes=[
            pltpu.VMEM((2 * d, 3 * d), BF16),
            pltpu.VMEM((d, 128), F32),
            pltpu.VMEM((3 * d, d), F32),
            pltpu.VMEM((d, FPAD), F32),
            pltpu.VMEM((d, 128), F32),
        ],
        compiler_params=params,
        name="attention_backward",
    )(q, k, v, dm, st, da, x, feats, *full)
    share2 = lax.psum_scatter(b2, "narrow", scatter_dimension=0, tiled=True)
    total2 = lax.psum(share2, "group")[0]

    fs, ds = ff // parts, d // parts
    return (
        jnp.transpose(act, (0, 2, 1)),
        jnp.transpose(dx, (0, 2, 1)),
        total2[:ds, 3 * d : 3 * d + nf].T,
        total2[:ds, 3 * d + FPAD],
        total2[:ds, :d],
        total2[:ds, d : 2 * d],
        total2[:ds, 2 * d : 3 * d],
        total1[:, 3 * fs : 3 * fs + ds].T,
        total1[:ds, 3 * fs + ds],
        total1[:, :fs],
        total1[:, fs : 2 * fs],
        total1[:, 2 * fs : 3 * fs].T,
    )


def solution(mesh):
    series = P(("group", "narrow"), None)
    return jax.shard_map(
        functools.partial(on_device, mesh.shape["narrow"]),
        mesh=mesh,
        in_specs=(series, series, P(), P(), P(("group", "narrow"))) + (P(),) * 10 + (P(("group", "narrow"), None, None),),
        out_specs=(
            P(("group", "narrow"), None, None),
            P(("group", "narrow"), None, None),
            P(None, "narrow"),
            P("narrow"),
            P("narrow", None),
            P("narrow", None),
            P("narrow", None),
            P("narrow", None),
            P("narrow"),
            P(None, "narrow"),
            P(None, "narrow"),
            P("narrow", None),
        ),
        check_vma=False,
    )
```

```python
import functools

import jax
import jax.numpy as jnp
import numpy as np
from jax import lax
from jax.experimental import pallas as pl
from jax.experimental.pallas import tpu as pltpu
from jax.sharding import PartitionSpec as P

HEADS = 9
HD = 16
DSETS = 4
FPAD = 96
QB = 256
TA = 512
TC = 256
TD = 256
NLAG = 84

NORM_EPS = 1e-05
SCALE_EPS = 1e-05
LOG2E = 1.4426950408889634
LN2 = 0.6931471805599453

F32 = jnp.float32
BF16 = jnp.bfloat16


def nn(left, right):
    return lax.dot_general(left, right, (((1,), (0,)), ((), ())), preferred_element_type=F32)


def nt(left, right):
    return lax.dot_general(left, right, (((1,), (1,)), ((), ())), preferred_element_type=F32)


def split(x):
    hi = x.astype(BF16)
    return hi, (x - hi.astype(F32)).astype(BF16)


def split3(x):
    hi = x.astype(BF16)
    rest = x - hi.astype(F32)
    mid = rest.astype(BF16)
    return hi, mid, (rest - mid.astype(F32)).astype(BF16)


def cat3(x):
    hi, lo = split(x)
    return jnp.concatenate([hi, hi, lo], axis=0)


def weight_cat(w):
    hi, lo = split(w)
    hi, lo = hi.astype(F32), lo.astype(F32)
    return jnp.concatenate([hi, lo, hi], axis=0).T.astype(BF16)


def weight_stack(w):
    hi, lo = split(w)
    return jnp.concatenate([hi, lo], axis=0)


def mm_stack(stack, x):
    m = stack.shape[0] // 2
    hi, lo = split(x)
    both = nn(stack, hi)
    return both[:m] + both[m:] + nn(stack[:m], lo)


def outer_sum(left, right):
    m = left.shape[0]
    lh, ll = split(left)
    rh, rl = split(right)
    both = nt(jnp.concatenate([lh, ll], axis=0), rh)
    return both[:m] + both[m:] + nt(lh, rl)


def column(row):
    n = row.shape[0]
    return jnp.broadcast_to(row[None, :], (8, n)).T[:, :1]


def lane_fold(x):
    total = x[:, :128]
    for i in range(1, x.shape[1] // 128):
        total = total + x[:, i * 128 : (i + 1) * 128]
    return total


def rotate(x, cos, sin):
    t = x.shape[1]
    pairs = x.reshape(HEADS, 2, HD // 2, t)
    a, b = pairs[:, 0], pairs[:, 1]
    first = a * cos - b * sin
    second = a * sin + b * cos
    return jnp.stack([first, second], axis=1).reshape(HEADS * HD, t)


def row_scales(scale, nlag):
    row = lax.broadcasted_iota(jnp.int32, (FPAD, 128), 0)
    scales = jnp.full((FPAD, 128), scale, F32)
    inverse, logs = 1.0 / scales, jnp.log(scales)
    return jnp.where(row < nlag, inverse, jnp.where(row == nlag, logs, 1.0))[:, :1]


def prepare_kernel(
    lag_ref, flag_ref, vals_ref, obs_ref, in_ref, wq_ref, wk_ref, wv_ref, wo_ref, wg_ref, wu_ref, wd_ref, ga_ref, gf_ref,
    feat_ref, w_in, w_qkv, w_out, w_gu, w_down, w_dh, w_dgu, w_dm, w_dqkv, gains,
):
    n_series, t = vals_ref.shape
    d, nf = in_ref.shape
    nlag = lag_ref.shape[0]
    ff = wg_ref.shape[1]
    obs = obs_ref[...].astype(F32)
    both = jnp.concatenate([vals_ref[...] * obs, obs], axis=0)
    lanes = lax.broadcasted_iota(jnp.int32, both.shape, 1)

    def one_lag(j, missing):
        lag = lag_ref[j]
        moved = jnp.where(lanes >= lag, pltpu.roll(both, lag, 1), 0.0)
        for s in range(n_series):
            feat_ref[s, pl.ds(j, 1), :] = moved[s : s + 1]
        return missing + flag_ref[j].astype(F32) * (1.0 - moved[n_series:])

    missing = lax.fori_loop(0, nlag, one_lag, jnp.zeros((n_series, t), F32), unroll=4)
    for s in range(n_series):
        feat_ref[s, nlag : nlag + 1, :] = jnp.ones((1, t), F32)
        feat_ref[s, nlag + 1 : nlag + 2, :] = missing[s : s + 1] * nlag**-0.5
        feat_ref[s, nlag + 2 :, :] = jnp.zeros((FPAD - nlag - 2, t), F32)

    w_in_rows = jnp.concatenate([in_ref[...].T, jnp.zeros((FPAD - nf, d), F32)], axis=0)
    w_in[...] = weight_cat(w_in_rows)
    for i, ref in enumerate((wq_ref, wk_ref, wv_ref)):
        w_qkv[i * d : (i + 1) * d, :] = weight_cat(ref[...])
        w_dqkv[:, i * d : (i + 1) * d] = weight_stack(ref[...])
    w_out[...] = weight_cat(wo_ref[...])
    w_gu[:ff, :] = weight_cat(wg_ref[...])
    w_gu[ff:, :] = weight_cat(wu_ref[...])
    w_down[...] = weight_stack(wd_ref[...])
    w_dh[...] = weight_cat(wd_ref[...])
    w_dgu[:, :ff] = weight_stack(wg_ref[...])
    w_dgu[:, ff:] = weight_stack(wu_ref[...])
    w_dm[...] = weight_cat(wo_ref[...].T)
    gains[...] = jnp.zeros_like(gains)
    gains[:, :1] = column(ga_ref[...])
    gains[:, 1:2] = column(gf_ref[...])


def forward_kernel(
    scale_ref, feat_ref, w_in, w_qkv, w_out, w_gu, w_down, w_dh, w_dgu, w_dm, gains, cos_ref, sin_ref, cot_ref,
    act_ref, q_ref, k_ref, v_ref, dm_ref, st_ref, da_ref, x_ref, b1_ref,
    mixed_ref, g_gu, g_down, g_out, g_gf,
):
    step = pl.program_id(0)
    d, t = cot_ref.shape[1], cot_ref.shape[2]
    ff = w_dh.shape[0]
    gain_attn, gain_ffn = gains[:, :1], gains[:, 1:2]
    scales = row_scales(scale_ref[step], NLAG)

    @pl.when(step == 0)
    def _():
        for ref in (g_gu, g_down, g_out, g_gf):
            ref[...] = jnp.zeros_like(ref)

    st_ref[0] = jnp.zeros(st_ref.shape[1:], F32)

    def project(i, _):
        cols = pl.ds(pl.multiple_of(i * TA, TA), TA)
        x = nn(w_in[...], cat3(feat_ref[0, :, cols] * scales))
        x_ref[0, :, cols] = x
        normed = x * lax.rsqrt(jnp.mean(x * x, axis=0, keepdims=True) + NORM_EPS) * gain_attn
        qkv = nn(w_qkv[...], cat3(normed))
        cos, sin = cos_ref[:, cols], sin_ref[:, cols]
        q_ref[0, :, cols] = rotate(qkv[:d], cos, sin) * (HD**-0.5 * LOG2E)
        k_ref[0, :, cols] = rotate(qkv[d : 2 * d], cos, sin)
        v_ref[0, :, cols] = qkv[2 * d :]
        return 0

    lax.fori_loop(0, t // TA, project, 0)

    causal = lax.broadcasted_iota(jnp.int32, (QB, QB), 0) <= lax.broadcasted_iota(jnp.int32, (QB, QB), 1)

    def head(h, _):
        rows = pl.ds(pl.multiple_of(h * HD, HD), HD)
        qh, ql = split(q_ref[0, rows, :])
        qc = jnp.concatenate([qh, ql, qh], axis=0)
        kh, kl = split(k_ref[0, rows, :])
        kh, kl = kh.astype(F32), kl.astype(F32)
        kc = jnp.concatenate([kh, kh, kl], axis=0).T.astype(BF16)
        vh, vl = split(v_ref[0, rows, :])
        vs = jnp.concatenate([vh, vl], axis=0)
        for block in range(t // QB):
            lo, top = block * QB, (block + 1) * QB
            s = nn(kc[:top], qc[:, lo:top])
            last = jnp.where(causal, s[lo:], -1e30)
            s = jnp.concatenate([s[:lo], last], axis=0) if block else last
            m = jnp.max(s, axis=0, keepdims=True)
            p = jnp.exp2(s - m)
            total = jnp.sum(p, axis=0, keepdims=True)
            ph, pl_ = split(p)
            both = nn(vs[:, :top], ph)
            out = both[:HD] + both[HD:] + nn(vh[:, :top], pl_)
            mixed_ref[rows, lo:top] = out / total
            st_ref[0, pl.ds(h, 1), lo:top] = m + jnp.log2(total)
        return 0

    lax.fori_loop(0, HEADS, head, 0, unroll=3)

    def feed(i, _):
        cols = pl.ds(pl.multiple_of(i * TC, TC), TC)
        mixed = mixed_ref[:, cols]
        attended = x_ref[0, :, cols] + nn(w_out[...], cat3(mixed))
        r2 = lax.rsqrt(jnp.mean(attended * attended, axis=0, keepdims=True) + NORM_EPS)
        scaled = attended * r2
        normed2 = scaled * gain_ffn
        gu = nn(w_gu[...], cat3(normed2))
        gate, up = gu[:ff], gu[ff:]
        sig = 1.0 / (1.0 + jnp.exp(-gate))
        silu = gate * sig
        hidden = silu * up
        act_ref[0, :, cols] = attended + mm_stack(w_down[...], hidden)

        g = cot_ref[0, :, cols]
        dh = nn(w_dh[...], cat3(g))
        dgate = dh * up * (sig + silu * (1.0 - sig))
        dup = dh * silu
        dgu = jnp.concatenate([dgate, dup], axis=0)
        dn2 = mm_stack(w_dgu[...], dgu)
        g_down[...] += outer_sum(hidden, g)
        g_gu[...] += outer_sum(dgu, normed2)
        weighted = dn2 * gain_ffn
        inner = jnp.mean(weighted * attended, axis=0, keepdims=True)
        da = g + r2 * weighted - attended * (r2 * r2 * r2 * inner)
        da_ref[0, :, cols] = da
        g_gf[...] += lane_fold(dn2 * scaled)
        g_out[...] += outer_sum(mixed, da)
        dm = nn(w_dm[...], cat3(da))
        dm_ref[0, :, cols] = dm
        prod = (dm * mixed).reshape(HEADS, HD, TC)
        for h in range(HEADS):
            st_ref[0, 16 + h : 17 + h, cols] = jnp.sum(prod[h], axis=0, keepdims=True)
        return 0

    lax.fori_loop(0, t // TC, feed, 0)

    @pl.when(step == pl.num_programs(0) - 1)
    def _():
        parts = b1_ref.shape[0]
        fs, ds = ff // parts, d // parts
        g_gu_t = g_gu[...].T
        g_down_t = g_down[...].T
        g_out_t = g_out[...].T
        gf = jnp.sum(g_gf[...], axis=1, keepdims=True)
        b1_ref[...] = jnp.zeros_like(b1_ref)
        for n in range(parts):
            gf_own = jnp.concatenate([gf[n * ds : (n + 1) * ds], jnp.zeros((d - ds, 1), F32)], axis=0)
            share = jnp.concatenate([
                g_gu_t[:, n * fs : (n + 1) * fs], g_gu_t[:, ff + n * fs : ff + (n + 1) * fs],
                g_down_t[:, n * fs : (n + 1) * fs], g_out_t[:, n * ds : (n + 1) * ds], gf_own,
            ], axis=1)
            put_share(b1_ref, n, share)


def put_share(ref, n, share):
    rows, cols = share.shape
    pad_rows, pad_cols = -rows % 8, -cols % 128
    if pad_rows:
        share = jnp.concatenate([share, jnp.zeros((pad_rows, cols), F32)], axis=0)
    if pad_cols:
        share = jnp.concatenate([share, jnp.zeros((share.shape[0], pad_cols), F32)], axis=1)
    height = share.shape[0]
    for c in range(share.shape[1] // 128):
        ref[n, c * height : (c + 1) * height, :] = share[:, c * 128 : (c + 1) * 128]


def backward_kernel(
    scale_ref, q_ref, k_ref, v_ref, dm_ref, st_ref, da_ref, x_ref, feat_ref, w_dqkv, gains, cos_ref, sin_ref,
    dx_ref, b2_ref,
    dqkv_ref, g_qkv, g_in, g_ga,
):
    step = pl.program_id(0)
    d, t = q_ref.shape[1], q_ref.shape[2]

    @pl.when(step == 0)
    def _():
        for ref in (g_qkv, g_in, g_ga):
            ref[...] = jnp.zeros_like(ref)

    nb = t // QB
    causal = lax.broadcasted_iota(jnp.int32, (QB, QB), 0) >= lax.broadcasted_iota(jnp.int32, (QB, QB), 1)
    ones = (lax.broadcasted_iota(jnp.int32, (HD, t), 0) < 3).astype(BF16)

    def extras(row):
        a, b, c = split3(row)
        pieces = jnp.concatenate([a.astype(F32), b.astype(F32), c.astype(F32)], axis=0)
        return jnp.concatenate([pieces, jnp.zeros((HD - 3, t), F32)], axis=0)

    def sides(block, row):
        hi, lo = split(block)
        hf, lf = hi.astype(F32), lo.astype(F32)
        tall = jnp.concatenate([hf, lf, hf, extras(-row)], axis=0).T.astype(BF16)
        return tall, jnp.concatenate([hi, lo], axis=0), hi

    def head(h, _):
        def rows_at(first):
            return pl.ds(pl.multiple_of(first + h * HD, HD), HD)

        rows = rows_at(0)
        qc, qs, qh = sides(q_ref[0, rows, :], st_ref[0, pl.ds(h, 1), :])
        mc, ms, mh = sides(dm_ref[0, rows, :], st_ref[0, pl.ds(16 + h, 1), :])
        kh, kl = split(k_ref[0, rows, :])
        kc = jnp.concatenate([kh, kh, kl, ones], axis=0)
        ks = jnp.concatenate([kh, kl], axis=0)
        vh, vl = split(v_ref[0, rows, :])
        vc = jnp.concatenate([vh, vh, vl, ones], axis=0)

        def scores(block):
            lo = block * QB
            cols = slice(lo, lo + QB)
            return nn(qc[lo:], kc[:, cols]), nn(mc[lo:], vc[:, cols])

        dq_blocks = [None] * nb
        ahead = scores(0)
        for block in range(nb):
            lo = block * QB
            cols = slice(lo, lo + QB)
            s, dp = ahead
            if block + 1 < nb:
                ahead = scores(block + 1)
            p = jnp.exp2(s)
            first = jnp.where(causal, p[:QB], 0.0)
            p = jnp.concatenate([first, p[QB:]], axis=0) if block + 1 < nb else first
            ds = p * dp
            ph, pl_ = split(p)
            dh, dl = split(ds)
            both = nn(ms[:, lo:], ph)
            dqkv_ref[rows_at(2 * d), cols] = both[:HD] + both[HD:] + nn(mh[:, lo:], pl_)
            both = nn(qs[:, lo:], dh)
            dqkv_ref[rows_at(d), cols] = both[:HD] + both[HD:] + nn(qh[:, lo:], dl)
            th, tl = split(ds.T)
            both = nn(ks[:, cols], th)
            part = both[:HD] + both[HD:] + nn(kh[:, cols], tl)
            for i in range(block, nb):
                piece = part[:, (i - block) * QB : (i - block + 1) * QB]
                dq_blocks[i] = piece if dq_blocks[i] is None else dq_blocks[i] + piece
        for i in range(nb):
            dqkv_ref[rows, i * QB : (i + 1) * QB] = dq_blocks[i]
        return 0

    lax.fori_loop(0, HEADS, head, 0, unroll=3)

    gain = gains[:, :1]
    scales = row_scales(scale_ref[step], NLAG)

    def finish(i, _):
        cols = pl.ds(pl.multiple_of(i * TD, TD), TD)
        cos, sin = cos_ref[:, cols], -sin_ref[:, cols]
        dq = rotate(dqkv_ref[:d, cols], cos, sin) * HD**-0.5
        dk = rotate(dqkv_ref[d : 2 * d, cols], cos, sin) * LN2
        dqkv = jnp.concatenate([dq, dk, dqkv_ref[2 * d :, cols]], axis=0)
        x = x_ref[0, :, cols]
        r = lax.rsqrt(jnp.mean(x * x, axis=0, keepdims=True) + NORM_EPS)
        xr = x * r
        dn = mm_stack(w_dqkv[...], dqkv)
        g_qkv[...] += outer_sum(dqkv, xr * gain)
        weighted = dn * gain
        inner = jnp.mean(weighted * x, axis=0, keepdims=True)
        dx = da_ref[0, :, cols] + r * weighted - x * (r * r * r * inner)
        dx_ref[0, :, cols] = dx
        g_ga[...] += lane_fold(dn * xr)
        g_in[...] += outer_sum(dx, feat_ref[0, :, cols] * scales)
        return 0

    lax.fori_loop(0, t // TD, finish, 0)

    @pl.when(step == pl.num_programs(0) - 1)
    def _():
        parts = b2_ref.shape[0]
        ds = d // parts
        g_qkv_t = g_qkv[...].T
        ga = jnp.sum(g_ga[...], axis=1, keepdims=True)
        b2_ref[...] = jnp.zeros_like(b2_ref)
        for n in range(parts):
            own = slice(n * ds, (n + 1) * ds)
            put_share(b2_ref, n, jnp.concatenate([g_qkv_t[own], g_in[own, :], ga[own]], axis=1))


def reduce_kernel(b1_ref, b2_ref, out_ref, recv1, pair, recv2, share, recv3, sem_s, sem_r, gsem_s, gsem_r, hsem_s, hsem_r):
    ny = b1_ref.shape[0]
    r1, r2 = b1_ref.shape[2], b2_ref.shape[2]
    groups, chunk = recv3.shape[0], recv3.shape[1]
    g = lax.axis_index("group")
    n = lax.axis_index("narrow")
    core, y = lax.rem(n, 2), lax.div(n, 2)
    other = 1 - core

    def at(group, narrow):
        return (group, narrow)

    mesh_id = pl.DeviceIdType.MESH
    barrier = pltpu.get_barrier_semaphore()
    pl.semaphore_signal(barrier, inc=1, device_id=at(g, y * 2 + other), device_id_type=mesh_id)
    for off in range(1, ny):
        peer = lax.rem(y + off, ny)
        pl.semaphore_signal(barrier, inc=1, device_id=at(g, peer * 2 + core), device_id_type=mesh_id)
    for off in range(1, groups):
        pl.semaphore_signal(barrier, inc=1, device_id=at(lax.rem(g + off, groups), n), device_id_type=mesh_id)
    pl.semaphore_wait(barrier, 1 + (ny - 1) + (groups - 1))

    def copy(src, dst, send, recv, to):
        return pltpu.make_async_remote_copy(
            src_ref=src, dst_ref=dst, send_sem=send, recv_sem=recv, device_id=to, device_id_type=mesh_id
        )

    sibling = at(g, y * 2 + other)
    first = copy(b1_ref.at[:, other], recv1.at[:, pl.ds(0, r1)], sem_s.at[0], sem_r.at[0], sibling)
    second = copy(b2_ref.at[:, other], recv1.at[:, pl.ds(r1, r2)], sem_s.at[1], sem_r.at[1], sibling)
    first.start()
    second.start()
    first.wait_recv()
    second.wait_recv()
    for i in range(ny):
        pair[i, :r1] = b1_ref[i, core] + recv1[i, :r1]
        pair[i, r1 : r1 + r2] = b2_ref[i, core] + recv1[i, r1 : r1 + r2]

    sends = []
    for off in range(1, ny):
        peer = lax.rem(y + off, ny)
        sends.append(copy(pair.at[peer], recv2.at[off - 1], gsem_s.at[off], gsem_r.at[off], at(g, peer * 2 + core)))
        sends[-1].start()
    for s in sends:
        s.wait_recv()
    total = pair[y]
    for off in range(1, ny):
        total += recv2[off - 1]
    share[...] = total.reshape(share.shape)

    sends_b = []
    for off in range(1, groups):
        peer = lax.rem(g + off, groups)
        sends_b.append(copy(share.at[peer], recv3.at[off], hsem_s.at[0, off], hsem_r.at[0, off], at(peer, n)))
        sends_b[-1].start()
    recv3[0] = share[g]
    for s in sends_b:
        s.wait_recv()
    out_ref[g] = jnp.sum(recv3[...], axis=0)
    sends_c = []
    for off in range(1, groups):
        peer = lax.rem(g + off, groups)
        sends_c.append(copy(out_ref.at[g], out_ref.at[g], hsem_s.at[1, off], hsem_r.at[1, off], at(peer, n)))
        sends_c[-1].start()
    for s in sends_c:
        s.wait_recv()
    for s in [first, second] + sends + sends_b + sends_c:
        s.wait_send()


def unpack_kernel(
    total_ref, g_in, g_ga, g_q, g_k, g_v, g_out, g_gf, g_gate, g_up, g_down,
):
    d, fs = g_gate.shape
    ds, nf = g_in.shape
    wide = round_up(3 * fs + ds + 1, 128) // 128
    one = jnp.concatenate([total_ref[c * d : (c + 1) * d, :] for c in range(wide)], axis=1)
    g_gate[...] = one[:, :fs]
    g_up[...] = one[:, fs : 2 * fs]
    g_down[...] = one[:, 2 * fs : 3 * fs]
    g_out[...] = one[:, 3 * fs : 3 * fs + ds].T
    g_gf[...] = one[:ds, 3 * fs + ds]
    base = wide * d
    height = round_up(ds, 8)
    wide = round_up(3 * d + FPAD + 1, 128) // 128
    two = jnp.concatenate([total_ref[base + c * height : base + c * height + ds, :] for c in range(wide)], axis=1)
    g_q[...] = two[:, :d]
    g_k[...] = two[:, d : 2 * d]
    g_v[...] = two[:, 2 * d : 3 * d]
    g_in[...] = two[:, 3 * d : 3 * d + nf]
    g_ga[...] = two[:, 3 * d + FPAD]


def rotation_tables(t):
    freqs = 10000.0 ** (-np.arange(HD // 2, dtype=np.float64) * 2.0 / HD)
    angles = freqs[:, None] * np.arange(t, dtype=np.float64)[None, :]
    return np.cos(angles).astype(np.float32), np.sin(angles).astype(np.float32)


def round_up(n, m):
    return (n + m - 1) // m * m


def on_device(
    groups, parts, series_values, observed, lag_steps, lag_flags, dataset_ids, in_proj, gain_attn, query_proj, key_proj,
    value_proj, out_proj, gain_ffn, gate_proj, up_proj, down_proj, cotangent,
):
    n_series, t = series_values.shape
    nf, d = in_proj.shape
    ff = gate_proj.shape[1]
    fs, ds = ff // parts, d // parts
    onehot, sums = local_sums(series_values, observed, dataset_ids)
    others = exchange_sums(sums, parts)

    cos, sin = rotation_tables(t)
    cos, sin = jnp.asarray(cos), jnp.asarray(sin)
    smem = pl.BlockSpec(memory_space=pltpu.SMEM)
    vmem = pl.BlockSpec(memory_space=pltpu.VMEM)

    def whole(a):
        return pl.BlockSpec(a.shape, lambda i: (0,) * a.ndim)

    def each(rows):
        return pl.BlockSpec((1, rows, t), lambda i: (i, 0, 0))

    def shape(*dims, dtype=F32):
        return jax.ShapeDtypeStruct(dims, dtype)

    params = pltpu.CompilerParams(dimension_semantics=("arbitrary",), vmem_limit_bytes=62 * 2**20)
    plain = pltpu.CompilerParams(vmem_limit_bytes=62 * 2**20)
    in_t, down_t = in_proj.T, down_proj.T
    raw, w_in, w_qkv, w_out, w_gu, w_down, w_dh, w_dgu, w_dm, w_dqkv, gains = pl.pallas_call(
        prepare_kernel,
        in_specs=[smem] * 2 + [vmem] * 12,
        out_specs=[vmem] * 11,
        out_shape=[
            shape(n_series, FPAD, t),
            shape(d, 3 * FPAD, dtype=BF16),
            shape(3 * d, 3 * d, dtype=BF16),
            shape(d, 3 * d, dtype=BF16),
            shape(2 * ff, 3 * d, dtype=BF16),
            shape(2 * d, ff, dtype=BF16),
            shape(ff, 3 * d, dtype=BF16),
            shape(2 * d, 2 * ff, dtype=BF16),
            shape(d, 3 * d, dtype=BF16),
            shape(2 * d, 3 * d, dtype=BF16),
            shape(d, 128),
        ],
        compiler_params=plain,
        cost_estimate=pl.CostEstimate(flops=2 * 10**7, bytes_accessed=8 * 10**6, transcendentals=0),
        name="split_weights_and_shift_lags",
    )(lag_steps, lag_flags, series_values, observed, in_t, query_proj, key_proj, value_proj, out_proj, gate_proj, up_proj,
      down_t, gain_attn, gain_ffn)

    sums = functools.reduce(jnp.add, others, sums)
    set_scale = sums[0] / jnp.maximum(sums[1], 1.0) + SCALE_EPS
    series_scale = jnp.sum(onehot * set_scale[None, :], axis=1)

    rows1 = round_up(3 * fs + ds + 1, 128) // 128 * d
    rows2 = round_up(3 * d + FPAD + 1, 128) // 128 * round_up(ds, 8)
    rows2 = round_up(rows1 + rows2, 8 * groups) - rows1
    full = [w_in, w_qkv, w_out, w_gu, w_down, w_dh, w_dgu, w_dm, gains, cos, sin]
    b1 = shape(parts, rows1, 128)
    act, q, k, v, dm, st, da, x, b1 = pl.pallas_call(
        forward_kernel,
        grid=(n_series,),
        in_specs=[smem, each(FPAD)] + [whole(a) for a in full] + [each(d)],
        out_specs=[each(d)] * 5 + [each(32)] + [each(d)] * 2 + [whole(b1)],
        out_shape=[shape(n_series, d, t)] * 5 + [shape(n_series, 32, t)] + [shape(n_series, d, t)] * 2 + [b1],
        scratch_shapes=[
            pltpu.VMEM((d, t), F32),
            pltpu.VMEM((2 * ff, d), F32),
            pltpu.VMEM((ff, d), F32),
            pltpu.VMEM((d, d), F32),
            pltpu.VMEM((d, 128), F32),
        ],
        compiler_params=params,
        name="forward_and_ffn",
    )(series_scale, raw, *full, jnp.transpose(cotangent, (0, 2, 1)))

    b2 = shape(parts, rows2, 128)
    full = [w_dqkv, gains, cos, sin]
    dx, b2 = pl.pallas_call(
        backward_kernel,
        grid=(n_series,),
        in_specs=[smem] + [each(d)] * 4 + [each(32)] + [each(d)] * 2 + [each(FPAD)] + [whole(a) for a in full],
        out_specs=[each(d), whole(b2)],
        out_shape=[shape(n_series, d, t), b2],
        scratch_shapes=[
            pltpu.VMEM((3 * d, t), F32),
            pltpu.VMEM((3 * d, d), F32),
            pltpu.VMEM((d, FPAD), F32),
            pltpu.VMEM((d, 128), F32),
        ],
        compiler_params=params,
        name="attention_backward",
    )(series_scale, q, k, v, dm, st, da, x, raw, *full)

    total = reduce_grads(b1, b2, groups, parts)
    grads = pl.pallas_call(
        unpack_kernel,
        in_specs=[vmem],
        out_specs=[vmem] * 10,
        out_shape=[
            shape(ds, nf), shape(ds), shape(ds, d), shape(ds, d), shape(ds, d), shape(ds, d), shape(ds),
            shape(d, fs), shape(d, fs), shape(d, fs),
        ],
        compiler_params=plain,
        name="unpack_gradients",
    )(total)
    return (
        jnp.transpose(act, (0, 2, 1)),
        jnp.transpose(dx, (0, 2, 1)),
        grads[0].T,
        *grads[1:9],
        grads[9].T,
    )


def local_sums(series_values, observed, dataset_ids):
    observed_f = observed.astype(F32)
    magnitude = jnp.sum(jnp.abs(series_values) * observed_f, axis=1)
    counted = jnp.sum(observed_f, axis=1)
    onehot = (dataset_ids[:, None] == jnp.arange(DSETS)[None, :]).astype(F32)
    return onehot, jnp.sum(onehot[None] * jnp.stack([magnitude, counted])[:, :, None], axis=1)


def exchange_sums(sums, parts):
    return [lax.ppermute(sums, "narrow", [(i, (i + off) % parts) for i in range(parts)]) for off in range(1, parts)]


def reduce_grads(b1, b2, groups, parts):
    ny = parts // 2
    rows1, rows2 = b1.shape[1], b2.shape[1]
    rows = rows1 + rows2
    chunk = rows // groups
    vmem = pl.BlockSpec(memory_space=pltpu.VMEM)
    dma = pltpu.SemaphoreType.DMA
    total = pl.pallas_call(
        reduce_kernel,
        in_specs=[vmem] * 2,
        out_specs=vmem,
        out_shape=jax.ShapeDtypeStruct((groups, chunk, 128), F32),
        scratch_shapes=[
            pltpu.VMEM((ny, rows, 128), F32),
            pltpu.VMEM((ny, rows, 128), F32),
            pltpu.VMEM((max(ny - 1, 1), rows, 128), F32),
            pltpu.VMEM((groups, chunk, 128), F32),
            pltpu.VMEM((groups, chunk, 128), F32),
            dma((2,)),
            dma((2,)),
            dma((ny,)),
            dma((ny,)),
            dma((2, groups)),
            dma((2, groups)),
        ],
        compiler_params=pltpu.CompilerParams(collective_id=0, has_side_effects=True, vmem_limit_bytes=40 * 2**20),
        name="reduce_gradients",
    )(b1.reshape(ny, 2, rows1, 128), b2.reshape(ny, 2, rows2, 128))
    return total.reshape(rows, 128)


def solution(mesh):
    series = P(("group", "narrow"), None)
    return jax.shard_map(
        functools.partial(on_device, mesh.shape["group"], mesh.shape["narrow"]),
        mesh=mesh,
        in_specs=(series, series, P(), P(), P(("group", "narrow"))) + (P(),) * 10 + (P(("group", "narrow"), None, None),),
        out_specs=(
            P(("group", "narrow"), None, None),
            P(("group", "narrow"), None, None),
            P(None, "narrow"),
            P("narrow"),
            P("narrow", None),
            P("narrow", None),
            P("narrow", None),
            P("narrow", None),
            P("narrow"),
            P(None, "narrow"),
            P(None, "narrow"),
            P("narrow", None),
        ),
        check_vma=False,
    )
```

```python
import functools

import jax
import jax.numpy as jnp
import numpy as np
from jax import lax
from jax.experimental import pallas as pl
from jax.experimental.pallas import tpu as pltpu
from jax.sharding import PartitionSpec as P

HEADS = 9
HD = 16
DSETS = 4
FPAD = 96
QB = 256
TA = 1024
TC = 1024
TD = 1024
NLAG = 84
AHEAD = 2

NORM_EPS = 1e-05
SCALE_EPS = 1e-05
LOG2E = 1.4426950408889634
LN2 = 0.6931471805599453

F32 = jnp.float32
BF16 = jnp.bfloat16


def nn(left, right):
    return lax.dot_general(left, right, (((1,), (0,)), ((), ())), preferred_element_type=F32)


def nt(left, right):
    return lax.dot_general(left, right, (((1,), (1,)), ((), ())), preferred_element_type=F32)


def split(x):
    hi = x.astype(BF16)
    return hi, (x - hi.astype(F32)).astype(BF16)


def split3(x):
    hi = x.astype(BF16)
    rest = x - hi.astype(F32)
    mid = rest.astype(BF16)
    return hi, mid, (rest - mid.astype(F32)).astype(BF16)


def cat3(x):
    hi, lo = split(x)
    return jnp.concatenate([hi, hi, lo], axis=0)


def weight_cat(w):
    hi, lo = split(w)
    hi, lo = hi.astype(F32), lo.astype(F32)
    return jnp.concatenate([hi, lo, hi], axis=0).T.astype(BF16)


def weight_stack(w):
    hi, lo = split(w)
    return jnp.concatenate([hi, lo], axis=0)


def mm_stack(stack, x):
    m = stack.shape[0] // 2
    hi, lo = split(x)
    both = nn(stack, hi)
    return both[:m] + both[m:] + nn(stack[:m], lo)


def outer_sum(left, right):
    m = left.shape[0]
    lh, ll = split(left)
    rh, rl = split(right)
    both = nt(jnp.concatenate([lh, ll], axis=0), rh)
    return both[:m] + both[m:] + nt(lh, rl)


def column(row):
    n = row.shape[0]
    return jnp.broadcast_to(row[None, :], (8, n)).T[:, :1]


def lane_fold(x):
    total = x[:, :128]
    for i in range(1, x.shape[1] // 128):
        total = total + x[:, i * 128 : (i + 1) * 128]
    return total


def rotate(x, cos, sin):
    t = x.shape[1]
    pairs = x.reshape(HEADS, 2, HD // 2, t)
    a, b = pairs[:, 0], pairs[:, 1]
    first = a * cos - b * sin
    second = a * sin + b * cos
    return jnp.stack([first, second], axis=1).reshape(HEADS * HD, t)


def row_scales(scale, nlag):
    row = lax.broadcasted_iota(jnp.int32, (FPAD, 128), 0)
    scales = jnp.full((FPAD, 128), scale, F32)
    inverse, logs = 1.0 / scales, jnp.log(scales)
    return jnp.where(row < nlag, inverse, jnp.where(row == nlag, logs, 1.0))[:, :1]


def prepare_kernel(
    lag_ref, flag_ref, vals_ref, obs_ref, in_ref, wq_ref, wk_ref, wv_ref, wo_ref, wg_ref, wu_ref, wd_ref, ga_ref, gf_ref,
    feat_ref, w_in, w_qkv, w_out, w_gu, w_down, w_dh, w_dgu, w_dm, w_dqkv, gains,
):
    n_series, t = vals_ref.shape
    d, nf = in_ref.shape
    nlag = lag_ref.shape[0]
    ff = wg_ref.shape[1]
    obs = obs_ref[...].astype(F32)
    both = jnp.concatenate([vals_ref[...] * obs, obs], axis=0)
    lanes = lax.broadcasted_iota(jnp.int32, both.shape, 1)

    def one_lag(j, missing):
        lag = lag_ref[j]
        moved = jnp.where(lanes >= lag, pltpu.roll(both, lag, 1), 0.0)
        for s in range(n_series):
            feat_ref[s, pl.ds(j, 1), :] = moved[s : s + 1]
        return missing + flag_ref[j].astype(F32) * (1.0 - moved[n_series:])

    missing = lax.fori_loop(0, nlag, one_lag, jnp.zeros((n_series, t), F32), unroll=12)
    for s in range(n_series):
        feat_ref[s, nlag : nlag + 1, :] = jnp.ones((1, t), F32)
        feat_ref[s, nlag + 1 : nlag + 2, :] = missing[s : s + 1] * nlag**-0.5
        feat_ref[s, nlag + 2 :, :] = jnp.zeros((FPAD - nlag - 2, t), F32)

    w_in_rows = jnp.concatenate([in_ref[...].T, jnp.zeros((FPAD - nf, d), F32)], axis=0)
    w_in[...] = weight_cat(w_in_rows)
    for i, ref in enumerate((wq_ref, wk_ref, wv_ref)):
        w_qkv[i * d : (i + 1) * d, :] = weight_cat(ref[...])
        w_dqkv[:, i * d : (i + 1) * d] = weight_stack(ref[...])
    w_out[...] = weight_cat(wo_ref[...])
    w_gu[:ff, :] = weight_cat(wg_ref[...])
    w_gu[ff:, :] = weight_cat(wu_ref[...])
    w_down[...] = weight_stack(wd_ref[...])
    w_dh[...] = weight_cat(wd_ref[...])
    w_dgu[:, :ff] = weight_stack(wg_ref[...])
    w_dgu[:, ff:] = weight_stack(wu_ref[...])
    w_dm[...] = weight_cat(wo_ref[...].T)
    gains[...] = jnp.zeros_like(gains)
    gains[:, :1] = column(ga_ref[...])
    gains[:, 1:2] = column(gf_ref[...])


def forward_kernel(
    scale_ref, feat_ref, w_in, w_qkv, w_out, w_gu, w_down, w_dh, w_dgu, w_dm, gains, cos_ref, sin_ref, cot_ref,
    act_ref, q_ref, k_ref, v_ref, dm_ref, st_ref, da_ref, x_ref, b1_ref,
    mixed_ref, g_gu, g_down, g_out, g_gf,
):
    step = pl.program_id(0)
    d, t = cot_ref.shape[1], cot_ref.shape[2]
    ff = w_dh.shape[0]
    gain_attn, gain_ffn = gains[:, :1], gains[:, 1:2]
    scales = row_scales(scale_ref[step], NLAG)

    @pl.when(step == 0)
    def _():
        for ref in (g_gu, g_down, g_out, g_gf):
            ref[...] = jnp.zeros_like(ref)

    st_ref[0] = jnp.zeros(st_ref.shape[1:], F32)

    def project(i, _):
        cols = pl.ds(pl.multiple_of(i * TA, TA), TA)
        x = nn(w_in[...], cat3(feat_ref[0, :, cols] * scales))
        x_ref[0, :, cols] = x
        normed = x * lax.rsqrt(jnp.mean(x * x, axis=0, keepdims=True) + NORM_EPS) * gain_attn
        qkv = nn(w_qkv[...], cat3(normed))
        cos, sin = cos_ref[:, cols], sin_ref[:, cols]
        q_ref[0, :, cols] = rotate(qkv[:d], cos, sin) * (HD**-0.5 * LOG2E)
        k_ref[0, :, cols] = rotate(qkv[d : 2 * d], cos, sin)
        v_ref[0, :, cols] = qkv[2 * d :]
        return 0

    lax.fori_loop(0, t // TA, project, 0)

    causal = lax.broadcasted_iota(jnp.int32, (QB, QB), 0) <= lax.broadcasted_iota(jnp.int32, (QB, QB), 1)

    def prepare(h):
        rows = slice(h * HD, (h + 1) * HD)
        qh, ql = split(q_ref[0, rows, :])
        qc = jnp.concatenate([qh, ql, qh], axis=0)
        kh, kl = split(k_ref[0, rows, :])
        kh, kl = kh.astype(F32), kl.astype(F32)
        kc = jnp.concatenate([kh, kh, kl], axis=0).T.astype(BF16)
        vh, vl = split(v_ref[0, rows, :])
        return qc, kc, jnp.concatenate([vh, vl], axis=0), vh

    def scores(sides, item):
        qc, kc = sides[:2]
        lo, top = item[1] * QB, (item[1] + 1) * QB
        return nn(kc[:top], qc[:, lo:top])

    def softmax(s, block):
        lo = block * QB
        last = jnp.where(causal, s[lo:], -1e30)
        s = jnp.concatenate([s[:lo], last], axis=0) if block else last
        return s, jnp.max(s, axis=0, keepdims=True)

    def mix(sides, soft, item):
        h, block = item
        vs, vh = sides[2:]
        s, m = soft
        lo, top = block * QB, (block + 1) * QB
        both = low = total = 0.0
        for c in range(block + 1):
            keys = slice(c * QB, (c + 1) * QB)
            p = jnp.exp2(s[keys] - m)
            total = total + jnp.sum(p, axis=0, keepdims=True)
            ph, pl_ = split(p)
            both = both + nn(vs[:, keys], ph)
            low = low + nn(vh[:, keys], pl_)
        mixed_ref[h * HD : (h + 1) * HD, lo:top] = (both[:HD] + both[HD:] + low) / total
        st_ref[0, h : h + 1, lo:top] = m + jnp.log2(total)

    sides = [prepare(h) for h in range(HEADS)]
    items = [(h, block) for block in reversed(range(t // QB)) for h in range(HEADS)]
    ahead = {}
    for j in range(len(items) + AHEAD):
        if j < len(items):
            ahead[j] = scores(sides[items[j][0]], items[j])
        if j >= AHEAD:
            item = items[j - AHEAD]
            mix(sides[item[0]], softmax(ahead.pop(j - AHEAD), item[1]), item)

    def feed(i, _):
        cols = pl.ds(pl.multiple_of(i * TC, TC), TC)
        mixed = mixed_ref[:, cols]
        attended = x_ref[0, :, cols] + nn(w_out[...], cat3(mixed))
        r2 = lax.rsqrt(jnp.mean(attended * attended, axis=0, keepdims=True) + NORM_EPS)
        scaled = attended * r2
        normed2 = scaled * gain_ffn
        gu = nn(w_gu[...], cat3(normed2))
        gate, up = gu[:ff], gu[ff:]
        sig = 1.0 / (1.0 + jnp.exp(-gate))
        silu = gate * sig
        hidden = silu * up
        act_ref[0, :, cols] = attended + mm_stack(w_down[...], hidden)

        g = cot_ref[0, :, cols]
        dh = nn(w_dh[...], cat3(g))
        dgate = dh * up * (sig + silu * (1.0 - sig))
        dup = dh * silu
        dgu = jnp.concatenate([dgate, dup], axis=0)
        dn2 = mm_stack(w_dgu[...], dgu)
        g_down[...] += outer_sum(hidden, g)
        g_gu[...] += outer_sum(dgu, normed2)
        weighted = dn2 * gain_ffn
        inner = jnp.mean(weighted * attended, axis=0, keepdims=True)
        da = g + r2 * weighted - attended * (r2 * r2 * r2 * inner)
        da_ref[0, :, cols] = da
        g_gf[...] += lane_fold(dn2 * scaled)
        g_out[...] += outer_sum(mixed, da)
        dm = nn(w_dm[...], cat3(da))
        dm_ref[0, :, cols] = dm
        prod = (dm * mixed).reshape(HEADS, HD, TC)
        for h in range(HEADS):
            st_ref[0, 16 + h : 17 + h, cols] = jnp.sum(prod[h], axis=0, keepdims=True)
        return 0

    lax.fori_loop(0, t // TC, feed, 0)

    @pl.when(step == pl.num_programs(0) - 1)
    def _():
        parts = b1_ref.shape[0]
        fs, ds = ff // parts, d // parts
        g_gu_t = g_gu[...].T
        g_down_t = g_down[...].T
        g_out_t = g_out[...].T
        gf = jnp.sum(g_gf[...], axis=1, keepdims=True)
        b1_ref[...] = jnp.zeros_like(b1_ref)
        for n in range(parts):
            gf_own = jnp.concatenate([gf[n * ds : (n + 1) * ds], jnp.zeros((d - ds, 1), F32)], axis=0)
            share = jnp.concatenate([
                g_gu_t[:, n * fs : (n + 1) * fs], g_gu_t[:, ff + n * fs : ff + (n + 1) * fs],
                g_down_t[:, n * fs : (n + 1) * fs], g_out_t[:, n * ds : (n + 1) * ds], gf_own,
            ], axis=1)
            put_share(b1_ref, n, share)


def put_share(ref, n, share):
    rows, cols = share.shape
    pad_rows, pad_cols = -rows % 8, -cols % 128
    if pad_rows:
        share = jnp.concatenate([share, jnp.zeros((pad_rows, cols), F32)], axis=0)
    if pad_cols:
        share = jnp.concatenate([share, jnp.zeros((share.shape[0], pad_cols), F32)], axis=1)
    height = share.shape[0]
    for c in range(share.shape[1] // 128):
        ref[n, c * height : (c + 1) * height, :] = share[:, c * 128 : (c + 1) * 128]


def backward_kernel(
    scale_ref, q_ref, k_ref, v_ref, dm_ref, st_ref, da_ref, x_ref, feat_ref, w_dqkv, gains, cos_ref, sin_ref,
    dx_ref, b2_ref,
    dqkv_ref, g_qkv, g_in, g_ga,
):
    step = pl.program_id(0)
    d, t = q_ref.shape[1], q_ref.shape[2]

    @pl.when(step == 0)
    def _():
        for ref in (g_qkv, g_in, g_ga):
            ref[...] = jnp.zeros_like(ref)

    nb = t // QB
    causal = lax.broadcasted_iota(jnp.int32, (QB, QB), 0) >= lax.broadcasted_iota(jnp.int32, (QB, QB), 1)
    ones = (lax.broadcasted_iota(jnp.int32, (HD, t), 0) < 3).astype(BF16)

    def extras(row):
        a, b, c = split3(row)
        pieces = jnp.concatenate([a.astype(F32), b.astype(F32), c.astype(F32)], axis=0)
        return jnp.concatenate([pieces, jnp.zeros((HD - 3, t), F32)], axis=0)

    def sides(block, row):
        hi, lo = split(block)
        hf, lf = hi.astype(F32), lo.astype(F32)
        tall = jnp.concatenate([hf, lf, hf, extras(-row)], axis=0).T.astype(BF16)
        return tall, jnp.concatenate([hi, lo], axis=0), hi

    def rows_at(first, h):
        return slice(first + h * HD, first + (h + 1) * HD)

    def prepare(h):
        rows = rows_at(0, h)
        qc, qs, qh = sides(q_ref[0, rows, :], st_ref[0, h : h + 1, :])
        mc, ms, mh = sides(dm_ref[0, rows, :], st_ref[0, 16 + h : 17 + h, :])
        kh, kl = split(k_ref[0, rows, :])
        kc = jnp.concatenate([kh, kh, kl, ones], axis=0)
        vh, vl = split(v_ref[0, rows, :])
        vc = jnp.concatenate([vh, vh, vl, ones], axis=0)
        return qc, mc, kc, vc, qs, qh, ms, mh, jnp.concatenate([kh, kl], axis=0), kh

    def tile(item):
        h, kb, qb = item
        return h, slice(kb * QB, (kb + 1) * QB), slice(qb * QB, (qb + 1) * QB)

    def scores(item):
        h, keys, steps = tile(item)
        qc, mc, kc, vc = prepared[h][:4]
        return nn(qc[steps], kc[:, keys]), nn(mc[steps], vc[:, keys])

    def differentiate(item, s, dp):
        h, keys, steps = tile(item)
        kb, qb = item[1:]
        qs, qh, ms, mh, ks, kh = prepared[h][4:]
        p = jnp.exp2(s)
        if kb == qb:
            p = jnp.where(causal, p, 0.0)
        ds = p * dp
        ph, pl_ = split(p)
        dh, dl = split(ds)
        th, tl = split(ds.T)
        both = nn(ms[:, steps], ph)
        dv = both[:HD] + both[HD:] + nn(mh[:, steps], pl_)
        both = nn(qs[:, steps], dh)
        dk = both[:HD] + both[HD:] + nn(qh[:, steps], dl)
        if qb > kb:
            dk, dv = dk + sums[h][0], dv + sums[h][1]
        sums[h] = dk, dv
        if qb == nb - 1:
            dqkv_ref[rows_at(d, h), keys] = dk
            dqkv_ref[rows_at(2 * d, h), keys] = dv
        both = nn(ks[:, keys], th)
        dq = both[:HD] + both[HD:] + nn(kh[:, keys], tl)
        if kb == qb:
            dqkv_ref[rows_at(0, h), steps] = dq
        else:
            dqkv_ref[rows_at(0, h), steps] += dq

    prepared = [prepare(h) for h in range(HEADS)]
    sums = {}
    items = [(h, kb, qb) for kb in reversed(range(nb)) for h in range(HEADS) for qb in range(kb, nb)]
    ahead = {}
    for j in range(len(items) + AHEAD):
        if j < len(items):
            ahead[j] = scores(items[j])
        if j >= AHEAD:
            differentiate(items[j - AHEAD], *ahead.pop(j - AHEAD))

    gain = gains[:, :1]
    scales = row_scales(scale_ref[step], NLAG)

    def finish(i, _):
        cols = pl.ds(pl.multiple_of(i * TD, TD), TD)
        cos, sin = cos_ref[:, cols], -sin_ref[:, cols]
        dq = rotate(dqkv_ref[:d, cols], cos, sin) * HD**-0.5
        dk = rotate(dqkv_ref[d : 2 * d, cols], cos, sin) * LN2
        dqkv = jnp.concatenate([dq, dk, dqkv_ref[2 * d :, cols]], axis=0)
        x = x_ref[0, :, cols]
        r = lax.rsqrt(jnp.mean(x * x, axis=0, keepdims=True) + NORM_EPS)
        xr = x * r
        dn = mm_stack(w_dqkv[...], dqkv)
        g_qkv[...] += outer_sum(dqkv, xr * gain)
        weighted = dn * gain
        inner = jnp.mean(weighted * x, axis=0, keepdims=True)
        dx = da_ref[0, :, cols] + r * weighted - x * (r * r * r * inner)
        dx_ref[0, :, cols] = dx
        g_ga[...] += lane_fold(dn * xr)
        g_in[...] += outer_sum(dx, feat_ref[0, :, cols] * scales)
        return 0

    lax.fori_loop(0, t // TD, finish, 0)

    @pl.when(step == pl.num_programs(0) - 1)
    def _():
        parts = b2_ref.shape[0]
        ds = d // parts
        g_qkv_t = g_qkv[...].T
        ga = jnp.sum(g_ga[...], axis=1, keepdims=True)
        b2_ref[...] = jnp.zeros_like(b2_ref)
        for n in range(parts):
            own = slice(n * ds, (n + 1) * ds)
            put_share(b2_ref, n, jnp.concatenate([g_qkv_t[own], g_in[own, :], ga[own]], axis=1))


def reduce_kernel(b1_ref, b2_ref, out_ref, recv1, pair, recv2, share, recv3, sem_s, sem_r, gsem_s, gsem_r, hsem_s, hsem_r):
    ny = b1_ref.shape[0]
    r1, r2 = b1_ref.shape[2], b2_ref.shape[2]
    groups, chunk = recv3.shape[0], recv3.shape[1]
    g = lax.axis_index("group")
    n = lax.axis_index("narrow")
    core, y = lax.rem(n, 2), lax.div(n, 2)
    other = 1 - core

    def at(group, narrow):
        return (group, narrow)

    mesh_id = pl.DeviceIdType.MESH
    barrier = pltpu.get_barrier_semaphore()
    pl.semaphore_signal(barrier, inc=1, device_id=at(g, y * 2 + other), device_id_type=mesh_id)
    for off in range(1, ny):
        peer = lax.rem(y + off, ny)
        pl.semaphore_signal(barrier, inc=1, device_id=at(g, peer * 2 + core), device_id_type=mesh_id)
    for off in range(1, groups):
        pl.semaphore_signal(barrier, inc=1, device_id=at(lax.rem(g + off, groups), n), device_id_type=mesh_id)
    pl.semaphore_wait(barrier, 1 + (ny - 1) + (groups - 1))

    def copy(src, dst, send, recv, to):
        return pltpu.make_async_remote_copy(
            src_ref=src, dst_ref=dst, send_sem=send, recv_sem=recv, device_id=to, device_id_type=mesh_id
        )

    sibling = at(g, y * 2 + other)
    first = copy(b1_ref.at[:, other], recv1.at[:, pl.ds(0, r1)], sem_s.at[0], sem_r.at[0], sibling)
    second = copy(b2_ref.at[:, other], recv1.at[:, pl.ds(r1, r2)], sem_s.at[1], sem_r.at[1], sibling)
    first.start()
    second.start()
    first.wait_recv()
    second.wait_recv()
    for i in range(ny):
        pair[i, :r1] = b1_ref[i, core] + recv1[i, :r1]
        pair[i, r1 : r1 + r2] = b2_ref[i, core] + recv1[i, r1 : r1 + r2]

    sends = []
    for off in range(1, ny):
        peer = lax.rem(y + off, ny)
        sends.append(copy(pair.at[peer], recv2.at[off - 1], gsem_s.at[off], gsem_r.at[off], at(g, peer * 2 + core)))
        sends[-1].start()
    for s in sends:
        s.wait_recv()
    total = pair[y]
    for off in range(1, ny):
        total += recv2[off - 1]
    share[...] = total.reshape(share.shape)

    sends_b = []
    for off in range(1, groups):
        peer = lax.rem(g + off, groups)
        sends_b.append(copy(share.at[peer], recv3.at[off], hsem_s.at[0, off], hsem_r.at[0, off], at(peer, n)))
        sends_b[-1].start()
    recv3[0] = share[g]
    for s in sends_b:
        s.wait_recv()
    out_ref[g] = jnp.sum(recv3[...], axis=0)
    sends_c = []
    for off in range(1, groups):
        peer = lax.rem(g + off, groups)
        sends_c.append(copy(out_ref.at[g], out_ref.at[g], hsem_s.at[1, off], hsem_r.at[1, off], at(peer, n)))
        sends_c[-1].start()
    for s in sends_c:
        s.wait_recv()
    for s in [first, second] + sends + sends_b + sends_c:
        s.wait_send()


def unpack_kernel(
    total_ref, g_in, g_ga, g_q, g_k, g_v, g_out, g_gf, g_gate, g_up, g_down,
):
    d, fs = g_gate.shape
    ds, nf = g_in.shape
    wide = round_up(3 * fs + ds + 1, 128) // 128
    one = jnp.concatenate([total_ref[c * d : (c + 1) * d, :] for c in range(wide)], axis=1)
    g_gate[...] = one[:, :fs]
    g_up[...] = one[:, fs : 2 * fs]
    g_down[...] = one[:, 2 * fs : 3 * fs]
    g_out[...] = one[:, 3 * fs : 3 * fs + ds].T
    g_gf[...] = one[:ds, 3 * fs + ds]
    base = wide * d
    height = round_up(ds, 8)
    wide = round_up(3 * d + FPAD + 1, 128) // 128
    two = jnp.concatenate([total_ref[base + c * height : base + c * height + ds, :] for c in range(wide)], axis=1)
    g_q[...] = two[:, :d]
    g_k[...] = two[:, d : 2 * d]
    g_v[...] = two[:, 2 * d : 3 * d]
    g_in[...] = two[:, 3 * d : 3 * d + nf]
    g_ga[...] = two[:, 3 * d + FPAD]


def rotation_tables(t):
    freqs = 10000.0 ** (-np.arange(HD // 2, dtype=np.float64) * 2.0 / HD)
    angles = freqs[:, None] * np.arange(t, dtype=np.float64)[None, :]
    return np.cos(angles).astype(np.float32), np.sin(angles).astype(np.float32)


def round_up(n, m):
    return (n + m - 1) // m * m


def on_device(
    groups, parts, series_values, observed, lag_steps, lag_flags, dataset_ids, in_proj, gain_attn, query_proj, key_proj,
    value_proj, out_proj, gain_ffn, gate_proj, up_proj, down_proj, cotangent,
):
    n_series, t = series_values.shape
    nf, d = in_proj.shape
    ff = gate_proj.shape[1]
    fs, ds = ff // parts, d // parts
    onehot, sums = local_sums(series_values, observed, dataset_ids)
    others = exchange_sums(sums, parts)

    cos, sin = rotation_tables(t)
    cos, sin = jnp.asarray(cos), jnp.asarray(sin)
    smem = pl.BlockSpec(memory_space=pltpu.SMEM)
    vmem = pl.BlockSpec(memory_space=pltpu.VMEM)

    def whole(a):
        return pl.BlockSpec(a.shape, lambda i: (0,) * a.ndim)

    def each(rows):
        return pl.BlockSpec((1, rows, t), lambda i: (i, 0, 0))

    def shape(*dims, dtype=F32):
        return jax.ShapeDtypeStruct(dims, dtype)

    params = pltpu.CompilerParams(dimension_semantics=("arbitrary",), vmem_limit_bytes=62 * 2**20)
    plain = pltpu.CompilerParams(vmem_limit_bytes=62 * 2**20)
    in_t, down_t = in_proj.T, down_proj.T
    raw, w_in, w_qkv, w_out, w_gu, w_down, w_dh, w_dgu, w_dm, w_dqkv, gains = pl.pallas_call(
        prepare_kernel,
        in_specs=[smem] * 2 + [vmem] * 12,
        out_specs=[vmem] * 11,
        out_shape=[
            shape(n_series, FPAD, t),
            shape(d, 3 * FPAD, dtype=BF16),
            shape(3 * d, 3 * d, dtype=BF16),
            shape(d, 3 * d, dtype=BF16),
            shape(2 * ff, 3 * d, dtype=BF16),
            shape(2 * d, ff, dtype=BF16),
            shape(ff, 3 * d, dtype=BF16),
            shape(2 * d, 2 * ff, dtype=BF16),
            shape(d, 3 * d, dtype=BF16),
            shape(2 * d, 3 * d, dtype=BF16),
            shape(d, 128),
        ],
        compiler_params=plain,
        cost_estimate=pl.CostEstimate(flops=2 * 10**7, bytes_accessed=8 * 10**6, transcendentals=0),
        name="split_weights_and_shift_lags",
    )(lag_steps, lag_flags, series_values, observed, in_t, query_proj, key_proj, value_proj, out_proj, gate_proj, up_proj,
      down_t, gain_attn, gain_ffn)

    sums = functools.reduce(jnp.add, others, sums)
    set_scale = sums[0] / jnp.maximum(sums[1], 1.0) + SCALE_EPS
    series_scale = jnp.sum(onehot * set_scale[None, :], axis=1)

    rows1 = round_up(3 * fs + ds + 1, 128) // 128 * d
    rows2 = round_up(3 * d + FPAD + 1, 128) // 128 * round_up(ds, 8)
    rows2 = round_up(rows1 + rows2, 8 * groups) - rows1
    full = [w_in, w_qkv, w_out, w_gu, w_down, w_dh, w_dgu, w_dm, gains, cos, sin]
    b1 = shape(parts, rows1, 128)
    act, q, k, v, dm, st, da, x, b1 = pl.pallas_call(
        forward_kernel,
        grid=(n_series,),
        in_specs=[smem, each(FPAD)] + [whole(a) for a in full] + [each(d)],
        out_specs=[each(d)] * 5 + [each(32)] + [each(d)] * 2 + [whole(b1)],
        out_shape=[shape(n_series, d, t)] * 5 + [shape(n_series, 32, t)] + [shape(n_series, d, t)] * 2 + [b1],
        scratch_shapes=[
            pltpu.VMEM((d, t), F32),
            pltpu.VMEM((2 * ff, d), F32),
            pltpu.VMEM((ff, d), F32),
            pltpu.VMEM((d, d), F32),
            pltpu.VMEM((d, 128), F32),
        ],
        compiler_params=params,
        name="forward_and_ffn",
    )(series_scale, raw, *full, jnp.transpose(cotangent, (0, 2, 1)))

    b2 = shape(parts, rows2, 128)
    full = [w_dqkv, gains, cos, sin]
    dx, b2 = pl.pallas_call(
        backward_kernel,
        grid=(n_series,),
        in_specs=[smem] + [each(d)] * 4 + [each(32)] + [each(d)] * 2 + [each(FPAD)] + [whole(a) for a in full],
        out_specs=[each(d), whole(b2)],
        out_shape=[shape(n_series, d, t), b2],
        scratch_shapes=[
            pltpu.VMEM((3 * d, t), F32),
            pltpu.VMEM((3 * d, d), F32),
            pltpu.VMEM((d, FPAD), F32),
            pltpu.VMEM((d, 128), F32),
        ],
        compiler_params=params,
        name="attention_backward",
    )(series_scale, q, k, v, dm, st, da, x, raw, *full)

    total = reduce_grads(b1, b2, groups, parts)
    grads = pl.pallas_call(
        unpack_kernel,
        in_specs=[vmem],
        out_specs=[vmem] * 10,
        out_shape=[
            shape(ds, nf), shape(ds), shape(ds, d), shape(ds, d), shape(ds, d), shape(ds, d), shape(ds),
            shape(d, fs), shape(d, fs), shape(d, fs),
        ],
        compiler_params=plain,
        name="unpack_gradients",
    )(total)
    return (
        jnp.transpose(act, (0, 2, 1)),
        jnp.transpose(dx, (0, 2, 1)),
        grads[0].T,
        *grads[1:9],
        grads[9].T,
    )


def local_sums(series_values, observed, dataset_ids):
    observed_f = observed.astype(F32)
    magnitude = jnp.sum(jnp.abs(series_values) * observed_f, axis=1)
    counted = jnp.sum(observed_f, axis=1)
    onehot = (dataset_ids[:, None] == jnp.arange(DSETS)[None, :]).astype(F32)
    return onehot, jnp.sum(onehot[None] * jnp.stack([magnitude, counted])[:, :, None], axis=1)


def exchange_sums(sums, parts):
    return [lax.ppermute(sums, "narrow", [(i, (i + off) % parts) for i in range(parts)]) for off in range(1, parts)]


def reduce_grads(b1, b2, groups, parts):
    ny = parts // 2
    rows1, rows2 = b1.shape[1], b2.shape[1]
    rows = rows1 + rows2
    chunk = rows // groups
    vmem = pl.BlockSpec(memory_space=pltpu.VMEM)
    dma = pltpu.SemaphoreType.DMA
    total = pl.pallas_call(
        reduce_kernel,
        in_specs=[vmem] * 2,
        out_specs=vmem,
        out_shape=jax.ShapeDtypeStruct((groups, chunk, 128), F32),
        scratch_shapes=[
            pltpu.VMEM((ny, rows, 128), F32),
            pltpu.VMEM((ny, rows, 128), F32),
            pltpu.VMEM((max(ny - 1, 1), rows, 128), F32),
            pltpu.VMEM((groups, chunk, 128), F32),
            pltpu.VMEM((groups, chunk, 128), F32),
            dma((2,)),
            dma((2,)),
            dma((ny,)),
            dma((ny,)),
            dma((2, groups)),
            dma((2, groups)),
        ],
        compiler_params=pltpu.CompilerParams(collective_id=0, has_side_effects=True, vmem_limit_bytes=40 * 2**20),
        name="reduce_gradients",
    )(b1.reshape(ny, 2, rows1, 128), b2.reshape(ny, 2, rows2, 128))
    return total.reshape(rows, 128)


def solution(mesh):
    series = P(("group", "narrow"), None)
    return jax.shard_map(
        functools.partial(on_device, mesh.shape["group"], mesh.shape["narrow"]),
        mesh=mesh,
        in_specs=(series, series, P(), P(), P(("group", "narrow"))) + (P(),) * 10 + (P(("group", "narrow"), None, None),),
        out_specs=(
            P(("group", "narrow"), None, None),
            P(("group", "narrow"), None, None),
            P(None, "narrow"),
            P("narrow"),
            P("narrow", None),
            P("narrow", None),
            P("narrow", None),
            P("narrow", None),
            P("narrow"),
            P(None, "narrow"),
            P(None, "narrow"),
            P("narrow", None),
        ),
        check_vma=False,
    )
```

```python
import functools

import jax
import jax.numpy as jnp
import numpy as np
from jax import lax
from jax.experimental import pallas as pl
from jax.experimental.pallas import tpu as pltpu
from jax.sharding import PartitionSpec as P

HEADS = 9
HD = 16
DSETS = 4
FPAD = 96
QB = 256
TA = 1024
TC = 1024
TD = 1024
NLAG = 84
AHEAD = 2

NORM_EPS = 1e-05
SCALE_EPS = 1e-05
LOG2E = 1.4426950408889634
LN2 = 0.6931471805599453

F32 = jnp.float32
BF16 = jnp.bfloat16


def nn(left, right):
    return lax.dot_general(left, right, (((1,), (0,)), ((), ())), preferred_element_type=F32)


def nt(left, right):
    return lax.dot_general(left, right, (((1,), (1,)), ((), ())), preferred_element_type=F32)


def split(x):
    hi = x.astype(BF16)
    return hi, (x - hi.astype(F32)).astype(BF16)


def split3(x):
    hi = x.astype(BF16)
    rest = x - hi.astype(F32)
    mid = rest.astype(BF16)
    return hi, mid, (rest - mid.astype(F32)).astype(BF16)


def cat3(x):
    hi, lo = split(x)
    return jnp.concatenate([hi, hi, lo], axis=0)


def weight_cat(w):
    hi, lo = split(w)
    hi, lo = hi.astype(F32), lo.astype(F32)
    return jnp.concatenate([hi, lo, hi], axis=0).T.astype(BF16)


def weight_stack(w):
    hi, lo = split(w)
    return jnp.concatenate([hi, lo], axis=0)


def mm_stack(stack, x):
    m = stack.shape[0] // 2
    hi, lo = split(x)
    both = nn(stack, hi)
    return both[:m] + both[m:] + nn(stack[:m], lo)


def outer_sum(left, right):
    m = left.shape[0]
    lh, ll = split(left)
    rh, rl = split(right)
    both = nt(jnp.concatenate([lh, ll], axis=0), rh)
    return both[:m] + both[m:] + nt(lh, rl)


def column(row):
    n = row.shape[0]
    return jnp.broadcast_to(row[None, :], (8, n)).T[:, :1]


def lane_fold(x):
    total = x[:, :128]
    for i in range(1, x.shape[1] // 128):
        total = total + x[:, i * 128 : (i + 1) * 128]
    return total


def rotate(x, cos, sin):
    t = x.shape[1]
    pairs = x.reshape(HEADS, 2, HD // 2, t)
    a, b = pairs[:, 0], pairs[:, 1]
    first = a * cos - b * sin
    second = a * sin + b * cos
    return jnp.stack([first, second], axis=1).reshape(HEADS * HD, t)


def row_scales(scale, nlag):
    row = lax.broadcasted_iota(jnp.int32, (FPAD, 128), 0)
    scales = jnp.full((FPAD, 128), scale, F32)
    inverse, logs = 1.0 / scales, jnp.log(scales)
    return jnp.where(row < nlag, inverse, jnp.where(row == nlag, logs, 1.0))[:, :1]


def prepare_kernel(
    lag_ref, flag_ref, vals_ref, obs_ref, in_ref, wq_ref, wk_ref, wv_ref, wo_ref, wg_ref, wu_ref, wd_ref, ga_ref, gf_ref,
    feat_ref, w_in, w_qkv, w_out, w_gu, w_down, w_dh, w_dgu, w_dm, w_dqkv, gains,
):
    n_series, t = vals_ref.shape
    d, nf = in_ref.shape
    nlag = lag_ref.shape[0]
    ff = wg_ref.shape[1]
    obs = obs_ref[...].astype(F32)
    both = jnp.concatenate([vals_ref[...] * obs, obs], axis=0)
    lanes = lax.broadcasted_iota(jnp.int32, both.shape, 1)

    def one_lag(j, missing):
        lag = lag_ref[j]
        moved = jnp.where(lanes >= lag, pltpu.roll(both, lag, 1), 0.0)
        for s in range(n_series):
            feat_ref[s, pl.ds(j, 1), :] = moved[s : s + 1]
        return missing + flag_ref[j].astype(F32) * (1.0 - moved[n_series:])

    missing = lax.fori_loop(0, nlag, one_lag, jnp.zeros((n_series, t), F32), unroll=12)
    for s in range(n_series):
        feat_ref[s, nlag : nlag + 1, :] = jnp.ones((1, t), F32)
        feat_ref[s, nlag + 1 : nlag + 2, :] = missing[s : s + 1] * nlag**-0.5
        feat_ref[s, nlag + 2 :, :] = jnp.zeros((FPAD - nlag - 2, t), F32)

    w_in_rows = jnp.concatenate([in_ref[...].T, jnp.zeros((FPAD - nf, d), F32)], axis=0)
    w_in[...] = weight_cat(w_in_rows)
    for i, ref in enumerate((wq_ref, wk_ref, wv_ref)):
        w_qkv[i * d : (i + 1) * d, :] = weight_cat(ref[...])
        w_dqkv[:, i * d : (i + 1) * d] = weight_stack(ref[...])
    w_out[...] = weight_cat(wo_ref[...])
    w_gu[:ff, :] = weight_cat(wg_ref[...])
    w_gu[ff:, :] = weight_cat(wu_ref[...])
    w_down[...] = weight_stack(wd_ref[...])
    w_dh[...] = weight_cat(wd_ref[...])
    w_dgu[:, :ff] = weight_stack(wg_ref[...])
    w_dgu[:, ff:] = weight_stack(wu_ref[...])
    w_dm[...] = weight_cat(wo_ref[...].T)
    gains[...] = jnp.zeros_like(gains)
    gains[:, :1] = column(ga_ref[...])
    gains[:, 1:2] = column(gf_ref[...])


def forward_kernel(
    scale_ref, feat_ref, w_in, w_qkv, w_out, w_gu, w_down, w_dh, w_dgu, w_dm, gains, cos_ref, sin_ref, cot_ref,
    act_ref, q_ref, k_ref, v_ref, dm_ref, st_ref, da_ref, x_ref, b1_ref,
    mixed_ref, g_gu, g_down, g_out, g_gf,
):
    step = pl.program_id(0)
    d, t = cot_ref.shape[1], cot_ref.shape[2]
    ff = w_dh.shape[0]
    gain_attn, gain_ffn = gains[:, :1], gains[:, 1:2]
    scales = row_scales(scale_ref[step], NLAG)

    @pl.when(step == 0)
    def _():
        for ref in (g_gu, g_down, g_out, g_gf):
            ref[...] = jnp.zeros_like(ref)

    st_ref[0] = jnp.zeros(st_ref.shape[1:], F32)

    def project(i, _):
        cols = pl.ds(pl.multiple_of(i * TA, TA), TA)
        x = nn(w_in[...], cat3(feat_ref[0, :, cols] * scales))
        x_ref[0, :, cols] = x
        normed = x * lax.rsqrt(jnp.mean(x * x, axis=0, keepdims=True) + NORM_EPS) * gain_attn
        qkv = nn(w_qkv[...], cat3(normed))
        cos, sin = cos_ref[:, cols], sin_ref[:, cols]
        q_ref[0, :, cols] = rotate(qkv[:d], cos, sin) * (HD**-0.5 * LOG2E)
        k_ref[0, :, cols] = rotate(qkv[d : 2 * d], cos, sin)
        v_ref[0, :, cols] = qkv[2 * d :]
        return 0

    lax.fori_loop(0, t // TA, project, 0)

    causal = lax.broadcasted_iota(jnp.int32, (QB, QB), 0) <= lax.broadcasted_iota(jnp.int32, (QB, QB), 1)

    def prepare(h):
        rows = slice(h * HD, (h + 1) * HD)
        qh, ql = split(q_ref[0, rows, :])
        qc = jnp.concatenate([qh, ql, qh], axis=0)
        kh, kl = split(k_ref[0, rows, :])
        kh, kl = kh.astype(F32), kl.astype(F32)
        kc = jnp.concatenate([kh, kh, kl], axis=0).T.astype(BF16)
        vh, vl = split(v_ref[0, rows, :])
        return qc, kc, jnp.concatenate([vh, vl], axis=0), vh

    def scores(sides, item):
        qc, kc = sides[:2]
        lo, top = item[1] * QB, (item[1] + 1) * QB
        return nn(kc[:top], qc[:, lo:top])

    def softmax(s, block):
        lo = block * QB
        last = jnp.where(causal, s[lo:], -1e30)
        s = jnp.concatenate([s[:lo], last], axis=0) if block else last
        return s, jnp.max(s, axis=0, keepdims=True)

    def mix(sides, soft, item):
        h, block = item
        vs, vh = sides[2:]
        s, m = soft
        lo, top = block * QB, (block + 1) * QB
        both = low = total = 0.0
        for c in range(block + 1):
            keys = slice(c * QB, (c + 1) * QB)
            p = jnp.exp2(s[keys] - m)
            total = total + jnp.sum(p, axis=0, keepdims=True)
            ph, pl_ = split(p)
            both = both + nn(vs[:, keys], ph)
            low = low + nn(vh[:, keys], pl_)
        mixed_ref[h * HD : (h + 1) * HD, lo:top] = (both[:HD] + both[HD:] + low) / total
        st_ref[0, h : h + 1, lo:top] = m + jnp.log2(total)

    sides = [prepare(h) for h in range(HEADS)]
    items = [(h, block) for block in reversed(range(t // QB)) for h in range(HEADS)]
    ahead = {}
    for j in range(len(items) + AHEAD):
        if j < len(items):
            ahead[j] = scores(sides[items[j][0]], items[j])
        if j >= AHEAD:
            item = items[j - AHEAD]
            mix(sides[item[0]], softmax(ahead.pop(j - AHEAD), item[1]), item)

    def feed(i, _):
        cols = pl.ds(pl.multiple_of(i * TC, TC), TC)
        mixed = mixed_ref[:, cols]
        attended = x_ref[0, :, cols] + nn(w_out[...], cat3(mixed))
        r2 = lax.rsqrt(jnp.mean(attended * attended, axis=0, keepdims=True) + NORM_EPS)
        scaled = attended * r2
        normed2 = scaled * gain_ffn
        gu = nn(w_gu[...], cat3(normed2))
        gate, up = gu[:ff], gu[ff:]
        sig = 1.0 / (1.0 + jnp.exp(-gate))
        silu = gate * sig
        hidden = silu * up
        act_ref[0, :, cols] = attended + mm_stack(w_down[...], hidden)

        g = cot_ref[0, :, cols]
        dh = nn(w_dh[...], cat3(g))
        dgate = dh * up * (sig + silu * (1.0 - sig))
        dup = dh * silu
        dgu = jnp.concatenate([dgate, dup], axis=0)
        dn2 = mm_stack(w_dgu[...], dgu)
        g_down[...] += outer_sum(hidden, g)
        g_gu[...] += outer_sum(dgu, normed2)
        weighted = dn2 * gain_ffn
        inner = jnp.mean(weighted * attended, axis=0, keepdims=True)
        da = g + r2 * weighted - attended * (r2 * r2 * r2 * inner)
        da_ref[0, :, cols] = da
        g_gf[...] += lane_fold(dn2 * scaled)
        g_out[...] += outer_sum(mixed, da)
        dm = nn(w_dm[...], cat3(da))
        dm_ref[0, :, cols] = dm
        prod = (dm * mixed).reshape(HEADS, HD, TC)
        for h in range(HEADS):
            st_ref[0, 16 + h : 17 + h, cols] = jnp.sum(prod[h], axis=0, keepdims=True)
        return 0

    lax.fori_loop(0, t // TC, feed, 0)

    @pl.when(step == pl.num_programs(0) - 1)
    def _():
        parts = 2 * b1_ref.shape[0]
        fs, ds = ff // parts, d // parts
        g_gu_t = g_gu[...].T
        g_down_t = g_down[...].T
        g_out_t = g_out[...].T
        gf = jnp.sum(g_gf[...], axis=1, keepdims=True)
        for n in range(parts):
            gf_own = jnp.concatenate([gf[n * ds : (n + 1) * ds], jnp.zeros((d - ds, 1), F32)], axis=0)
            share = jnp.concatenate([
                g_gu_t[:, n * fs : (n + 1) * fs], g_gu_t[:, ff + n * fs : ff + (n + 1) * fs],
                g_down_t[:, n * fs : (n + 1) * fs], g_out_t[:, n * ds : (n + 1) * ds], gf_own,
            ], axis=1)
            b1_ref[n // 2, n % 2] = stack_columns(share, b1_ref.shape[2])


def stack_columns(share, height):
    rows, cols = share.shape
    pad_cols = -cols % 128
    if pad_cols:
        share = jnp.concatenate([share, jnp.zeros((rows, pad_cols), F32)], axis=1)
    pieces = [share[:, c * 128 : (c + 1) * 128] for c in range(share.shape[1] // 128)]
    left = height - len(pieces) * rows
    if left:
        pieces.append(jnp.zeros((left, 128), F32))
    return jnp.concatenate(pieces, axis=0)


def at(group, narrow):
    return (group, narrow)


def greet(groups, ny):
    g, n = lax.axis_index("group"), lax.axis_index("narrow")
    core, y = lax.rem(n, 2), lax.div(n, 2)
    barrier = pltpu.get_barrier_semaphore()
    peers = [at(g, y * 2 + 1 - core)]
    peers += [at(g, lax.rem(y + off, ny) * 2 + core) for off in range(1, ny)]
    peers += [at(lax.rem(g + off, groups), n) for off in range(1, groups)]
    for peer in peers:
        pl.semaphore_signal(barrier, inc=1, device_id=peer, device_id_type=pl.DeviceIdType.MESH)
    pl.semaphore_wait(barrier, len(peers))


def share_phases(src, total_ref, base, recv1, pair, recv2, share, recv3, send_sem, recv_sem):
    ny, rows = src.shape[0], src.shape[2]
    groups, chunk = recv3.shape[0], recv3.shape[1]
    g, n = lax.axis_index("group"), lax.axis_index("narrow")
    core, y = lax.rem(n, 2), lax.div(n, 2)

    def copy(i, source, target, to):
        return pltpu.make_async_remote_copy(
            src_ref=source, dst_ref=target, send_sem=send_sem.at[i], recv_sem=recv_sem.at[i], device_id=to,
            device_id_type=pl.DeviceIdType.MESH,
        )

    def over_core():
        return [copy(0, src.at[:, 1 - core], recv1, at(g, y * 2 + 1 - core))]

    def over_y():
        peers = [lax.rem(y + off, ny) for off in range(1, ny)]
        return [copy(1 + i, pair.at[p], recv2.at[i], at(g, p * 2 + core)) for i, p in enumerate(peers)]

    def over_group():
        peers = [lax.rem(g + off, groups) for off in range(1, groups)]
        return [copy(ny + i, share.at[p], recv3.at[1 + i], at(p, n)) for i, p in enumerate(peers)]

    def gather():
        own = total_ref.at[g, pl.ds(base, chunk)]
        peers = [lax.rem(g + off, groups) for off in range(1, groups)]
        return [copy(ny + groups - 1 + i, own, own, at(p, n)) for i, p in enumerate(peers)]

    def start(copies):
        for c in copies:
            c.start()

    def arrive(copies):
        for c in copies:
            c.wait_recv()

    def one():
        start(over_core())

    def two():
        arrive(over_core())
        for i in range(ny):
            pair[i] = src[i, core] + recv1[i]
        start(over_y())

    def three():
        arrive(over_y())
        total = pair[y]
        for i in range(ny - 1):
            total += recv2[i]
        share[...] = total.reshape(groups, chunk, 128)
        start(over_group())

    def four():
        recv3[0] = share[g]
        arrive(over_group())
        total_ref[g, base : base + chunk] = jnp.sum(recv3[...], axis=0)
        start(gather())

    def five():
        arrive(gather())
        for copies in (over_core(), over_y(), over_group(), gather()):
            for c in copies:
                c.wait_send()

    return one, two, three, four, five


def backward_kernel(
    dx_steps, scale_ref, q_ref, k_ref, v_ref, dm_ref, st_ref, da_ref, x_ref, feat_ref, w_dqkv, gains, cos_ref, sin_ref, b1_ref,
    dx_ref, out_ref,
    dqkv_ref, g_qkv, g_in, g_ga, b2_ref, total_ref, *buffers,
):
    step = pl.program_id(0)
    early = share_phases(b1_ref, total_ref, 0, *buffers[:7])
    late = share_phases(b2_ref, total_ref, b1_ref.shape[2] // total_ref.shape[0], *buffers[7:])

    @pl.when(step == 0)
    def _():
        greet(total_ref.shape[0], b1_ref.shape[0])

    for i, phase in enumerate(early[:4]):

        @pl.when(step == min(i, dx_steps - 1))
        def _():
            phase()

    d, t = q_ref.shape[1], q_ref.shape[2]

    @pl.when(step == 0)
    def _():
        for ref in (g_qkv, g_in, g_ga):
            ref[...] = jnp.zeros_like(ref)

    nb = t // QB
    causal = lax.broadcasted_iota(jnp.int32, (QB, QB), 0) >= lax.broadcasted_iota(jnp.int32, (QB, QB), 1)
    ones = (lax.broadcasted_iota(jnp.int32, (HD, t), 0) < 3).astype(BF16)

    def extras(row):
        a, b, c = split3(row)
        pieces = jnp.concatenate([a.astype(F32), b.astype(F32), c.astype(F32)], axis=0)
        return jnp.concatenate([pieces, jnp.zeros((HD - 3, t), F32)], axis=0)

    def sides(block, row):
        hi, lo = split(block)
        hf, lf = hi.astype(F32), lo.astype(F32)
        tall = jnp.concatenate([hf, lf, hf, extras(-row)], axis=0).T.astype(BF16)
        return tall, jnp.concatenate([hi, lo], axis=0), hi

    def rows_at(first, h):
        return slice(first + h * HD, first + (h + 1) * HD)

    def prepare(h):
        rows = rows_at(0, h)
        qc, qs, qh = sides(q_ref[0, rows, :], st_ref[0, h : h + 1, :])
        mc, ms, mh = sides(dm_ref[0, rows, :], st_ref[0, 16 + h : 17 + h, :])
        kh, kl = split(k_ref[0, rows, :])
        kc = jnp.concatenate([kh, kh, kl, ones], axis=0)
        vh, vl = split(v_ref[0, rows, :])
        vc = jnp.concatenate([vh, vh, vl, ones], axis=0)
        return qc, mc, kc, vc, qs, qh, ms, mh, jnp.concatenate([kh, kl], axis=0), kh

    def tile(item):
        h, kb, qb = item
        return h, slice(kb * QB, (kb + 1) * QB), slice(qb * QB, (qb + 1) * QB)

    def scores(item):
        h, keys, steps = tile(item)
        qc, mc, kc, vc = prepared[h][:4]
        return nn(qc[steps], kc[:, keys]), nn(mc[steps], vc[:, keys])

    def differentiate(item, s, dp):
        h, keys, steps = tile(item)
        kb, qb = item[1:]
        qs, qh, ms, mh, ks, kh = prepared[h][4:]
        p = jnp.exp2(s)
        if kb == qb:
            p = jnp.where(causal, p, 0.0)
        ds = p * dp
        ph, pl_ = split(p)
        dh, dl = split(ds)
        th, tl = split(ds.T)
        both = nn(ms[:, steps], ph)
        dv = both[:HD] + both[HD:] + nn(mh[:, steps], pl_)
        both = nn(qs[:, steps], dh)
        dk = both[:HD] + both[HD:] + nn(qh[:, steps], dl)
        if qb > kb:
            dk, dv = dk + sums[h][0], dv + sums[h][1]
        sums[h] = dk, dv
        if qb == nb - 1:
            dqkv_ref[rows_at(d, h), keys] = dk
            dqkv_ref[rows_at(2 * d, h), keys] = dv
        both = nn(ks[:, keys], th)
        dq = both[:HD] + both[HD:] + nn(kh[:, keys], tl)
        if kb == qb:
            dqkv_ref[rows_at(0, h), steps] = dq
        else:
            dqkv_ref[rows_at(0, h), steps] += dq

    prepared = [prepare(h) for h in range(HEADS)]
    sums = {}
    items = [(h, kb, qb) for kb in reversed(range(nb)) for h in range(HEADS) for qb in range(kb, nb)]
    ahead = {}
    for j in range(len(items) + AHEAD):
        if j < len(items):
            ahead[j] = scores(items[j])
        if j >= AHEAD:
            differentiate(items[j - AHEAD], *ahead.pop(j - AHEAD))

    gain = gains[:, :1]
    scales = row_scales(scale_ref[step], NLAG)

    def finish(i, _):
        cols = pl.ds(pl.multiple_of(i * TD, TD), TD)
        cos, sin = cos_ref[:, cols], -sin_ref[:, cols]
        dq = rotate(dqkv_ref[:d, cols], cos, sin) * HD**-0.5
        dk = rotate(dqkv_ref[d : 2 * d, cols], cos, sin) * LN2
        dqkv = jnp.concatenate([dq, dk, dqkv_ref[2 * d :, cols]], axis=0)
        x = x_ref[0, :, cols]
        r = lax.rsqrt(jnp.mean(x * x, axis=0, keepdims=True) + NORM_EPS)
        xr = x * r
        dn = mm_stack(w_dqkv[...], dqkv)
        g_qkv[...] += outer_sum(dqkv, xr * gain)
        weighted = dn * gain
        inner = jnp.mean(weighted * x, axis=0, keepdims=True)
        dx = da_ref[0, :, cols] + r * weighted - x * (r * r * r * inner)
        dx_ref[0, :, cols] = dx
        g_ga[...] += lane_fold(dn * xr)
        g_in[...] += outer_sum(dx, feat_ref[0, :, cols] * scales)
        return 0

    lax.fori_loop(0, t // TD, finish, 0)

    @pl.when(step == pl.num_programs(0) - 1)
    def _():
        parts = 2 * b2_ref.shape[0]
        ds = d // parts
        g_qkv_t = g_qkv[...].T
        ga = jnp.sum(g_ga[...], axis=1, keepdims=True)
        for n in range(parts):
            own = slice(n * ds, (n + 1) * ds)
            share = jnp.concatenate([g_qkv_t[own], g_in[own, :], ga[own]], axis=1)
            b2_ref[n // 2, n % 2] = stack_columns(share, b2_ref.shape[2])
        for phase in late[:4]:
            phase()
        for end in (early[4], late[4]):
            end()
        out_ref[...] = total_ref[...]


def unpack_kernel(total_ref, dx_ref, dx_out, *grads):
    dx_out[...] = dx_ref[...]

    @pl.when(pl.program_id(0) == 0)
    def _():
        unpack(total_ref, *grads)


def unpack(total_ref, g_in, g_ga, g_q, g_k, g_v, g_out, g_gf, g_gate, g_up, g_down):
    d, fs = g_gate.shape
    ds, nf = g_in.shape
    groups = total_ref.shape[0]
    wide = round_up(3 * fs + ds + 1, 128) // 128
    c1 = round_up(wide * d, 8 * groups) // groups
    one = jnp.concatenate([total_ref[g, :c1] for g in range(groups)], axis=0)
    one = jnp.concatenate([one[c * d : (c + 1) * d, :] for c in range(wide)], axis=1)
    g_gate[...] = one[:, :fs]
    g_up[...] = one[:, fs : 2 * fs]
    g_down[...] = one[:, 2 * fs : 3 * fs]
    g_out[...] = one[:, 3 * fs : 3 * fs + ds].T
    g_gf[...] = one[:ds, 3 * fs + ds]
    wide = round_up(3 * d + FPAD + 1, 128) // 128
    two = jnp.concatenate([total_ref[g, c1:] for g in range(groups)], axis=0)
    two = jnp.concatenate([two[c * ds : (c + 1) * ds, :] for c in range(wide)], axis=1)
    g_q[...] = two[:, :d]
    g_k[...] = two[:, d : 2 * d]
    g_v[...] = two[:, 2 * d : 3 * d]
    g_in[...] = two[:, 3 * d : 3 * d + nf]
    g_ga[...] = two[:, 3 * d + FPAD]


def rotation_tables(t):
    freqs = 10000.0 ** (-np.arange(HD // 2, dtype=np.float64) * 2.0 / HD)
    angles = freqs[:, None] * np.arange(t, dtype=np.float64)[None, :]
    return np.cos(angles).astype(np.float32), np.sin(angles).astype(np.float32)


def round_up(n, m):
    return (n + m - 1) // m * m


def on_device(
    groups, parts, series_values, observed, lag_steps, lag_flags, dataset_ids, in_proj, gain_attn, query_proj, key_proj,
    value_proj, out_proj, gain_ffn, gate_proj, up_proj, down_proj, cotangent,
):
    n_series, t = series_values.shape
    nf, d = in_proj.shape
    ff = gate_proj.shape[1]
    fs, ds = ff // parts, d // parts
    onehot, sums = local_sums(series_values, observed, dataset_ids)
    others = exchange_sums(sums, parts)

    cos, sin = rotation_tables(t)
    cos, sin = jnp.asarray(cos), jnp.asarray(sin)
    smem = pl.BlockSpec(memory_space=pltpu.SMEM)
    vmem = pl.BlockSpec(memory_space=pltpu.VMEM)

    def whole(a):
        return pl.BlockSpec(a.shape, lambda i: (0,) * a.ndim)

    def each(rows):
        return pl.BlockSpec((1, rows, t), lambda i: (i, 0, 0))

    def shape(*dims, dtype=F32):
        return jax.ShapeDtypeStruct(dims, dtype)

    params = pltpu.CompilerParams(dimension_semantics=("arbitrary",), vmem_limit_bytes=62 * 2**20)
    plain = pltpu.CompilerParams(vmem_limit_bytes=62 * 2**20)
    in_t, down_t = in_proj.T, down_proj.T
    raw, w_in, w_qkv, w_out, w_gu, w_down, w_dh, w_dgu, w_dm, w_dqkv, gains = pl.pallas_call(
        prepare_kernel,
        in_specs=[smem] * 2 + [vmem] * 12,
        out_specs=[vmem] * 11,
        out_shape=[
            shape(n_series, FPAD, t),
            shape(d, 3 * FPAD, dtype=BF16),
            shape(3 * d, 3 * d, dtype=BF16),
            shape(d, 3 * d, dtype=BF16),
            shape(2 * ff, 3 * d, dtype=BF16),
            shape(2 * d, ff, dtype=BF16),
            shape(ff, 3 * d, dtype=BF16),
            shape(2 * d, 2 * ff, dtype=BF16),
            shape(d, 3 * d, dtype=BF16),
            shape(2 * d, 3 * d, dtype=BF16),
            shape(d, 128),
        ],
        compiler_params=plain,
        cost_estimate=pl.CostEstimate(flops=2 * 10**7, bytes_accessed=8 * 10**6, transcendentals=0),
        name="split_weights_and_shift_lags",
    )(lag_steps, lag_flags, series_values, observed, in_t, query_proj, key_proj, value_proj, out_proj, gate_proj, up_proj,
      down_t, gain_attn, gain_ffn)

    sums = functools.reduce(jnp.add, others, sums)
    set_scale = sums[0] / jnp.maximum(sums[1], 1.0) + SCALE_EPS
    series_scale = jnp.sum(onehot * set_scale[None, :], axis=1)

    rows1 = round_up(round_up(3 * fs + ds + 1, 128) // 128 * d, 8 * groups)
    rows2 = round_up(round_up(3 * d + FPAD + 1, 128) // 128 * ds, 8 * groups)
    full = [w_in, w_qkv, w_out, w_gu, w_down, w_dh, w_dgu, w_dm, gains, cos, sin]
    b1 = shape(parts // 2, 2, rows1, 128)
    act, q, k, v, dm, st, da, x, b1 = pl.pallas_call(
        forward_kernel,
        grid=(n_series,),
        in_specs=[smem, each(FPAD)] + [whole(a) for a in full] + [each(d)],
        out_specs=[each(d)] * 5 + [each(32)] + [each(d)] * 2 + [whole(b1)],
        out_shape=[shape(n_series, d, t)] * 5 + [shape(n_series, 32, t)] + [shape(n_series, d, t)] * 2 + [b1],
        scratch_shapes=[
            pltpu.VMEM((d, t), F32),
            pltpu.VMEM((2 * ff, d), F32),
            pltpu.VMEM((ff, d), F32),
            pltpu.VMEM((d, d), F32),
            pltpu.VMEM((d, 128), F32),
        ],
        compiler_params=params,
        name="forward_and_ffn",
    )(series_scale, raw, *full, jnp.transpose(cotangent, (0, 2, 1)))

    ny = parts // 2
    c1, c2 = rows1 // groups, rows2 // groups
    total = shape(groups, c1 + c2, 128)
    full = [w_dqkv, gains, cos, sin, b1]
    copies = ny + 2 * (groups - 1)
    dma = pltpu.SemaphoreType.DMA
    buffers = []
    for rows, chunk in ((rows1, c1), (rows2, c2)):
        buffers += [
            pltpu.VMEM((ny, rows, 128), F32),
            pltpu.VMEM((ny, rows, 128), F32),
            pltpu.VMEM((max(ny - 1, 1), rows, 128), F32),
            pltpu.VMEM((groups, chunk, 128), F32),
            pltpu.VMEM((groups, chunk, 128), F32),
            dma((copies,)),
            dma((copies,)),
        ]
    dx, total = pl.pallas_call(
        functools.partial(backward_kernel, n_series),
        grid=(n_series,),
        in_specs=[smem] + [each(d)] * 4 + [each(32)] + [each(d)] * 2 + [each(FPAD)] + [whole(a) for a in full],
        out_specs=[each(d), whole(total)],
        out_shape=[shape(n_series, d, t), total],
        scratch_shapes=[
            pltpu.VMEM((3 * d, t), F32),
            pltpu.VMEM((3 * d, d), F32),
            pltpu.VMEM((d, FPAD), F32),
            pltpu.VMEM((d, 128), F32),
            pltpu.VMEM((ny, 2, rows2, 128), F32),
            pltpu.VMEM((groups, c1 + c2, 128), F32),
            *buffers,
        ],
        compiler_params=pltpu.CompilerParams(
            dimension_semantics=("arbitrary",), vmem_limit_bytes=62 * 2**20, collective_id=0, has_side_effects=True
        ),
        name="attention_backward_and_sums",
    )(series_scale, q, k, v, dm, st, da, x, raw, *full)

    grads = [
        shape(ds, nf), shape(ds), shape(ds, d), shape(ds, d), shape(ds, d), shape(ds, d), shape(ds),
        shape(d, fs), shape(d, fs), shape(d, fs),
    ]
    dx, *grads = pl.pallas_call(
        unpack_kernel,
        grid=(n_series,),
        in_specs=[whole(total), each(d)],
        out_specs=[each(d)] + [whole(a) for a in grads],
        out_shape=[shape(n_series, d, t)] + grads,
        compiler_params=params,
        name="unpack_gradients",
    )(total, dx)
    return (
        jnp.transpose(act, (0, 2, 1)),
        jnp.transpose(dx, (0, 2, 1)),
        grads[0].T,
        *grads[1:9],
        grads[9].T,
    )


def local_sums(series_values, observed, dataset_ids):
    observed_f = observed.astype(F32)
    magnitude = jnp.sum(jnp.abs(series_values) * observed_f, axis=1)
    counted = jnp.sum(observed_f, axis=1)
    onehot = (dataset_ids[:, None] == jnp.arange(DSETS)[None, :]).astype(F32)
    return onehot, jnp.sum(onehot[None] * jnp.stack([magnitude, counted])[:, :, None], axis=1)


def exchange_sums(sums, parts):
    return [lax.ppermute(sums, "narrow", [(i, (i + off) % parts) for i in range(parts)]) for off in range(1, parts)]


def solution(mesh):
    series = P(("group", "narrow"), None)
    return jax.shard_map(
        functools.partial(on_device, mesh.shape["group"], mesh.shape["narrow"]),
        mesh=mesh,
        in_specs=(series, series, P(), P(), P(("group", "narrow"))) + (P(),) * 10 + (P(("group", "narrow"), None, None),),
        out_specs=(
            P(("group", "narrow"), None, None),
            P(("group", "narrow"), None, None),
            P(None, "narrow"),
            P("narrow"),
            P("narrow", None),
            P("narrow", None),
            P("narrow", None),
            P("narrow", None),
            P("narrow"),
            P(None, "narrow"),
            P(None, "narrow"),
            P("narrow", None),
        ),
        check_vma=False,
    )
```

```python
import functools

import jax
import jax.numpy as jnp
import numpy as np
from jax import lax
from jax.experimental import pallas as pl
from jax.experimental.pallas import tpu as pltpu
from jax.sharding import PartitionSpec as P

HEADS = 9
HD = 16
DSETS = 4
FPAD = 96
QB = 256
TA = 1024
TC = 1024
TD = 1024
NLAG = 84
AHEAD = 2

NORM_EPS = 1e-05
SCALE_EPS = 1e-05
LOG2E = 1.4426950408889634
LN2 = 0.6931471805599453

F32 = jnp.float32
BF16 = jnp.bfloat16


def nn(left, right):
    return lax.dot_general(left, right, (((1,), (0,)), ((), ())), preferred_element_type=F32)


def nt(left, right):
    return lax.dot_general(left, right, (((1,), (1,)), ((), ())), preferred_element_type=F32)


def split(x):
    hi = x.astype(BF16)
    return hi, (x - hi.astype(F32)).astype(BF16)


def split3(x):
    hi = x.astype(BF16)
    rest = x - hi.astype(F32)
    mid = rest.astype(BF16)
    return hi, mid, (rest - mid.astype(F32)).astype(BF16)


def cat3(x):
    hi, lo = split(x)
    return jnp.concatenate([hi, hi, lo], axis=0)


def weight_cat(w):
    hi, lo = split(w)
    hi, lo = hi.astype(F32), lo.astype(F32)
    return jnp.concatenate([hi, lo, hi], axis=0).T.astype(BF16)


def weight_stack(w):
    hi, lo = split(w)
    return jnp.concatenate([hi, lo], axis=0)


def mm_stack(stack, x):
    m = stack.shape[0] // 2
    hi, lo = split(x)
    both = nn(stack, hi)
    return both[:m] + both[m:] + nn(stack[:m], lo)


def outer_sum(left, right):
    m = left.shape[0]
    lh, ll = split(left)
    rh, rl = split(right)
    both = nt(jnp.concatenate([lh, ll], axis=0), rh)
    return both[:m] + both[m:] + nt(lh, rl)


def column(row):
    n = row.shape[0]
    return jnp.broadcast_to(row[None, :], (8, n)).T[:, :1]


def lane_fold(x):
    total = x[:, :128]
    for i in range(1, x.shape[1] // 128):
        total = total + x[:, i * 128 : (i + 1) * 128]
    return total


def rotate(x, cos, sin):
    t = x.shape[1]
    pairs = x.reshape(HEADS, 2, HD // 2, t)
    a, b = pairs[:, 0], pairs[:, 1]
    first = a * cos - b * sin
    second = a * sin + b * cos
    return jnp.stack([first, second], axis=1).reshape(HEADS * HD, t)


def row_scales(scale, nlag):
    row = lax.broadcasted_iota(jnp.int32, (FPAD, 128), 0)
    scales = jnp.broadcast_to(scale, (FPAD, 128))
    inverse, logs = 1.0 / scales, jnp.log(scales)
    return jnp.where(row < nlag, inverse, jnp.where(row == nlag, logs, 1.0))[:, :1]


def prepare_kernel(
    parts, lag_ref, flag_ref, ids_ref, vals_ref, obs_ref, in_ref, wq_ref, wk_ref, wv_ref, wo_ref, wg_ref, wu_ref, wd_ref,
    ga_ref, gf_ref,
    scale_ref, feat_ref, w_in, w_qkv, w_out, w_gu, w_down, w_dh, w_dgu, w_dm, w_dqkv, gains,
    own, others, send_sem, recv_sem,
):
    n_series, t = vals_ref.shape
    d, nf = in_ref.shape
    nlag = lag_ref.shape[0]
    ff = wg_ref.shape[1]
    obs = obs_ref[...].astype(F32)
    both = jnp.concatenate([vals_ref[...] * obs, obs], axis=0)

    g, n = lax.axis_index("group"), lax.axis_index("narrow")
    barrier = pltpu.get_barrier_semaphore()
    copies = []
    for off in range(1, parts):
        peer = (g, lax.rem(n + off, parts))
        pl.semaphore_signal(barrier, inc=1, device_id=peer, device_id_type=pl.DeviceIdType.MESH)
        copies.append(pltpu.make_async_remote_copy(
            src_ref=own, dst_ref=others.at[off - 1], send_sem=send_sem.at[off - 1], recv_sem=recv_sem.at[off - 1],
            device_id=peer, device_id_type=pl.DeviceIdType.MESH,
        ))
    series = lax.broadcasted_iota(jnp.int32, (n_series, 128), 0)
    ids = jnp.zeros((n_series, 128), jnp.int32)
    for s in range(n_series):
        ids = jnp.where(series == s, ids_ref[s], ids)
    member = (lax.broadcasted_iota(jnp.int32, (n_series, 128), 1) == ids).astype(F32)
    magnitude = jnp.sum(jnp.abs(both[:n_series]), axis=1, keepdims=True)
    counted = jnp.sum(obs, axis=1, keepdims=True)
    own[...] = jnp.concatenate([
        jnp.sum(member * magnitude, axis=0, keepdims=True), jnp.sum(member * counted, axis=0, keepdims=True),
        jnp.zeros((6, 128), F32),
    ], axis=0)

    lanes = lax.broadcasted_iota(jnp.int32, both.shape, 1)

    def one_lag(j, missing):
        lag = lag_ref[j]
        moved = jnp.where(lanes >= lag, pltpu.roll(both, lag, 1), 0.0)
        for s in range(n_series):
            feat_ref[s, pl.ds(j, 1), :] = moved[s : s + 1]
        return missing + flag_ref[j].astype(F32) * (1.0 - moved[n_series:])

    missing = lax.fori_loop(0, nlag, one_lag, jnp.zeros((n_series, t), F32), unroll=12)
    for s in range(n_series):
        feat_ref[s, nlag : nlag + 1, :] = jnp.ones((1, t), F32)
        feat_ref[s, nlag + 1 : nlag + 2, :] = missing[s : s + 1] * nlag**-0.5
        feat_ref[s, nlag + 2 :, :] = jnp.zeros((FPAD - nlag - 2, t), F32)

    pl.semaphore_wait(barrier, parts - 1)
    for c in copies:
        c.start()

    w_in_rows = jnp.concatenate([in_ref[...].T, jnp.zeros((FPAD - nf, d), F32)], axis=0)
    w_in[...] = weight_cat(w_in_rows)
    for i, ref in enumerate((wq_ref, wk_ref, wv_ref)):
        w_qkv[i * d : (i + 1) * d, :] = weight_cat(ref[...])
        w_dqkv[:, i * d : (i + 1) * d] = weight_stack(ref[...])
    w_out[...] = weight_cat(wo_ref[...])
    w_gu[:ff, :] = weight_cat(wg_ref[...])
    w_gu[ff:, :] = weight_cat(wu_ref[...])
    w_down[...] = weight_stack(wd_ref[...])
    w_dh[...] = weight_cat(wd_ref[...])
    w_dgu[:, :ff] = weight_stack(wg_ref[...])
    w_dgu[:, ff:] = weight_stack(wu_ref[...])
    w_dm[...] = weight_cat(wo_ref[...].T)
    gains[...] = jnp.zeros_like(gains)
    gains[:, :1] = column(ga_ref[...])
    gains[:, 1:2] = column(gf_ref[...])

    for c in copies:
        c.wait()
    total = own[...]
    for i in range(parts - 1):
        total = total + others[i]
    set_scale = total[:1] / jnp.maximum(total[1:2], 1.0) + SCALE_EPS
    series_scale = jnp.sum(jnp.where(member > 0.0, set_scale, 0.0), axis=1, keepdims=True)
    scale_ref[...] = jnp.broadcast_to(series_scale, scale_ref.shape)


def forward_kernel(
    scale_ref, feat_ref, w_in, w_qkv, w_out, w_gu, w_down, w_dh, w_dgu, w_dm, gains, cos_ref, sin_ref, cot_ref,
    act_ref, q_ref, k_ref, v_ref, dm_ref, st_ref, da_ref, x_ref, b1_ref,
    mixed_ref, g_gu, g_down, g_out, g_gf,
):
    step = pl.program_id(0)
    d, t = cot_ref.shape[1], cot_ref.shape[2]
    ff = w_dh.shape[0]
    gain_attn, gain_ffn = gains[:, :1], gains[:, 1:2]
    scales = row_scales(scale_ref[pl.ds(step, 1), :], NLAG)

    @pl.when(step == 0)
    def _():
        for ref in (g_gu, g_down, g_out, g_gf):
            ref[...] = jnp.zeros_like(ref)

    st_ref[0] = jnp.zeros(st_ref.shape[1:], F32)

    def project(i, _):
        cols = pl.ds(pl.multiple_of(i * TA, TA), TA)
        x = nn(w_in[...], cat3(feat_ref[0, :, cols] * scales))
        x_ref[0, :, cols] = x
        normed = x * lax.rsqrt(jnp.mean(x * x, axis=0, keepdims=True) + NORM_EPS) * gain_attn
        qkv = nn(w_qkv[...], cat3(normed))
        cos, sin = cos_ref[:, cols], sin_ref[:, cols]
        q_ref[0, :, cols] = rotate(qkv[:d], cos, sin) * (HD**-0.5 * LOG2E)
        k_ref[0, :, cols] = rotate(qkv[d : 2 * d], cos, sin)
        v_ref[0, :, cols] = qkv[2 * d :]
        return 0

    lax.fori_loop(0, t // TA, project, 0)

    causal = lax.broadcasted_iota(jnp.int32, (QB, QB), 0) <= lax.broadcasted_iota(jnp.int32, (QB, QB), 1)

    def prepare(h):
        rows = slice(h * HD, (h + 1) * HD)
        qh, ql = split(q_ref[0, rows, :])
        qc = jnp.concatenate([qh, ql, qh], axis=0)
        kh, kl = split(k_ref[0, rows, :])
        kh, kl = kh.astype(F32), kl.astype(F32)
        kc = jnp.concatenate([kh, kh, kl], axis=0).T.astype(BF16)
        vh, vl = split(v_ref[0, rows, :])
        return qc, kc, jnp.concatenate([vh, vl], axis=0), vh

    def scores(sides, item):
        qc, kc = sides[:2]
        lo, top = item[1] * QB, (item[1] + 1) * QB
        return nn(kc[:top], qc[:, lo:top])

    def softmax(s, block):
        lo = block * QB
        last = jnp.where(causal, s[lo:], -1e30)
        s = jnp.concatenate([s[:lo], last], axis=0) if block else last
        return s, jnp.max(s, axis=0, keepdims=True)

    def mix(sides, soft, item):
        h, block = item
        vs, vh = sides[2:]
        s, m = soft
        lo, top = block * QB, (block + 1) * QB
        both = low = total = 0.0
        for c in range(block + 1):
            keys = slice(c * QB, (c + 1) * QB)
            p = jnp.exp2(s[keys] - m)
            total = total + jnp.sum(p, axis=0, keepdims=True)
            ph, pl_ = split(p)
            both = both + nn(vs[:, keys], ph)
            low = low + nn(vh[:, keys], pl_)
        mixed_ref[h * HD : (h + 1) * HD, lo:top] = (both[:HD] + both[HD:] + low) / total
        st_ref[0, h : h + 1, lo:top] = m + jnp.log2(total)

    sides = [prepare(h) for h in range(HEADS)]
    items = [(h, block) for block in reversed(range(t // QB)) for h in range(HEADS)]
    ahead = {}
    for j in range(len(items) + AHEAD):
        if j < len(items):
            ahead[j] = scores(sides[items[j][0]], items[j])
        if j >= AHEAD:
            item = items[j - AHEAD]
            mix(sides[item[0]], softmax(ahead.pop(j - AHEAD), item[1]), item)

    def feed(i, _):
        cols = pl.ds(pl.multiple_of(i * TC, TC), TC)
        mixed = mixed_ref[:, cols]
        attended = x_ref[0, :, cols] + nn(w_out[...], cat3(mixed))
        r2 = lax.rsqrt(jnp.mean(attended * attended, axis=0, keepdims=True) + NORM_EPS)
        scaled = attended * r2
        normed2 = scaled * gain_ffn
        gu = nn(w_gu[...], cat3(normed2))
        gate, up = gu[:ff], gu[ff:]
        sig = 1.0 / (1.0 + jnp.exp(-gate))
        silu = gate * sig
        hidden = silu * up
        act_ref[0, :, cols] = attended + mm_stack(w_down[...], hidden)

        g = cot_ref[0, :, cols]
        dh = nn(w_dh[...], cat3(g))
        dgate = dh * up * (sig + silu * (1.0 - sig))
        dup = dh * silu
        dgu = jnp.concatenate([dgate, dup], axis=0)
        dn2 = mm_stack(w_dgu[...], dgu)
        g_down[...] += outer_sum(hidden, g)
        g_gu[...] += outer_sum(dgu, normed2)
        weighted = dn2 * gain_ffn
        inner = jnp.mean(weighted * attended, axis=0, keepdims=True)
        da = g + r2 * weighted - attended * (r2 * r2 * r2 * inner)
        da_ref[0, :, cols] = da
        g_gf[...] += lane_fold(dn2 * scaled)
        g_out[...] += outer_sum(mixed, da)
        dm = nn(w_dm[...], cat3(da))
        dm_ref[0, :, cols] = dm
        prod = (dm * mixed).reshape(HEADS, HD, TC)
        for h in range(HEADS):
            st_ref[0, 16 + h : 17 + h, cols] = jnp.sum(prod[h], axis=0, keepdims=True)
        return 0

    lax.fori_loop(0, t // TC, feed, 0)

    @pl.when(step == pl.num_programs(0) - 1)
    def _():
        parts = 2 * b1_ref.shape[0]
        fs, ds = ff // parts, d // parts
        g_gu_t = g_gu[...].T
        g_down_t = g_down[...].T
        g_out_t = g_out[...].T
        gf = jnp.sum(g_gf[...], axis=1, keepdims=True)
        for n in range(parts):
            gf_own = jnp.concatenate([gf[n * ds : (n + 1) * ds], jnp.zeros((d - ds, 1), F32)], axis=0)
            share = jnp.concatenate([
                g_gu_t[:, n * fs : (n + 1) * fs], g_gu_t[:, ff + n * fs : ff + (n + 1) * fs],
                g_down_t[:, n * fs : (n + 1) * fs], g_out_t[:, n * ds : (n + 1) * ds], gf_own,
            ], axis=1)
            b1_ref[n // 2, n % 2] = stack_columns(share, b1_ref.shape[2])


def stack_columns(share, height):
    rows, cols = share.shape
    pad_cols = -cols % 128
    if pad_cols:
        share = jnp.concatenate([share, jnp.zeros((rows, pad_cols), F32)], axis=1)
    pieces = [share[:, c * 128 : (c + 1) * 128] for c in range(share.shape[1] // 128)]
    left = height - len(pieces) * rows
    if left:
        pieces.append(jnp.zeros((left, 128), F32))
    return jnp.concatenate(pieces, axis=0)


def at(group, narrow):
    return (group, narrow)


def greet(groups, ny):
    g, n = lax.axis_index("group"), lax.axis_index("narrow")
    core, y = lax.rem(n, 2), lax.div(n, 2)
    barrier = pltpu.get_barrier_semaphore()
    peers = [at(g, y * 2 + 1 - core)]
    peers += [at(g, lax.rem(y + off, ny) * 2 + core) for off in range(1, ny)]
    peers += [at(lax.rem(g + off, groups), n) for off in range(1, groups)]
    for peer in peers:
        pl.semaphore_signal(barrier, inc=1, device_id=peer, device_id_type=pl.DeviceIdType.MESH)
    pl.semaphore_wait(barrier, len(peers))


def share_phases(src, total_ref, base, recv1, pair, recv2, share, recv3, send_sem, recv_sem):
    ny, rows = src.shape[0], src.shape[2]
    groups, chunk = recv3.shape[0], recv3.shape[1]
    g, n = lax.axis_index("group"), lax.axis_index("narrow")
    core, y = lax.rem(n, 2), lax.div(n, 2)

    def copy(i, source, target, to):
        return pltpu.make_async_remote_copy(
            src_ref=source, dst_ref=target, send_sem=send_sem.at[i], recv_sem=recv_sem.at[i], device_id=to,
            device_id_type=pl.DeviceIdType.MESH,
        )

    def over_core():
        return [copy(0, src.at[:, 1 - core], recv1, at(g, y * 2 + 1 - core))]

    def over_y():
        peers = [lax.rem(y + off, ny) for off in range(1, ny)]
        return [copy(1 + i, pair.at[p], recv2.at[i], at(g, p * 2 + core)) for i, p in enumerate(peers)]

    def over_group():
        peers = [lax.rem(g + off, groups) for off in range(1, groups)]
        return [copy(ny + i, share.at[p], recv3.at[1 + i], at(p, n)) for i, p in enumerate(peers)]

    def gather():
        own = total_ref.at[g, pl.ds(base, chunk)]
        peers = [lax.rem(g + off, groups) for off in range(1, groups)]
        return [copy(ny + groups - 1 + i, own, own, at(p, n)) for i, p in enumerate(peers)]

    def start(copies):
        for c in copies:
            c.start()

    def arrive(copies):
        for c in copies:
            c.wait_recv()

    def one():
        start(over_core())

    def two():
        arrive(over_core())
        for i in range(ny):
            pair[i] = src[i, core] + recv1[i]
        start(over_y())

    def three():
        arrive(over_y())
        total = pair[y]
        for i in range(ny - 1):
            total += recv2[i]
        share[...] = total.reshape(groups, chunk, 128)
        start(over_group())

    def four():
        recv3[0] = share[g]
        arrive(over_group())
        total_ref[g, base : base + chunk] = jnp.sum(recv3[...], axis=0)
        start(gather())

    def five():
        arrive(gather())
        for copies in (over_core(), over_y(), over_group(), gather()):
            for c in copies:
                c.wait_send()

    return one, two, three, four, five


def backward_kernel(
    dx_steps, scale_ref, q_ref, k_ref, v_ref, dm_ref, st_ref, da_ref, x_ref, feat_ref, w_dqkv, gains, cos_ref, sin_ref, b1_ref,
    dx_ref, out_ref,
    dqkv_ref, g_qkv, g_in, g_ga, b2_ref, total_ref, *buffers,
):
    step = pl.program_id(0)
    early = share_phases(b1_ref, total_ref, 0, *buffers[:7])
    late = share_phases(b2_ref, total_ref, b1_ref.shape[2] // total_ref.shape[0], *buffers[7:])

    @pl.when(step == 0)
    def _():
        greet(total_ref.shape[0], b1_ref.shape[0])

    for i, phase in enumerate(early[:4]):

        @pl.when(step == min(i, dx_steps - 1))
        def _():
            phase()

    d, t = q_ref.shape[1], q_ref.shape[2]

    @pl.when(step == 0)
    def _():
        for ref in (g_qkv, g_in, g_ga):
            ref[...] = jnp.zeros_like(ref)

    nb = t // QB
    causal = lax.broadcasted_iota(jnp.int32, (QB, QB), 0) >= lax.broadcasted_iota(jnp.int32, (QB, QB), 1)
    ones = (lax.broadcasted_iota(jnp.int32, (HD, t), 0) < 3).astype(BF16)

    def extras(row):
        a, b, c = split3(row)
        pieces = jnp.concatenate([a.astype(F32), b.astype(F32), c.astype(F32)], axis=0)
        return jnp.concatenate([pieces, jnp.zeros((HD - 3, t), F32)], axis=0)

    def sides(block, row):
        hi, lo = split(block)
        hf, lf = hi.astype(F32), lo.astype(F32)
        tall = jnp.concatenate([hf, lf, hf, extras(-row)], axis=0).T.astype(BF16)
        return tall, jnp.concatenate([hi, lo], axis=0), hi

    def rows_at(first, h):
        return slice(first + h * HD, first + (h + 1) * HD)

    def prepare(h):
        rows = rows_at(0, h)
        qc, qs, qh = sides(q_ref[0, rows, :], st_ref[0, h : h + 1, :])
        mc, ms, mh = sides(dm_ref[0, rows, :], st_ref[0, 16 + h : 17 + h, :])
        kh, kl = split(k_ref[0, rows, :])
        kc = jnp.concatenate([kh, kh, kl, ones], axis=0)
        vh, vl = split(v_ref[0, rows, :])
        vc = jnp.concatenate([vh, vh, vl, ones], axis=0)
        return qc, mc, kc, vc, qs, qh, ms, mh, jnp.concatenate([kh, kl], axis=0), kh

    def tile(item):
        h, kb, qb = item
        return h, slice(kb * QB, (kb + 1) * QB), slice(qb * QB, (qb + 1) * QB)

    def scores(item):
        h, keys, steps = tile(item)
        qc, mc, kc, vc = prepared[h][:4]
        return nn(qc[steps], kc[:, keys]), nn(mc[steps], vc[:, keys])

    def differentiate(item, s, dp):
        h, keys, steps = tile(item)
        kb, qb = item[1:]
        qs, qh, ms, mh, ks, kh = prepared[h][4:]
        p = jnp.exp2(s)
        if kb == qb:
            p = jnp.where(causal, p, 0.0)
        ds = p * dp
        ph, pl_ = split(p)
        dh, dl = split(ds)
        th, tl = split(ds.T)
        both = nn(ms[:, steps], ph)
        dv = both[:HD] + both[HD:] + nn(mh[:, steps], pl_)
        both = nn(qs[:, steps], dh)
        dk = both[:HD] + both[HD:] + nn(qh[:, steps], dl)
        if qb > kb:
            dk, dv = dk + sums[h][0], dv + sums[h][1]
        sums[h] = dk, dv
        if qb == nb - 1:
            dqkv_ref[rows_at(d, h), keys] = dk
            dqkv_ref[rows_at(2 * d, h), keys] = dv
        both = nn(ks[:, keys], th)
        dq = both[:HD] + both[HD:] + nn(kh[:, keys], tl)
        if kb == qb:
            dqkv_ref[rows_at(0, h), steps] = dq
        else:
            dqkv_ref[rows_at(0, h), steps] += dq

    prepared = [prepare(h) for h in range(HEADS)]
    sums = {}
    items = [(h, kb, qb) for kb in reversed(range(nb)) for h in range(HEADS) for qb in range(kb, nb)]
    ahead = {}
    for j in range(len(items) + AHEAD):
        if j < len(items):
            ahead[j] = scores(items[j])
        if j >= AHEAD:
            differentiate(items[j - AHEAD], *ahead.pop(j - AHEAD))

    gain = gains[:, :1]
    scales = row_scales(scale_ref[pl.ds(step, 1), :], NLAG)

    def finish(i, _):
        cols = pl.ds(pl.multiple_of(i * TD, TD), TD)
        cos, sin = cos_ref[:, cols], -sin_ref[:, cols]
        dq = rotate(dqkv_ref[:d, cols], cos, sin) * HD**-0.5
        dk = rotate(dqkv_ref[d : 2 * d, cols], cos, sin) * LN2
        dqkv = jnp.concatenate([dq, dk, dqkv_ref[2 * d :, cols]], axis=0)
        x = x_ref[0, :, cols]
        r = lax.rsqrt(jnp.mean(x * x, axis=0, keepdims=True) + NORM_EPS)
        xr = x * r
        dn = mm_stack(w_dqkv[...], dqkv)
        g_qkv[...] += outer_sum(dqkv, xr * gain)
        weighted = dn * gain
        inner = jnp.mean(weighted * x, axis=0, keepdims=True)
        dx = da_ref[0, :, cols] + r * weighted - x * (r * r * r * inner)
        dx_ref[0, :, cols] = dx
        g_ga[...] += lane_fold(dn * xr)
        g_in[...] += outer_sum(dx, feat_ref[0, :, cols] * scales)
        return 0

    lax.fori_loop(0, t // TD, finish, 0)

    @pl.when(step == pl.num_programs(0) - 1)
    def _():
        parts = 2 * b2_ref.shape[0]
        ds = d // parts
        g_qkv_t = g_qkv[...].T
        ga = jnp.sum(g_ga[...], axis=1, keepdims=True)
        for n in range(parts):
            own = slice(n * ds, (n + 1) * ds)
            share = jnp.concatenate([g_qkv_t[own], g_in[own, :], ga[own]], axis=1)
            b2_ref[n // 2, n % 2] = stack_columns(share, b2_ref.shape[2])
        for phase in late[:4]:
            phase()
        for end in (early[4], late[4]):
            end()
        out_ref[...] = total_ref[...]


def unpack_kernel(total_ref, dx_ref, dx_out, *grads):
    dx_out[...] = dx_ref[...]

    @pl.when(pl.program_id(0) == 0)
    def _():
        unpack(total_ref, *grads)


def unpack(total_ref, g_in, g_ga, g_q, g_k, g_v, g_out, g_gf, g_gate, g_up, g_down):
    d, fs = g_gate.shape
    ds, nf = g_in.shape
    groups = total_ref.shape[0]
    wide = round_up(3 * fs + ds + 1, 128) // 128
    c1 = round_up(wide * d, 8 * groups) // groups
    one = jnp.concatenate([total_ref[g, :c1] for g in range(groups)], axis=0)
    one = jnp.concatenate([one[c * d : (c + 1) * d, :] for c in range(wide)], axis=1)
    g_gate[...] = one[:, :fs]
    g_up[...] = one[:, fs : 2 * fs]
    g_down[...] = one[:, 2 * fs : 3 * fs]
    g_out[...] = one[:, 3 * fs : 3 * fs + ds].T
    g_gf[...] = one[:ds, 3 * fs + ds]
    wide = round_up(3 * d + FPAD + 1, 128) // 128
    two = jnp.concatenate([total_ref[g, c1:] for g in range(groups)], axis=0)
    two = jnp.concatenate([two[c * ds : (c + 1) * ds, :] for c in range(wide)], axis=1)
    g_q[...] = two[:, :d]
    g_k[...] = two[:, d : 2 * d]
    g_v[...] = two[:, 2 * d : 3 * d]
    g_in[...] = two[:, 3 * d : 3 * d + nf]
    g_ga[...] = two[:, 3 * d + FPAD]


def rotation_tables(t):
    freqs = 10000.0 ** (-np.arange(HD // 2, dtype=np.float64) * 2.0 / HD)
    angles = freqs[:, None] * np.arange(t, dtype=np.float64)[None, :]
    return np.cos(angles).astype(np.float32), np.sin(angles).astype(np.float32)


def round_up(n, m):
    return (n + m - 1) // m * m


def on_device(
    groups, parts, series_values, observed, lag_steps, lag_flags, dataset_ids, in_proj, gain_attn, query_proj, key_proj,
    value_proj, out_proj, gain_ffn, gate_proj, up_proj, down_proj, cotangent,
):
    n_series, t = series_values.shape
    nf, d = in_proj.shape
    ff = gate_proj.shape[1]
    fs, ds = ff // parts, d // parts
    cos, sin = rotation_tables(t)
    cos, sin = jnp.asarray(cos), jnp.asarray(sin)
    smem = pl.BlockSpec(memory_space=pltpu.SMEM)
    vmem = pl.BlockSpec(memory_space=pltpu.VMEM)

    def whole(a):
        return pl.BlockSpec(a.shape, lambda i: (0,) * a.ndim)

    def each(rows):
        return pl.BlockSpec((1, rows, t), lambda i: (i, 0, 0))

    def shape(*dims, dtype=F32):
        return jax.ShapeDtypeStruct(dims, dtype)

    params = pltpu.CompilerParams(dimension_semantics=("arbitrary",), vmem_limit_bytes=62 * 2**20)
    plain = pltpu.CompilerParams(vmem_limit_bytes=62 * 2**20)
    in_t, down_t = in_proj.T, down_proj.T
    series_scale, raw, w_in, w_qkv, w_out, w_gu, w_down, w_dh, w_dgu, w_dm, w_dqkv, gains = pl.pallas_call(
        functools.partial(prepare_kernel, parts),
        in_specs=[smem] * 3 + [vmem] * 12,
        out_specs=[vmem] * 12,
        out_shape=[
            shape(n_series, 128),
            shape(n_series, FPAD, t),
            shape(d, 3 * FPAD, dtype=BF16),
            shape(3 * d, 3 * d, dtype=BF16),
            shape(d, 3 * d, dtype=BF16),
            shape(2 * ff, 3 * d, dtype=BF16),
            shape(2 * d, ff, dtype=BF16),
            shape(ff, 3 * d, dtype=BF16),
            shape(2 * d, 2 * ff, dtype=BF16),
            shape(d, 3 * d, dtype=BF16),
            shape(2 * d, 3 * d, dtype=BF16),
            shape(d, 128),
        ],
        scratch_shapes=[
            pltpu.VMEM((8, 128), F32),
            pltpu.VMEM((parts - 1, 8, 128), F32),
            pltpu.SemaphoreType.DMA((parts - 1,)),
            pltpu.SemaphoreType.DMA((parts - 1,)),
        ],
        compiler_params=pltpu.CompilerParams(vmem_limit_bytes=62 * 2**20, collective_id=1, has_side_effects=True),
        name="sums_weights_and_lags",
    )(lag_steps, lag_flags, dataset_ids, series_values, observed, in_t, query_proj, key_proj, value_proj, out_proj, gate_proj, up_proj,
      down_t, gain_attn, gain_ffn)

    rows1 = round_up(round_up(3 * fs + ds + 1, 128) // 128 * d, 8 * groups)
    rows2 = round_up(round_up(3 * d + FPAD + 1, 128) // 128 * ds, 8 * groups)
    full = [w_in, w_qkv, w_out, w_gu, w_down, w_dh, w_dgu, w_dm, gains, cos, sin]
    b1 = shape(parts // 2, 2, rows1, 128)
    act, q, k, v, dm, st, da, x, b1 = pl.pallas_call(
        forward_kernel,
        grid=(n_series,),
        in_specs=[whole(series_scale), each(FPAD)] + [whole(a) for a in full] + [each(d)],
        out_specs=[each(d)] * 5 + [each(32)] + [each(d)] * 2 + [whole(b1)],
        out_shape=[shape(n_series, d, t)] * 5 + [shape(n_series, 32, t)] + [shape(n_series, d, t)] * 2 + [b1],
        scratch_shapes=[
            pltpu.VMEM((d, t), F32),
            pltpu.VMEM((2 * ff, d), F32),
            pltpu.VMEM((ff, d), F32),
            pltpu.VMEM((d, d), F32),
            pltpu.VMEM((d, 128), F32),
        ],
        compiler_params=params,
        name="forward_and_ffn",
    )(series_scale, raw, *full, jnp.transpose(cotangent, (0, 2, 1)))

    ny = parts // 2
    c1, c2 = rows1 // groups, rows2 // groups
    total = shape(groups, c1 + c2, 128)
    full = [w_dqkv, gains, cos, sin, b1]
    copies = ny + 2 * (groups - 1)
    dma = pltpu.SemaphoreType.DMA
    buffers = []
    for rows, chunk in ((rows1, c1), (rows2, c2)):
        buffers += [
            pltpu.VMEM((ny, rows, 128), F32),
            pltpu.VMEM((ny, rows, 128), F32),
            pltpu.VMEM((max(ny - 1, 1), rows, 128), F32),
            pltpu.VMEM((groups, chunk, 128), F32),
            pltpu.VMEM((groups, chunk, 128), F32),
            dma((copies,)),
            dma((copies,)),
        ]
    dx, total = pl.pallas_call(
        functools.partial(backward_kernel, n_series),
        grid=(n_series,),
        in_specs=[whole(series_scale)] + [each(d)] * 4 + [each(32)] + [each(d)] * 2 + [each(FPAD)] + [whole(a) for a in full],
        out_specs=[each(d), whole(total)],
        out_shape=[shape(n_series, d, t), total],
        scratch_shapes=[
            pltpu.VMEM((3 * d, t), F32),
            pltpu.VMEM((3 * d, d), F32),
            pltpu.VMEM((d, FPAD), F32),
            pltpu.VMEM((d, 128), F32),
            pltpu.VMEM((ny, 2, rows2, 128), F32),
            pltpu.VMEM((groups, c1 + c2, 128), F32),
            *buffers,
        ],
        compiler_params=pltpu.CompilerParams(
            dimension_semantics=("arbitrary",), vmem_limit_bytes=62 * 2**20, collective_id=0, has_side_effects=True
        ),
        name="attention_backward_and_sums",
    )(series_scale, q, k, v, dm, st, da, x, raw, *full)

    grads = [
        shape(ds, nf), shape(ds), shape(ds, d), shape(ds, d), shape(ds, d), shape(ds, d), shape(ds),
        shape(d, fs), shape(d, fs), shape(d, fs),
    ]
    dx, *grads = pl.pallas_call(
        unpack_kernel,
        grid=(n_series,),
        in_specs=[whole(total), each(d)],
        out_specs=[each(d)] + [whole(a) for a in grads],
        out_shape=[shape(n_series, d, t)] + grads,
        compiler_params=params,
        name="unpack_gradients",
    )(total, dx)
    return (
        jnp.transpose(act, (0, 2, 1)),
        jnp.transpose(dx, (0, 2, 1)),
        grads[0].T,
        *grads[1:9],
        grads[9].T,
    )


def solution(mesh):
    series = P(("group", "narrow"), None)
    return jax.shard_map(
        functools.partial(on_device, mesh.shape["group"], mesh.shape["narrow"]),
        mesh=mesh,
        in_specs=(series, series, P(), P(), P(("group", "narrow"))) + (P(),) * 10 + (P(("group", "narrow"), None, None),),
        out_specs=(
            P(("group", "narrow"), None, None),
            P(("group", "narrow"), None, None),
            P(None, "narrow"),
            P("narrow"),
            P("narrow", None),
            P("narrow", None),
            P("narrow", None),
            P("narrow", None),
            P("narrow"),
            P(None, "narrow"),
            P(None, "narrow"),
            P("narrow", None),
        ),
        check_vma=False,
    )
```

```python
import functools

import jax
import jax.numpy as jnp
import numpy as np
from jax import lax
from jax.experimental import pallas as pl
from jax.experimental.pallas import tpu as pltpu
from jax.sharding import PartitionSpec as P

HEADS = 9
HD = 16
DSETS = 4
FPAD = 96
QB = 256
TA = 1024
TC = 1024
TD = 1024
NLAG = 84
AHEAD = 2

NORM_EPS = 1e-05
SCALE_EPS = 1e-05
LOG2E = 1.4426950408889634
LN2 = 0.6931471805599453

F32 = jnp.float32
BF16 = jnp.bfloat16


def nn(left, right):
    return lax.dot_general(left, right, (((1,), (0,)), ((), ())), preferred_element_type=F32)


def nt(left, right):
    return lax.dot_general(left, right, (((1,), (1,)), ((), ())), preferred_element_type=F32)


def split(x):
    hi = x.astype(BF16)
    return hi, (x - hi.astype(F32)).astype(BF16)


def split3(x):
    hi = x.astype(BF16)
    rest = x - hi.astype(F32)
    mid = rest.astype(BF16)
    return hi, mid, (rest - mid.astype(F32)).astype(BF16)


def cat3(x):
    hi, lo = split(x)
    return jnp.concatenate([hi, hi, lo], axis=0)


def weight_cat(w):
    hi, lo = split(w)
    hi, lo = hi.astype(F32), lo.astype(F32)
    return jnp.concatenate([hi, lo, hi], axis=0).T.astype(BF16)


def weight_stack(w):
    hi, lo = split(w)
    return jnp.concatenate([hi, lo], axis=0)


def mm_stack(stack, x):
    m = stack.shape[0] // 2
    hi, lo = split(x)
    both = nn(stack, hi)
    return both[:m] + both[m:] + nn(stack[:m], lo)


def outer_sum(left, right):
    m = left.shape[0]
    lh, ll = split(left)
    rh, rl = split(right)
    both = nt(jnp.concatenate([lh, ll], axis=0), rh)
    return both[:m] + both[m:] + nt(lh, rl)


def column(row):
    n = row.shape[0]
    return jnp.broadcast_to(row[None, :], (8, n)).T[:, :1]


def lane_fold(x):
    total = x[:, :128]
    for i in range(1, x.shape[1] // 128):
        total = total + x[:, i * 128 : (i + 1) * 128]
    return total


def rotate(x, cos, sin):
    t = x.shape[1]
    pairs = x.reshape(HEADS, 2, HD // 2, t)
    a, b = pairs[:, 0], pairs[:, 1]
    first = a * cos - b * sin
    second = a * sin + b * cos
    return jnp.stack([first, second], axis=1).reshape(HEADS * HD, t)


def row_scales(scale, nlag):
    row = lax.broadcasted_iota(jnp.int32, (FPAD, 128), 0)
    scales = jnp.broadcast_to(scale, (FPAD, 128))
    inverse, logs = 1.0 / scales, jnp.log(scales)
    return jnp.where(row < nlag, inverse, jnp.where(row == nlag, logs, 1.0))[:, :1]


def prepare_kernel(
    parts, n_in, lag_ref, flag_ref, ids_ref, *refs
):
    sources, refs = refs[:n_in], refs[n_in:]
    scale_ref, feat_ref, w_in, w_qkv, w_out, w_gu, w_down, w_dh, w_dgu, w_dm, w_dqkv, gains, cos_ref, sin_ref = refs[:14]
    own, others, send_sem, recv_sem, fetch_sem, *fetched = refs[14:]
    vals_ref, obs_ref, in_ref, wq_ref, wk_ref, wv_ref, wo_ref, wg_ref, wu_ref, wd_ref, ga_ref, gf_ref = fetched
    fetched = fetched + [cos_ref, sin_ref]
    fetches = [pltpu.make_async_copy(sources[i], fetched[i], fetch_sem.at[i]) for i in range(n_in)]
    for c in fetches:
        c.start()
    n_series, t = vals_ref.shape
    d, nf = in_ref.shape
    nlag = lag_ref.shape[0]
    ff = wg_ref.shape[1]
    for c in fetches[:2]:
        c.wait()
    obs = obs_ref[...].astype(F32)
    both = jnp.concatenate([vals_ref[...] * obs, obs], axis=0)

    g, n = lax.axis_index("group"), lax.axis_index("narrow")
    barrier = pltpu.get_barrier_semaphore()
    copies = []
    for off in range(1, parts):
        peer = (g, lax.rem(n + off, parts))
        pl.semaphore_signal(barrier, inc=1, device_id=peer, device_id_type=pl.DeviceIdType.MESH)
        copies.append(pltpu.make_async_remote_copy(
            src_ref=own, dst_ref=others.at[off - 1], send_sem=send_sem.at[off - 1], recv_sem=recv_sem.at[off - 1],
            device_id=peer, device_id_type=pl.DeviceIdType.MESH,
        ))
    series = lax.broadcasted_iota(jnp.int32, (n_series, 128), 0)
    ids = jnp.zeros((n_series, 128), jnp.int32)
    for s in range(n_series):
        ids = jnp.where(series == s, ids_ref[s], ids)
    member = (lax.broadcasted_iota(jnp.int32, (n_series, 128), 1) == ids).astype(F32)
    magnitude = jnp.sum(jnp.abs(both[:n_series]), axis=1, keepdims=True)
    counted = jnp.sum(obs, axis=1, keepdims=True)
    own[...] = jnp.concatenate([
        jnp.sum(member * magnitude, axis=0, keepdims=True), jnp.sum(member * counted, axis=0, keepdims=True),
        jnp.zeros((6, 128), F32),
    ], axis=0)

    lanes = lax.broadcasted_iota(jnp.int32, both.shape, 1)

    def one_lag(j, missing):
        lag = lag_ref[j]
        moved = jnp.where(lanes >= lag, pltpu.roll(both, lag, 1), 0.0)
        for s in range(n_series):
            feat_ref[s, pl.ds(j, 1), :] = moved[s : s + 1]
        return missing + flag_ref[j].astype(F32) * (1.0 - moved[n_series:])

    missing = lax.fori_loop(0, nlag, one_lag, jnp.zeros((n_series, t), F32), unroll=12)
    for s in range(n_series):
        feat_ref[s, nlag : nlag + 1, :] = jnp.ones((1, t), F32)
        feat_ref[s, nlag + 1 : nlag + 2, :] = missing[s : s + 1] * nlag**-0.5
        feat_ref[s, nlag + 2 :, :] = jnp.zeros((FPAD - nlag - 2, t), F32)

    pl.semaphore_wait(barrier, parts - 1)
    for c in copies:
        c.start()

    for c in fetches[2:]:
        c.wait()
    w_in_rows = jnp.concatenate([in_ref[...].T, jnp.zeros((FPAD - nf, d), F32)], axis=0)
    w_in[...] = weight_cat(w_in_rows)
    for i, ref in enumerate((wq_ref, wk_ref, wv_ref)):
        w_qkv[i * d : (i + 1) * d, :] = weight_cat(ref[...])
        w_dqkv[:, i * d : (i + 1) * d] = weight_stack(ref[...])
    w_out[...] = weight_cat(wo_ref[...])
    w_gu[:ff, :] = weight_cat(wg_ref[...])
    w_gu[ff:, :] = weight_cat(wu_ref[...])
    w_down[...] = weight_stack(wd_ref[...])
    w_dh[...] = weight_cat(wd_ref[...])
    w_dgu[:, :ff] = weight_stack(wg_ref[...])
    w_dgu[:, ff:] = weight_stack(wu_ref[...])
    w_dm[...] = weight_cat(wo_ref[...].T)
    gains[...] = jnp.zeros_like(gains)
    gains[:, :1] = column(ga_ref[...])
    gains[:, 1:2] = column(gf_ref[...])

    for c in copies:
        c.wait()
    total = own[...]
    for i in range(parts - 1):
        total = total + others[i]
    set_scale = total[:1] / jnp.maximum(total[1:2], 1.0) + SCALE_EPS
    series_scale = jnp.sum(jnp.where(member > 0.0, set_scale, 0.0), axis=1, keepdims=True)
    scale_ref[...] = jnp.broadcast_to(series_scale, scale_ref.shape)


def forward_kernel(
    scale_ref, feat_ref, w_in, w_qkv, w_out, w_gu, w_down, w_dh, w_dgu, w_dm, gains, cos_ref, sin_ref, cot_ref,
    act_ref, q_ref, k_ref, v_ref, dm_ref, st_ref, da_ref, x_ref, b1_ref,
    mixed_ref, g_gu, g_down, g_out, g_gf, cot_buf, cot_sem,
):
    step = pl.program_id(0)
    d, t = cot_ref.shape[1], cot_ref.shape[2]

    def fetch(i):
        return pltpu.make_async_copy(cot_ref.at[i], cot_buf.at[i % 2], cot_sem.at[i % 2])

    ff = w_dh.shape[0]
    gain_attn, gain_ffn = gains[:, :1], gains[:, 1:2]
    scales = row_scales(scale_ref[pl.ds(step, 1), :], NLAG)

    @pl.when(step == 0)
    def _():
        fetch(0).start()
        for ref in (g_gu, g_down, g_out, g_gf):
            ref[...] = jnp.zeros_like(ref)

    @pl.when(step + 1 < pl.num_programs(0))
    def _():
        fetch(step + 1).start()

    st_ref[0] = jnp.zeros(st_ref.shape[1:], F32)

    def project(i, _):
        cols = pl.ds(pl.multiple_of(i * TA, TA), TA)
        x = nn(w_in[...], cat3(feat_ref[0, :, cols] * scales))
        x_ref[0, :, cols] = x
        normed = x * lax.rsqrt(jnp.mean(x * x, axis=0, keepdims=True) + NORM_EPS) * gain_attn
        qkv = nn(w_qkv[...], cat3(normed))
        cos, sin = cos_ref[:, cols], sin_ref[:, cols]
        q_ref[0, :, cols] = rotate(qkv[:d], cos, sin) * (HD**-0.5 * LOG2E)
        k_ref[0, :, cols] = rotate(qkv[d : 2 * d], cos, sin)
        v_ref[0, :, cols] = qkv[2 * d :]
        return 0

    lax.fori_loop(0, t // TA, project, 0)

    causal = lax.broadcasted_iota(jnp.int32, (QB, QB), 0) <= lax.broadcasted_iota(jnp.int32, (QB, QB), 1)

    def prepare(h):
        rows = slice(h * HD, (h + 1) * HD)
        qh, ql = split(q_ref[0, rows, :])
        qc = jnp.concatenate([qh, ql, qh], axis=0)
        kh, kl = split(k_ref[0, rows, :])
        kh, kl = kh.astype(F32), kl.astype(F32)
        kc = jnp.concatenate([kh, kh, kl], axis=0).T.astype(BF16)
        vh, vl = split(v_ref[0, rows, :])
        return qc, kc, jnp.concatenate([vh, vl], axis=0), vh

    def scores(sides, item):
        qc, kc = sides[:2]
        lo, top = item[1] * QB, (item[1] + 1) * QB
        return nn(kc[:top], qc[:, lo:top])

    def softmax(s, block):
        lo = block * QB
        last = jnp.where(causal, s[lo:], -1e30)
        s = jnp.concatenate([s[:lo], last], axis=0) if block else last
        return s, jnp.max(s, axis=0, keepdims=True)

    def mix(sides, soft, item):
        h, block = item
        vs, vh = sides[2:]
        s, m = soft
        lo, top = block * QB, (block + 1) * QB
        both = low = total = 0.0
        for c in range(block + 1):
            keys = slice(c * QB, (c + 1) * QB)
            p = jnp.exp2(s[keys] - m)
            total = total + jnp.sum(p, axis=0, keepdims=True)
            ph, pl_ = split(p)
            both = both + nn(vs[:, keys], ph)
            low = low + nn(vh[:, keys], pl_)
        mixed_ref[h * HD : (h + 1) * HD, lo:top] = (both[:HD] + both[HD:] + low) / total
        st_ref[0, h : h + 1, lo:top] = m + jnp.log2(total)

    sides = [prepare(h) for h in range(HEADS)]
    items = [(h, block) for block in reversed(range(t // QB)) for h in range(HEADS)]
    ahead = {}
    for j in range(len(items) + AHEAD):
        if j < len(items):
            ahead[j] = scores(sides[items[j][0]], items[j])
        if j >= AHEAD:
            item = items[j - AHEAD]
            mix(sides[item[0]], softmax(ahead.pop(j - AHEAD), item[1]), item)

    fetch(step).wait()

    def feed(i, _):
        cols = pl.ds(pl.multiple_of(i * TC, TC), TC)
        mixed = mixed_ref[:, cols]
        attended = x_ref[0, :, cols] + nn(w_out[...], cat3(mixed))
        r2 = lax.rsqrt(jnp.mean(attended * attended, axis=0, keepdims=True) + NORM_EPS)
        scaled = attended * r2
        normed2 = scaled * gain_ffn
        gu = nn(w_gu[...], cat3(normed2))
        gate, up = gu[:ff], gu[ff:]
        sig = 1.0 / (1.0 + jnp.exp(-gate))
        silu = gate * sig
        hidden = silu * up
        act_ref[0, :, cols] = attended + mm_stack(w_down[...], hidden)

        g = cot_buf[step % 2, :, cols]
        dh = nn(w_dh[...], cat3(g))
        dgate = dh * up * (sig + silu * (1.0 - sig))
        dup = dh * silu
        dgu = jnp.concatenate([dgate, dup], axis=0)
        dn2 = mm_stack(w_dgu[...], dgu)
        g_down[...] += outer_sum(hidden, g)
        g_gu[...] += outer_sum(dgu, normed2)
        weighted = dn2 * gain_ffn
        inner = jnp.mean(weighted * attended, axis=0, keepdims=True)
        da = g + r2 * weighted - attended * (r2 * r2 * r2 * inner)
        da_ref[0, :, cols] = da
        g_gf[...] += lane_fold(dn2 * scaled)
        g_out[...] += outer_sum(mixed, da)
        dm = nn(w_dm[...], cat3(da))
        dm_ref[0, :, cols] = dm
        prod = (dm * mixed).reshape(HEADS, HD, TC)
        for h in range(HEADS):
            st_ref[0, 16 + h : 17 + h, cols] = jnp.sum(prod[h], axis=0, keepdims=True)
        return 0

    lax.fori_loop(0, t // TC, feed, 0)

    @pl.when(step == pl.num_programs(0) - 1)
    def _():
        parts = 2 * b1_ref.shape[0]
        fs, ds = ff // parts, d // parts
        g_gu_t = g_gu[...].T
        g_down_t = g_down[...].T
        g_out_t = g_out[...].T
        gf = jnp.sum(g_gf[...], axis=1, keepdims=True)
        for n in range(parts):
            gf_own = jnp.concatenate([gf[n * ds : (n + 1) * ds], jnp.zeros((d - ds, 1), F32)], axis=0)
            share = jnp.concatenate([
                g_gu_t[:, n * fs : (n + 1) * fs], g_gu_t[:, ff + n * fs : ff + (n + 1) * fs],
                g_down_t[:, n * fs : (n + 1) * fs], g_out_t[:, n * ds : (n + 1) * ds], gf_own,
            ], axis=1)
            b1_ref[n // 2, n % 2] = stack_columns(share, b1_ref.shape[2])


def stack_columns(share, height):
    rows, cols = share.shape
    pad_cols = -cols % 128
    if pad_cols:
        share = jnp.concatenate([share, jnp.zeros((rows, pad_cols), F32)], axis=1)
    pieces = [share[:, c * 128 : (c + 1) * 128] for c in range(share.shape[1] // 128)]
    left = height - len(pieces) * rows
    if left:
        pieces.append(jnp.zeros((left, 128), F32))
    return jnp.concatenate(pieces, axis=0)


def at(group, narrow):
    return (group, narrow)


def greet(groups, ny):
    g, n = lax.axis_index("group"), lax.axis_index("narrow")
    core, y = lax.rem(n, 2), lax.div(n, 2)
    barrier = pltpu.get_barrier_semaphore()
    peers = [at(g, y * 2 + 1 - core)]
    peers += [at(g, lax.rem(y + off, ny) * 2 + core) for off in range(1, ny)]
    peers += [at(lax.rem(g + off, groups), n) for off in range(1, groups)]
    for peer in peers:
        pl.semaphore_signal(barrier, inc=1, device_id=peer, device_id_type=pl.DeviceIdType.MESH)
    pl.semaphore_wait(barrier, len(peers))


def share_phases(src, total_ref, base, recv1, pair, recv2, share, recv3, send_sem, recv_sem):
    ny, rows = src.shape[0], src.shape[2]
    groups, chunk = recv3.shape[0], recv3.shape[1]
    g, n = lax.axis_index("group"), lax.axis_index("narrow")
    core, y = lax.rem(n, 2), lax.div(n, 2)

    def copy(i, source, target, to):
        return pltpu.make_async_remote_copy(
            src_ref=source, dst_ref=target, send_sem=send_sem.at[i], recv_sem=recv_sem.at[i], device_id=to,
            device_id_type=pl.DeviceIdType.MESH,
        )

    def over_core():
        return [copy(0, src.at[:, 1 - core], recv1, at(g, y * 2 + 1 - core))]

    def over_y():
        peers = [lax.rem(y + off, ny) for off in range(1, ny)]
        return [copy(1 + i, pair.at[p], recv2.at[i], at(g, p * 2 + core)) for i, p in enumerate(peers)]

    def over_group():
        peers = [lax.rem(g + off, groups) for off in range(1, groups)]
        return [copy(ny + i, share.at[p], recv3.at[1 + i], at(p, n)) for i, p in enumerate(peers)]

    def gather():
        own = total_ref.at[g, pl.ds(base, chunk)]
        peers = [lax.rem(g + off, groups) for off in range(1, groups)]
        return [copy(ny + groups - 1 + i, own, own, at(p, n)) for i, p in enumerate(peers)]

    def start(copies):
        for c in copies:
            c.start()

    def arrive(copies):
        for c in copies:
            c.wait_recv()

    def one():
        start(over_core())

    def two():
        arrive(over_core())
        for i in range(ny):
            pair[i] = src[i, core] + recv1[i]
        start(over_y())

    def three():
        arrive(over_y())
        total = pair[y]
        for i in range(ny - 1):
            total += recv2[i]
        share[...] = total.reshape(groups, chunk, 128)
        start(over_group())

    def four():
        recv3[0] = share[g]
        arrive(over_group())
        total_ref[g, base : base + chunk] = jnp.sum(recv3[...], axis=0)
        start(gather())

    def five():
        arrive(gather())
        for copies in (over_core(), over_y(), over_group(), gather()):
            for c in copies:
                c.wait_send()

    return one, two, three, four, five


def backward_kernel(
    dx_steps, scale_ref, q_ref, k_ref, v_ref, dm_ref, st_ref, da_ref, x_ref, feat_ref, w_dqkv, gains, cos_ref, sin_ref, b1_ref,
    dx_ref, out_ref,
    dqkv_ref, g_qkv, g_in, g_ga, b2_ref, total_ref, *buffers,
):
    step = pl.program_id(0)
    early = share_phases(b1_ref, total_ref, 0, *buffers[:7])
    late = share_phases(b2_ref, total_ref, b1_ref.shape[2] // total_ref.shape[0], *buffers[7:])

    @pl.when(step == 0)
    def _():
        greet(total_ref.shape[0], b1_ref.shape[0])

    for i, phase in enumerate(early[:4]):

        @pl.when(step == min(i, dx_steps - 1))
        def _():
            phase()

    d, t = q_ref.shape[1], q_ref.shape[2]

    @pl.when(step == 0)
    def _():
        for ref in (g_qkv, g_in, g_ga):
            ref[...] = jnp.zeros_like(ref)

    nb = t // QB
    causal = lax.broadcasted_iota(jnp.int32, (QB, QB), 0) >= lax.broadcasted_iota(jnp.int32, (QB, QB), 1)
    ones = (lax.broadcasted_iota(jnp.int32, (HD, t), 0) < 3).astype(BF16)

    def extras(row):
        a, b, c = split3(row)
        pieces = jnp.concatenate([a.astype(F32), b.astype(F32), c.astype(F32)], axis=0)
        return jnp.concatenate([pieces, jnp.zeros((HD - 3, t), F32)], axis=0)

    def sides(block, row):
        hi, lo = split(block)
        hf, lf = hi.astype(F32), lo.astype(F32)
        tall = jnp.concatenate([hf, lf, hf, extras(-row)], axis=0).T.astype(BF16)
        return tall, jnp.concatenate([hi, lo], axis=0), hi

    def rows_at(first, h):
        return slice(first + h * HD, first + (h + 1) * HD)

    def prepare(h):
        rows = rows_at(0, h)
        qc, qs, qh = sides(q_ref[0, rows, :], st_ref[0, h : h + 1, :])
        mc, ms, mh = sides(dm_ref[0, rows, :], st_ref[0, 16 + h : 17 + h, :])
        kh, kl = split(k_ref[0, rows, :])
        kc = jnp.concatenate([kh, kh, kl, ones], axis=0)
        vh, vl = split(v_ref[0, rows, :])
        vc = jnp.concatenate([vh, vh, vl, ones], axis=0)
        return qc, mc, kc, vc, qs, qh, ms, mh, jnp.concatenate([kh, kl], axis=0), kh

    def tile(item):
        h, kb, qb = item
        return h, slice(kb * QB, (kb + 1) * QB), slice(qb * QB, (qb + 1) * QB)

    def scores(item):
        h, keys, steps = tile(item)
        qc, mc, kc, vc = prepared[h][:4]
        return nn(qc[steps], kc[:, keys]), nn(mc[steps], vc[:, keys])

    def differentiate(item, s, dp):
        h, keys, steps = tile(item)
        kb, qb = item[1:]
        qs, qh, ms, mh, ks, kh = prepared[h][4:]
        p = jnp.exp2(s)
        if kb == qb:
            p = jnp.where(causal, p, 0.0)
        ds = p * dp
        ph, pl_ = split(p)
        dh, dl = split(ds)
        th, tl = split(ds.T)
        both = nn(ms[:, steps], ph)
        dv = both[:HD] + both[HD:] + nn(mh[:, steps], pl_)
        both = nn(qs[:, steps], dh)
        dk = both[:HD] + both[HD:] + nn(qh[:, steps], dl)
        if qb > kb:
            dk, dv = dk + sums[h][0], dv + sums[h][1]
        sums[h] = dk, dv
        if qb == nb - 1:
            dqkv_ref[rows_at(d, h), keys] = dk
            dqkv_ref[rows_at(2 * d, h), keys] = dv
        both = nn(ks[:, keys], th)
        dq = both[:HD] + both[HD:] + nn(kh[:, keys], tl)
        if kb == qb:
            dqkv_ref[rows_at(0, h), steps] = dq
        else:
            dqkv_ref[rows_at(0, h), steps] += dq

    prepared = [prepare(h) for h in range(HEADS)]
    sums = {}
    items = [(h, kb, qb) for kb in reversed(range(nb)) for h in range(HEADS) for qb in range(kb, nb)]
    ahead = {}
    for j in range(len(items) + AHEAD):
        if j < len(items):
            ahead[j] = scores(items[j])
        if j >= AHEAD:
            differentiate(items[j - AHEAD], *ahead.pop(j - AHEAD))

    gain = gains[:, :1]
    scales = row_scales(scale_ref[pl.ds(step, 1), :], NLAG)

    def finish(i, _):
        cols = pl.ds(pl.multiple_of(i * TD, TD), TD)
        cos, sin = cos_ref[:, cols], -sin_ref[:, cols]
        dq = rotate(dqkv_ref[:d, cols], cos, sin) * HD**-0.5
        dk = rotate(dqkv_ref[d : 2 * d, cols], cos, sin) * LN2
        dqkv = jnp.concatenate([dq, dk, dqkv_ref[2 * d :, cols]], axis=0)
        x = x_ref[0, :, cols]
        r = lax.rsqrt(jnp.mean(x * x, axis=0, keepdims=True) + NORM_EPS)
        xr = x * r
        dn = mm_stack(w_dqkv[...], dqkv)
        g_qkv[...] += outer_sum(dqkv, xr * gain)
        weighted = dn * gain
        inner = jnp.mean(weighted * x, axis=0, keepdims=True)
        dx = da_ref[0, :, cols] + r * weighted - x * (r * r * r * inner)
        dx_ref[0, :, cols] = dx
        g_ga[...] += lane_fold(dn * xr)
        g_in[...] += outer_sum(dx, feat_ref[0, :, cols] * scales)
        return 0

    lax.fori_loop(0, t // TD, finish, 0)

    @pl.when(step == pl.num_programs(0) - 1)
    def _():
        parts = 2 * b2_ref.shape[0]
        ds = d // parts
        g_qkv_t = g_qkv[...].T
        ga = jnp.sum(g_ga[...], axis=1, keepdims=True)
        for n in range(parts):
            own = slice(n * ds, (n + 1) * ds)
            share = jnp.concatenate([g_qkv_t[own], g_in[own, :], ga[own]], axis=1)
            b2_ref[n // 2, n % 2] = stack_columns(share, b2_ref.shape[2])
        for phase in late[:4]:
            phase()
        for end in (early[4], late[4]):
            end()
        out_ref[...] = total_ref[...]


def unpack_kernel(total_ref, dx_ref, dx_out, *grads):
    dx_out[...] = dx_ref[...]

    @pl.when(pl.program_id(0) == 0)
    def _():
        unpack(total_ref, *grads)


def unpack(total_ref, g_in, g_ga, g_q, g_k, g_v, g_out, g_gf, g_gate, g_up, g_down):
    d, fs = g_gate.shape
    ds, nf = g_in.shape
    groups = total_ref.shape[0]
    wide = round_up(3 * fs + ds + 1, 128) // 128
    c1 = round_up(wide * d, 8 * groups) // groups
    one = jnp.concatenate([total_ref[g, :c1] for g in range(groups)], axis=0)
    one = jnp.concatenate([one[c * d : (c + 1) * d, :] for c in range(wide)], axis=1)
    g_gate[...] = one[:, :fs]
    g_up[...] = one[:, fs : 2 * fs]
    g_down[...] = one[:, 2 * fs : 3 * fs]
    g_out[...] = one[:, 3 * fs : 3 * fs + ds].T
    g_gf[...] = one[:ds, 3 * fs + ds]
    wide = round_up(3 * d + FPAD + 1, 128) // 128
    two = jnp.concatenate([total_ref[g, c1:] for g in range(groups)], axis=0)
    two = jnp.concatenate([two[c * ds : (c + 1) * ds, :] for c in range(wide)], axis=1)
    g_q[...] = two[:, :d]
    g_k[...] = two[:, d : 2 * d]
    g_v[...] = two[:, 2 * d : 3 * d]
    g_in[...] = two[:, 3 * d : 3 * d + nf]
    g_ga[...] = two[:, 3 * d + FPAD]


def rotation_tables(t):
    freqs = 10000.0 ** (-np.arange(HD // 2, dtype=np.float64) * 2.0 / HD)
    angles = freqs[:, None] * np.arange(t, dtype=np.float64)[None, :]
    return np.cos(angles).astype(np.float32), np.sin(angles).astype(np.float32)


def in_hbm(x):
    return pltpu.with_memory_space_constraint(x, pltpu.HBM)


def round_up(n, m):
    return (n + m - 1) // m * m


def on_device(
    groups, parts, series_values, observed, lag_steps, lag_flags, dataset_ids, in_proj, gain_attn, query_proj, key_proj,
    value_proj, out_proj, gain_ffn, gate_proj, up_proj, down_proj, cotangent,
):
    n_series, t = series_values.shape
    nf, d = in_proj.shape
    ff = gate_proj.shape[1]
    fs, ds = ff // parts, d // parts
    cos, sin = rotation_tables(t)
    cos, sin = jnp.asarray(cos), jnp.asarray(sin)
    smem = pl.BlockSpec(memory_space=pltpu.SMEM)
    vmem = pl.BlockSpec(memory_space=pltpu.VMEM)

    def whole(a):
        return pl.BlockSpec(a.shape, lambda i: (0,) * a.ndim)

    def each(rows):
        return pl.BlockSpec((1, rows, t), lambda i: (i, 0, 0))

    def shape(*dims, dtype=F32):
        return jax.ShapeDtypeStruct(dims, dtype)

    params = pltpu.CompilerParams(dimension_semantics=("arbitrary",), vmem_limit_bytes=28 * 2**20)
    plain = pltpu.CompilerParams(vmem_limit_bytes=62 * 2**20)
    in_t, down_t = in_proj.T, down_proj.T
    hbm = pl.BlockSpec(memory_space=pltpu.HBM)
    sources = [series_values, observed, in_t, query_proj, key_proj, value_proj, out_proj, gate_proj, up_proj, down_t,
               gain_attn, gain_ffn, cos, sin]
    series_scale, raw, w_in, w_qkv, w_out, w_gu, w_down, w_dh, w_dgu, w_dm, w_dqkv, gains, cos, sin = pl.pallas_call(
        functools.partial(prepare_kernel, parts, len(sources)),
        in_specs=[smem] * 3 + [hbm] * len(sources),
        out_specs=[vmem] * 14,
        out_shape=[
            shape(n_series, 128),
            shape(n_series, FPAD, t),
            shape(d, 3 * FPAD, dtype=BF16),
            shape(3 * d, 3 * d, dtype=BF16),
            shape(d, 3 * d, dtype=BF16),
            shape(2 * ff, 3 * d, dtype=BF16),
            shape(2 * d, ff, dtype=BF16),
            shape(ff, 3 * d, dtype=BF16),
            shape(2 * d, 2 * ff, dtype=BF16),
            shape(d, 3 * d, dtype=BF16),
            shape(2 * d, 3 * d, dtype=BF16),
            shape(d, 128),
            shape(*cos.shape),
            shape(*sin.shape),
        ],
        scratch_shapes=[
            pltpu.VMEM((8, 128), F32),
            pltpu.VMEM((parts - 1, 8, 128), F32),
            pltpu.SemaphoreType.DMA((parts - 1,)),
            pltpu.SemaphoreType.DMA((parts - 1,)),
            pltpu.SemaphoreType.DMA((len(sources),)),
            *[pltpu.VMEM(a.shape, a.dtype) for a in sources[:12]],
        ],
        compiler_params=pltpu.CompilerParams(vmem_limit_bytes=20 * 2**20, collective_id=1, has_side_effects=True),
        name="sums_weights_and_lags",
    )(*[in_hbm(a) for a in (lag_steps, lag_flags, dataset_ids, *sources)])

    rows1 = round_up(round_up(3 * fs + ds + 1, 128) // 128 * d, 8 * groups)
    rows2 = round_up(round_up(3 * d + FPAD + 1, 128) // 128 * ds, 8 * groups)
    full = [w_in, w_qkv, w_out, w_gu, w_down, w_dh, w_dgu, w_dm, gains, cos, sin]
    b1 = shape(parts // 2, 2, rows1, 128)
    act, q, k, v, dm, st, da, x, b1 = pl.pallas_call(
        forward_kernel,
        grid=(n_series,),
        in_specs=[whole(series_scale), each(FPAD)] + [whole(a) for a in full] + [hbm],
        out_specs=[each(d)] * 5 + [each(32)] + [each(d)] * 2 + [whole(b1)],
        out_shape=[shape(n_series, d, t)] * 5 + [shape(n_series, 32, t)] + [shape(n_series, d, t)] * 2 + [b1],
        scratch_shapes=[
            pltpu.VMEM((d, t), F32),
            pltpu.VMEM((2 * ff, d), F32),
            pltpu.VMEM((ff, d), F32),
            pltpu.VMEM((d, d), F32),
            pltpu.VMEM((d, 128), F32),
            pltpu.VMEM((2, d, t), F32),
            pltpu.SemaphoreType.DMA((2,)),
        ],
        compiler_params=params,
        name="forward_and_ffn",
    )(series_scale, raw, *full, in_hbm(jnp.transpose(cotangent, (0, 2, 1))))

    ny = parts // 2
    c1, c2 = rows1 // groups, rows2 // groups
    total = shape(groups, c1 + c2, 128)
    full = [w_dqkv, gains, cos, sin, b1]
    copies = ny + 2 * (groups - 1)
    dma = pltpu.SemaphoreType.DMA
    buffers = []
    for rows, chunk in ((rows1, c1), (rows2, c2)):
        buffers += [
            pltpu.VMEM((ny, rows, 128), F32),
            pltpu.VMEM((ny, rows, 128), F32),
            pltpu.VMEM((max(ny - 1, 1), rows, 128), F32),
            pltpu.VMEM((groups, chunk, 128), F32),
            pltpu.VMEM((groups, chunk, 128), F32),
            dma((copies,)),
            dma((copies,)),
        ]
    dx, total = pl.pallas_call(
        functools.partial(backward_kernel, n_series),
        grid=(n_series,),
        in_specs=[whole(series_scale)] + [each(d)] * 4 + [each(32)] + [each(d)] * 2 + [each(FPAD)] + [whole(a) for a in full],
        out_specs=[each(d), whole(total)],
        out_shape=[shape(n_series, d, t), total],
        scratch_shapes=[
            pltpu.VMEM((3 * d, t), F32),
            pltpu.VMEM((3 * d, d), F32),
            pltpu.VMEM((d, FPAD), F32),
            pltpu.VMEM((d, 128), F32),
            pltpu.VMEM((ny, 2, rows2, 128), F32),
            pltpu.VMEM((groups, c1 + c2, 128), F32),
            *buffers,
        ],
        compiler_params=pltpu.CompilerParams(
            dimension_semantics=("arbitrary",), vmem_limit_bytes=28 * 2**20, collective_id=0, has_side_effects=True
        ),
        name="attention_backward_and_sums",
    )(series_scale, q, k, v, dm, st, da, x, raw, *full)

    grads = [
        shape(ds, nf), shape(ds), shape(ds, d), shape(ds, d), shape(ds, d), shape(ds, d), shape(ds),
        shape(d, fs), shape(d, fs), shape(d, fs),
    ]
    dx, *grads = pl.pallas_call(
        unpack_kernel,
        grid=(n_series,),
        in_specs=[whole(total), each(d)],
        out_specs=[each(d)] + [whole(a) for a in grads],
        out_shape=[shape(n_series, d, t)] + grads,
        compiler_params=params,
        name="unpack_gradients",
    )(total, dx)
    return (
        jnp.transpose(act, (0, 2, 1)),
        jnp.transpose(dx, (0, 2, 1)),
        grads[0].T,
        *grads[1:9],
        grads[9].T,
    )


def solution(mesh):
    series = P(("group", "narrow"), None)
    return jax.shard_map(
        functools.partial(on_device, mesh.shape["group"], mesh.shape["narrow"]),
        mesh=mesh,
        in_specs=(series, series, P(), P(), P(("group", "narrow"))) + (P(),) * 10 + (P(("group", "narrow"), None, None),),
        out_specs=(
            P(("group", "narrow"), None, None),
            P(("group", "narrow"), None, None),
            P(None, "narrow"),
            P("narrow"),
            P("narrow", None),
            P("narrow", None),
            P("narrow", None),
            P("narrow", None),
            P("narrow"),
            P(None, "narrow"),
            P(None, "narrow"),
            P("narrow", None),
        ),
        check_vma=False,
    )
```

```python
import functools

import jax
import jax.numpy as jnp
import numpy as np
from jax import lax
from jax.experimental import pallas as pl
from jax.experimental.pallas import tpu as pltpu
from jax.sharding import PartitionSpec as P

HEADS = 9
HD = 16
DSETS = 4
FPAD = 96
QB = 256
TA = 1024
TC = 1024
TD = 1024
NLAG = 84
AHEAD = 2

NORM_EPS = 1e-05
SCALE_EPS = 1e-05
LOG2E = 1.4426950408889634
LN2 = 0.6931471805599453

F32 = jnp.float32
BF16 = jnp.bfloat16


def nn(left, right):
    return lax.dot_general(left, right, (((1,), (0,)), ((), ())), preferred_element_type=F32)


def nt(left, right):
    return lax.dot_general(left, right, (((1,), (1,)), ((), ())), preferred_element_type=F32)


def split(x):
    hi = x.astype(BF16)
    return hi, (x - hi.astype(F32)).astype(BF16)


def split3(x):
    hi = x.astype(BF16)
    rest = x - hi.astype(F32)
    mid = rest.astype(BF16)
    return hi, mid, (rest - mid.astype(F32)).astype(BF16)


def cat3(x):
    hi, lo = split(x)
    return jnp.concatenate([hi, hi, lo], axis=0)


def weight_cat(w):
    hi, lo = split(w)
    hi, lo = hi.astype(F32), lo.astype(F32)
    return jnp.concatenate([hi, lo, hi], axis=0).T.astype(BF16)


def weight_stack(w):
    hi, lo = split(w)
    return jnp.concatenate([hi, lo], axis=0)


def mm_stack(stack, x):
    m = stack.shape[0] // 2
    hi, lo = split(x)
    both = nn(stack, hi)
    return both[:m] + both[m:] + nn(stack[:m], lo)


def outer_sum(left, right):
    m = left.shape[0]
    lh, ll = split(left)
    rh, rl = split(right)
    both = nt(jnp.concatenate([lh, ll], axis=0), rh)
    return both[:m] + both[m:] + nt(lh, rl)


def column(row):
    n = row.shape[0]
    return jnp.broadcast_to(row[None, :], (8, n)).T[:, :1]


def lane_fold(x):
    total = x[:, :128]
    for i in range(1, x.shape[1] // 128):
        total = total + x[:, i * 128 : (i + 1) * 128]
    return total


def rotate(x, cos, sin):
    t = x.shape[1]
    pairs = x.reshape(HEADS, 2, HD // 2, t)
    a, b = pairs[:, 0], pairs[:, 1]
    first = a * cos - b * sin
    second = a * sin + b * cos
    return jnp.stack([first, second], axis=1).reshape(HEADS * HD, t)


def row_scales(scale, nlag):
    row = lax.broadcasted_iota(jnp.int32, (FPAD, 128), 0)
    scales = jnp.broadcast_to(scale, (FPAD, 128))
    inverse, logs = 1.0 / scales, jnp.log(scales)
    return jnp.where(row < nlag, inverse, jnp.where(row == nlag, logs, 1.0))[:, :1]


def prepare_kernel(
    parts, n_in, lag_ref, flag_ref, ids_ref, *refs
):
    sources, refs = refs[:n_in], refs[n_in:]
    scale_ref, feat_ref, w_in, w_qkv, w_out, w_gu, w_down, w_dh, w_dgu, w_dm, w_dqkv, gains, cos_ref, sin_ref = refs[:14]
    own, others, send_sem, recv_sem, fetch_sem, *fetched = refs[14:]
    vals_ref, obs_ref, in_ref, wq_ref, wk_ref, wv_ref, wo_ref, wg_ref, wu_ref, wd_ref, ga_ref, gf_ref = fetched
    fetched = fetched + [cos_ref, sin_ref]
    fetches = [pltpu.make_async_copy(sources[i], fetched[i], fetch_sem.at[i]) for i in range(n_in)]
    for c in fetches:
        c.start()
    n_series, t = vals_ref.shape
    d, nf = in_ref.shape
    nlag = lag_ref.shape[0]
    ff = wg_ref.shape[1]
    for c in fetches[:2]:
        c.wait()
    obs = obs_ref[...].astype(F32)
    both = jnp.concatenate([vals_ref[...] * obs, obs], axis=0)

    g, n = lax.axis_index("group"), lax.axis_index("narrow")
    barrier = pltpu.get_barrier_semaphore()
    copies = []
    for off in range(1, parts):
        peer = (g, lax.rem(n + off, parts))
        pl.semaphore_signal(barrier, inc=1, device_id=peer, device_id_type=pl.DeviceIdType.MESH)
        copies.append(pltpu.make_async_remote_copy(
            src_ref=own, dst_ref=others.at[off - 1], send_sem=send_sem.at[off - 1], recv_sem=recv_sem.at[off - 1],
            device_id=peer, device_id_type=pl.DeviceIdType.MESH,
        ))
    series = lax.broadcasted_iota(jnp.int32, (n_series, 128), 0)
    ids = jnp.zeros((n_series, 128), jnp.int32)
    for s in range(n_series):
        ids = jnp.where(series == s, ids_ref[s], ids)
    member = (lax.broadcasted_iota(jnp.int32, (n_series, 128), 1) == ids).astype(F32)
    magnitude = jnp.sum(jnp.abs(both[:n_series]), axis=1, keepdims=True)
    counted = jnp.sum(obs, axis=1, keepdims=True)
    own[...] = jnp.concatenate([
        jnp.sum(member * magnitude, axis=0, keepdims=True), jnp.sum(member * counted, axis=0, keepdims=True),
        jnp.zeros((6, 128), F32),
    ], axis=0)

    lanes = lax.broadcasted_iota(jnp.int32, both.shape, 1)

    def one_lag(j, missing):
        lag = lag_ref[j]
        moved = jnp.where(lanes >= lag, pltpu.roll(both, lag, 1), 0.0)
        for s in range(n_series):
            feat_ref[s, pl.ds(j, 1), :] = moved[s : s + 1]
        return missing + flag_ref[j].astype(F32) * (1.0 - moved[n_series:])

    missing = lax.fori_loop(0, nlag, one_lag, jnp.zeros((n_series, t), F32), unroll=12)
    for s in range(n_series):
        feat_ref[s, nlag : nlag + 1, :] = jnp.ones((1, t), F32)
        feat_ref[s, nlag + 1 : nlag + 2, :] = missing[s : s + 1] * nlag**-0.5
        feat_ref[s, nlag + 2 :, :] = jnp.zeros((FPAD - nlag - 2, t), F32)

    pl.semaphore_wait(barrier, parts - 1)
    for c in copies:
        c.start()

    for c in fetches[2:]:
        c.wait()
    w_in_rows = jnp.concatenate([in_ref[...].T, jnp.zeros((FPAD - nf, d), F32)], axis=0)
    w_in[...] = weight_cat(w_in_rows)
    for i, ref in enumerate((wq_ref, wk_ref, wv_ref)):
        w_qkv[i * d : (i + 1) * d, :] = weight_cat(ref[...])
        w_dqkv[:, i * d : (i + 1) * d] = weight_stack(ref[...])
    w_out[...] = weight_cat(wo_ref[...])
    w_gu[:ff, :] = weight_cat(wg_ref[...])
    w_gu[ff:, :] = weight_cat(wu_ref[...])
    w_down[...] = weight_stack(wd_ref[...])
    w_dh[...] = weight_cat(wd_ref[...])
    w_dgu[:, :ff] = weight_stack(wg_ref[...])
    w_dgu[:, ff:] = weight_stack(wu_ref[...])
    w_dm[...] = weight_cat(wo_ref[...].T)
    gains[...] = jnp.zeros_like(gains)
    gains[:, :1] = column(ga_ref[...])
    gains[:, 1:2] = column(gf_ref[...])

    for c in copies:
        c.wait()
    total = own[...]
    for i in range(parts - 1):
        total = total + others[i]
    set_scale = total[:1] / jnp.maximum(total[1:2], 1.0) + SCALE_EPS
    series_scale = jnp.sum(jnp.where(member > 0.0, set_scale, 0.0), axis=1, keepdims=True)
    scale_ref[...] = jnp.broadcast_to(series_scale, scale_ref.shape)


def forward_kernel(
    scale_ref, feat_ref, w_in, w_qkv, w_out, w_gu, w_down, w_dh, w_dgu, w_dm, gains, cos_ref, sin_ref, cot_ref,
    act_ref, q_ref, k_ref, v_ref, dm_ref, st_ref, da_ref, x_ref, b1_ref,
    mixed_ref, g_gu, g_down, g_out, g_gf, cot_buf, cot_sem,
):
    step = pl.program_id(0)
    d, t = cot_ref.shape[1], cot_ref.shape[2]

    def fetch(i):
        return pltpu.make_async_copy(cot_ref.at[i], cot_buf.at[i % 2], cot_sem.at[i % 2])

    ff = w_dh.shape[0]
    gain_attn, gain_ffn = gains[:, :1], gains[:, 1:2]
    scales = row_scales(scale_ref[pl.ds(step, 1), :], NLAG)

    @pl.when(step == 0)
    def _():
        fetch(0).start()
        for ref in (g_gu, g_down, g_out, g_gf):
            ref[...] = jnp.zeros_like(ref)

    @pl.when(step + 1 < pl.num_programs(0))
    def _():
        fetch(step + 1).start()

    st_ref[0] = jnp.zeros(st_ref.shape[1:], F32)

    def project(i, _):
        cols = pl.ds(pl.multiple_of(i * TA, TA), TA)
        x = nn(w_in[...], cat3(feat_ref[0, :, cols] * scales))
        x_ref[0, :, cols] = x
        normed = x * lax.rsqrt(jnp.mean(x * x, axis=0, keepdims=True) + NORM_EPS) * gain_attn
        qkv = nn(w_qkv[...], cat3(normed))
        cos, sin = cos_ref[:, cols], sin_ref[:, cols]
        q_ref[0, :, cols] = rotate(qkv[:d], cos, sin) * (HD**-0.5 * LOG2E)
        k_ref[0, :, cols] = rotate(qkv[d : 2 * d], cos, sin)
        v_ref[0, :, cols] = qkv[2 * d :]
        return 0

    lax.fori_loop(0, t // TA, project, 0)

    causal = lax.broadcasted_iota(jnp.int32, (QB, QB), 0) <= lax.broadcasted_iota(jnp.int32, (QB, QB), 1)

    def prepare(h):
        rows = slice(h * HD, (h + 1) * HD)
        qh, ql = split(q_ref[0, rows, :])
        qc = jnp.concatenate([qh, ql, qh], axis=0)
        kh, kl = split(k_ref[0, rows, :])
        kh, kl = kh.astype(F32), kl.astype(F32)
        kc = jnp.concatenate([kh, kh, kl], axis=0).T.astype(BF16)
        vh, vl = split(v_ref[0, rows, :])
        return qc, kc, jnp.concatenate([vh, vl], axis=0), vh

    def scores(sides, item):
        qc, kc = sides[:2]
        lo, top = item[1] * QB, (item[1] + 1) * QB
        return nn(kc[:top], qc[:, lo:top])

    def softmax(s, block):
        lo = block * QB
        last = jnp.where(causal, s[lo:], -1e30)
        s = jnp.concatenate([s[:lo], last], axis=0) if block else last
        return s, jnp.max(s, axis=0, keepdims=True)

    def mix(sides, soft, item):
        h, block = item
        vs, vh = sides[2:]
        s, m = soft
        lo, top = block * QB, (block + 1) * QB
        both = low = total = 0.0
        for c in range(block + 1):
            keys = slice(c * QB, (c + 1) * QB)
            p = jnp.exp2(s[keys] - m)
            total = total + jnp.sum(p, axis=0, keepdims=True)
            ph, pl_ = split(p)
            both = both + nn(vs[:, keys], ph)
            low = low + nn(vh[:, keys], pl_)
        mixed_ref[h * HD : (h + 1) * HD, lo:top] = (both[:HD] + both[HD:] + low) / total
        st_ref[0, h : h + 1, lo:top] = m + jnp.log2(total)

    sides = [prepare(h) for h in range(HEADS)]
    items = [(h, block) for block in reversed(range(t // QB)) for h in range(HEADS)]
    ahead = {}
    for j in range(len(items) + AHEAD):
        if j < len(items):
            ahead[j] = scores(sides[items[j][0]], items[j])
        if j >= AHEAD:
            item = items[j - AHEAD]
            mix(sides[item[0]], softmax(ahead.pop(j - AHEAD), item[1]), item)

    fetch(step).wait()

    def feed(i, _):
        cols = pl.ds(pl.multiple_of(i * TC, TC), TC)
        mixed = mixed_ref[:, cols]
        attended = x_ref[0, :, cols] + nn(w_out[...], cat3(mixed))
        r2 = lax.rsqrt(jnp.mean(attended * attended, axis=0, keepdims=True) + NORM_EPS)
        scaled = attended * r2
        normed2 = scaled * gain_ffn
        gu = nn(w_gu[...], cat3(normed2))
        gate, up = gu[:ff], gu[ff:]
        sig = 1.0 / (1.0 + jnp.exp(-gate))
        silu = gate * sig
        hidden = silu * up
        act_ref[0, :, cols] = attended + mm_stack(w_down[...], hidden)

        g = cot_buf[step % 2, :, cols]
        dh = nn(w_dh[...], cat3(g))
        dgate = dh * up * (sig + silu * (1.0 - sig))
        dup = dh * silu
        dgu = jnp.concatenate([dgate, dup], axis=0)
        dn2 = mm_stack(w_dgu[...], dgu)
        g_down[...] += outer_sum(hidden, g)
        g_gu[...] += outer_sum(dgu, normed2)
        weighted = dn2 * gain_ffn
        inner = jnp.mean(weighted * attended, axis=0, keepdims=True)
        da = g + r2 * weighted - attended * (r2 * r2 * r2 * inner)
        da_ref[0, :, cols] = da
        g_gf[...] += lane_fold(dn2 * scaled)
        g_out[...] += outer_sum(mixed, da)
        dm = nn(w_dm[...], cat3(da))
        dm_ref[0, :, cols] = dm
        prod = (dm * mixed).reshape(HEADS, HD, TC)
        for h in range(HEADS):
            st_ref[0, 16 + h : 17 + h, cols] = jnp.sum(prod[h], axis=0, keepdims=True)
        return 0

    lax.fori_loop(0, t // TC, feed, 0)

    @pl.when(step == pl.num_programs(0) - 1)
    def _():
        parts = 2 * b1_ref.shape[0]
        fs, ds = ff // parts, d // parts
        g_gu_t = g_gu[...].T
        g_down_t = g_down[...].T
        g_out_t = g_out[...].T
        gf = jnp.sum(g_gf[...], axis=1, keepdims=True)
        for n in range(parts):
            gf_own = jnp.concatenate([gf[n * ds : (n + 1) * ds], jnp.zeros((d - ds, 1), F32)], axis=0)
            share = jnp.concatenate([
                g_gu_t[:, n * fs : (n + 1) * fs], g_gu_t[:, ff + n * fs : ff + (n + 1) * fs],
                g_down_t[:, n * fs : (n + 1) * fs], g_out_t[:, n * ds : (n + 1) * ds], gf_own,
            ], axis=1)
            b1_ref[n // 2, n % 2] = stack_columns(share, b1_ref.shape[2])


def stack_columns(share, height):
    rows, cols = share.shape
    pad_cols = -cols % 128
    if pad_cols:
        share = jnp.concatenate([share, jnp.zeros((rows, pad_cols), F32)], axis=1)
    pieces = [share[:, c * 128 : (c + 1) * 128] for c in range(share.shape[1] // 128)]
    left = height - len(pieces) * rows
    if left:
        pieces.append(jnp.zeros((left, 128), F32))
    return jnp.concatenate(pieces, axis=0)


def at(group, narrow):
    return (group, narrow)


def plane_peers(groups, ny):
    g, n = lax.axis_index("group"), lax.axis_index("narrow")
    core, y = lax.rem(n, 2), lax.div(n, 2)
    for i in range(1, ny * groups):
        peer_y, peer_g = lax.rem(y + i // groups, ny), lax.rem(g + i % groups, groups)
        yield i, peer_y, peer_g, at(peer_g, peer_y * 2 + core)


def greet(groups, ny):
    g, n = lax.axis_index("group"), lax.axis_index("narrow")
    core, y = lax.rem(n, 2), lax.div(n, 2)
    barrier = pltpu.get_barrier_semaphore()
    peers = [at(g, y * 2 + 1 - core)] + [peer for _, _, _, peer in plane_peers(groups, ny)]
    for peer in peers:
        pl.semaphore_signal(barrier, inc=1, device_id=peer, device_id_type=pl.DeviceIdType.MESH)
    pl.semaphore_wait(barrier, len(peers))


def share_phases(src, total_ref, base, recv1, pair, recv2, send_sem, recv_sem):
    ny, groups, chunk = pair.shape[:3]
    g, n = lax.axis_index("group"), lax.axis_index("narrow")
    core, y = lax.rem(n, 2), lax.div(n, 2)

    def copy(i, source, target, to):
        return pltpu.make_async_remote_copy(
            src_ref=source, dst_ref=target, send_sem=send_sem.at[i], recv_sem=recv_sem.at[i], device_id=to,
            device_id_type=pl.DeviceIdType.MESH,
        )

    def over_core():
        return [copy(0, src.at[:, 1 - core], recv1, at(g, y * 2 + 1 - core))]

    def over_plane():
        return [copy(i, pair.at[py, pg], recv2.at[i], peer) for i, py, pg, peer in plane_peers(groups, ny)]

    def gather():
        own = total_ref.at[g, pl.ds(base, chunk)]
        peers = [lax.rem(g + off, groups) for off in range(1, groups)]
        return [copy(ny * groups + i, own, own, at(p, n)) for i, p in enumerate(peers)]

    def start(copies):
        for c in copies:
            c.start()

    def arrive(copies):
        for c in copies:
            c.wait_recv()

    def one():
        start(over_core())

    def two():
        arrive(over_core())
        for i in range(ny):
            pair[i] = (src[i, core] + recv1[i]).reshape(groups, chunk, 128)
        start(over_plane())

    def three():
        recv2[0] = pair[y, g]
        arrive(over_plane())
        total_ref[g, base : base + chunk] = jnp.sum(recv2[...], axis=0)
        start(gather())

    def four():
        arrive(gather())
        for copies in (over_core(), over_plane(), gather()):
            for c in copies:
                c.wait_send()

    return one, two, three, four


def backward_kernel(
    dx_steps, scale_ref, q_ref, k_ref, v_ref, dm_ref, st_ref, da_ref, x_ref, feat_ref, w_dqkv, gains, cos_ref, sin_ref, b1_ref,
    dx_ref, out_ref,
    dqkv_ref, g_qkv, g_in, g_ga, b2_ref, total_ref, *buffers,
):
    step = pl.program_id(0)
    early = share_phases(b1_ref, total_ref, 0, *buffers[:5])
    late = share_phases(b2_ref, total_ref, b1_ref.shape[2] // total_ref.shape[0], *buffers[5:])

    @pl.when(step == 0)
    def _():
        greet(total_ref.shape[0], b1_ref.shape[0])

    for i, phase in enumerate(early[:3]):

        @pl.when(step == min(i, dx_steps - 1))
        def _():
            phase()

    d, t = q_ref.shape[1], q_ref.shape[2]

    @pl.when(step == 0)
    def _():
        for ref in (g_qkv, g_in, g_ga):
            ref[...] = jnp.zeros_like(ref)

    nb = t // QB
    causal = lax.broadcasted_iota(jnp.int32, (QB, QB), 0) >= lax.broadcasted_iota(jnp.int32, (QB, QB), 1)
    ones = (lax.broadcasted_iota(jnp.int32, (HD, t), 0) < 3).astype(BF16)

    def extras(row):
        a, b, c = split3(row)
        pieces = jnp.concatenate([a.astype(F32), b.astype(F32), c.astype(F32)], axis=0)
        return jnp.concatenate([pieces, jnp.zeros((HD - 3, t), F32)], axis=0)

    def sides(block, row):
        hi, lo = split(block)
        hf, lf = hi.astype(F32), lo.astype(F32)
        tall = jnp.concatenate([hf, lf, hf, extras(-row)], axis=0).T.astype(BF16)
        return tall, jnp.concatenate([hi, lo], axis=0), hi

    def rows_at(first, h):
        return slice(first + h * HD, first + (h + 1) * HD)

    def prepare(h):
        rows = rows_at(0, h)
        qc, qs, qh = sides(q_ref[0, rows, :], st_ref[0, h : h + 1, :])
        mc, ms, mh = sides(dm_ref[0, rows, :], st_ref[0, 16 + h : 17 + h, :])
        kh, kl = split(k_ref[0, rows, :])
        kc = jnp.concatenate([kh, kh, kl, ones], axis=0)
        vh, vl = split(v_ref[0, rows, :])
        vc = jnp.concatenate([vh, vh, vl, ones], axis=0)
        return qc, mc, kc, vc, qs, qh, ms, mh, jnp.concatenate([kh, kl], axis=0), kh

    def tile(item):
        h, kb, qb = item
        return h, slice(kb * QB, (kb + 1) * QB), slice(qb * QB, (qb + 1) * QB)

    def scores(item):
        h, keys, steps = tile(item)
        qc, mc, kc, vc = prepared[h][:4]
        return nn(qc[steps], kc[:, keys]), nn(mc[steps], vc[:, keys])

    def differentiate(item, s, dp):
        h, keys, steps = tile(item)
        kb, qb = item[1:]
        qs, qh, ms, mh, ks, kh = prepared[h][4:]
        p = jnp.exp2(s)
        if kb == qb:
            p = jnp.where(causal, p, 0.0)
        ds = p * dp
        ph, pl_ = split(p)
        dh, dl = split(ds)
        th, tl = split(ds.T)
        both = nn(ms[:, steps], ph)
        dv = both[:HD] + both[HD:] + nn(mh[:, steps], pl_)
        both = nn(qs[:, steps], dh)
        dk = both[:HD] + both[HD:] + nn(qh[:, steps], dl)
        if qb > kb:
            dk, dv = dk + sums[h][0], dv + sums[h][1]
        sums[h] = dk, dv
        if qb == nb - 1:
            dqkv_ref[rows_at(d, h), keys] = dk
            dqkv_ref[rows_at(2 * d, h), keys] = dv
        both = nn(ks[:, keys], th)
        dq = both[:HD] + both[HD:] + nn(kh[:, keys], tl)
        if kb == qb:
            dqkv_ref[rows_at(0, h), steps] = dq
        else:
            dqkv_ref[rows_at(0, h), steps] += dq

    prepared = [prepare(h) for h in range(HEADS)]
    sums = {}
    items = [(h, kb, qb) for kb in reversed(range(nb)) for h in range(HEADS) for qb in range(kb, nb)]
    ahead = {}
    for j in range(len(items) + AHEAD):
        if j < len(items):
            ahead[j] = scores(items[j])
        if j >= AHEAD:
            differentiate(items[j - AHEAD], *ahead.pop(j - AHEAD))

    gain = gains[:, :1]
    scales = row_scales(scale_ref[pl.ds(step, 1), :], NLAG)

    def finish(i, _):
        cols = pl.ds(pl.multiple_of(i * TD, TD), TD)
        cos, sin = cos_ref[:, cols], -sin_ref[:, cols]
        dq = rotate(dqkv_ref[:d, cols], cos, sin) * HD**-0.5
        dk = rotate(dqkv_ref[d : 2 * d, cols], cos, sin) * LN2
        dqkv = jnp.concatenate([dq, dk, dqkv_ref[2 * d :, cols]], axis=0)
        x = x_ref[0, :, cols]
        r = lax.rsqrt(jnp.mean(x * x, axis=0, keepdims=True) + NORM_EPS)
        xr = x * r
        dn = mm_stack(w_dqkv[...], dqkv)
        g_qkv[...] += outer_sum(dqkv, xr * gain)
        weighted = dn * gain
        inner = jnp.mean(weighted * x, axis=0, keepdims=True)
        dx = da_ref[0, :, cols] + r * weighted - x * (r * r * r * inner)
        dx_ref[0, :, cols] = dx
        g_ga[...] += lane_fold(dn * xr)
        g_in[...] += outer_sum(dx, feat_ref[0, :, cols] * scales)
        return 0

    lax.fori_loop(0, t // TD, finish, 0)

    @pl.when(step == pl.num_programs(0) - 1)
    def _():
        parts = 2 * b2_ref.shape[0]
        ds = d // parts
        g_qkv_t = g_qkv[...].T
        ga = jnp.sum(g_ga[...], axis=1, keepdims=True)
        for n in range(parts):
            own = slice(n * ds, (n + 1) * ds)
            share = jnp.concatenate([g_qkv_t[own], g_in[own, :], ga[own]], axis=1)
            b2_ref[n // 2, n % 2] = stack_columns(share, b2_ref.shape[2])
        for phase in late[:3]:
            phase()
        for end in (early[3], late[3]):
            end()
        out_ref[...] = total_ref[...]


def unpack_kernel(total_ref, dx_ref, dx_out, *refs):
    grads, sems = refs[:-1], refs[-1]
    copies = [pltpu.make_async_copy(dx_ref.at[i], dx_out.at[i], sems.at[i]) for i in range(dx_ref.shape[0])]
    for c in copies:
        c.start()
    unpack(total_ref, *grads)
    for c in copies:
        c.wait()


def unpack(total_ref, g_in, g_ga, g_q, g_k, g_v, g_out, g_gf, g_gate, g_up, g_down):
    d, fs = g_gate.shape
    ds, nf = g_in.shape
    groups = total_ref.shape[0]
    wide = round_up(3 * fs + ds + 1, 128) // 128
    c1 = round_up(wide * d, 8 * groups) // groups
    one = jnp.concatenate([total_ref[g, :c1] for g in range(groups)], axis=0)
    one = jnp.concatenate([one[c * d : (c + 1) * d, :] for c in range(wide)], axis=1)
    g_gate[...] = one[:, :fs]
    g_up[...] = one[:, fs : 2 * fs]
    g_down[...] = one[:, 2 * fs : 3 * fs]
    g_out[...] = one[:, 3 * fs : 3 * fs + ds].T
    g_gf[...] = one[:ds, 3 * fs + ds]
    wide = round_up(3 * d + FPAD + 1, 128) // 128
    two = jnp.concatenate([total_ref[g, c1:] for g in range(groups)], axis=0)
    two = jnp.concatenate([two[c * ds : (c + 1) * ds, :] for c in range(wide)], axis=1)
    g_q[...] = two[:, :d]
    g_k[...] = two[:, d : 2 * d]
    g_v[...] = two[:, 2 * d : 3 * d]
    g_in[...] = two[:, 3 * d : 3 * d + nf]
    g_ga[...] = two[:, 3 * d + FPAD]


def rotation_tables(t):
    freqs = 10000.0 ** (-np.arange(HD // 2, dtype=np.float64) * 2.0 / HD)
    angles = freqs[:, None] * np.arange(t, dtype=np.float64)[None, :]
    return np.cos(angles).astype(np.float32), np.sin(angles).astype(np.float32)


def in_hbm(x):
    return pltpu.with_memory_space_constraint(x, pltpu.HBM)


def round_up(n, m):
    return (n + m - 1) // m * m


def on_device(
    groups, parts, series_values, observed, lag_steps, lag_flags, dataset_ids, in_proj, gain_attn, query_proj, key_proj,
    value_proj, out_proj, gain_ffn, gate_proj, up_proj, down_proj, cotangent,
):
    n_series, t = series_values.shape
    nf, d = in_proj.shape
    ff = gate_proj.shape[1]
    fs, ds = ff // parts, d // parts
    cos, sin = rotation_tables(t)
    cos, sin = jnp.asarray(cos), jnp.asarray(sin)
    smem = pl.BlockSpec(memory_space=pltpu.SMEM)
    vmem = pl.BlockSpec(memory_space=pltpu.VMEM)

    def whole(a):
        return pl.BlockSpec(a.shape, lambda i: (0,) * a.ndim)

    def each(rows):
        return pl.BlockSpec((1, rows, t), lambda i: (i, 0, 0))

    def shape(*dims, dtype=F32):
        return jax.ShapeDtypeStruct(dims, dtype)

    params = pltpu.CompilerParams(dimension_semantics=("arbitrary",), vmem_limit_bytes=28 * 2**20)
    plain = pltpu.CompilerParams(vmem_limit_bytes=62 * 2**20)
    in_t, down_t = in_proj.T, down_proj.T
    hbm = pl.BlockSpec(memory_space=pltpu.HBM)
    sources = [series_values, observed, in_t, query_proj, key_proj, value_proj, out_proj, gate_proj, up_proj, down_t,
               gain_attn, gain_ffn, cos, sin]
    series_scale, raw, w_in, w_qkv, w_out, w_gu, w_down, w_dh, w_dgu, w_dm, w_dqkv, gains, cos, sin = pl.pallas_call(
        functools.partial(prepare_kernel, parts, len(sources)),
        in_specs=[smem] * 3 + [hbm] * len(sources),
        out_specs=[vmem] * 14,
        out_shape=[
            shape(n_series, 128),
            shape(n_series, FPAD, t),
            shape(d, 3 * FPAD, dtype=BF16),
            shape(3 * d, 3 * d, dtype=BF16),
            shape(d, 3 * d, dtype=BF16),
            shape(2 * ff, 3 * d, dtype=BF16),
            shape(2 * d, ff, dtype=BF16),
            shape(ff, 3 * d, dtype=BF16),
            shape(2 * d, 2 * ff, dtype=BF16),
            shape(d, 3 * d, dtype=BF16),
            shape(2 * d, 3 * d, dtype=BF16),
            shape(d, 128),
            shape(*cos.shape),
            shape(*sin.shape),
        ],
        scratch_shapes=[
            pltpu.VMEM((8, 128), F32),
            pltpu.VMEM((parts - 1, 8, 128), F32),
            pltpu.SemaphoreType.DMA((parts - 1,)),
            pltpu.SemaphoreType.DMA((parts - 1,)),
            pltpu.SemaphoreType.DMA((len(sources),)),
            *[pltpu.VMEM(a.shape, a.dtype) for a in sources[:12]],
        ],
        compiler_params=pltpu.CompilerParams(vmem_limit_bytes=20 * 2**20, collective_id=1, has_side_effects=True),
        name="sums_weights_and_lags",
    )(*[in_hbm(a) for a in (lag_steps, lag_flags, dataset_ids, *sources)])

    rows1 = round_up(round_up(3 * fs + ds + 1, 128) // 128 * d, 8 * groups)
    rows2 = round_up(round_up(3 * d + FPAD + 1, 128) // 128 * ds, 8 * groups)
    full = [w_in, w_qkv, w_out, w_gu, w_down, w_dh, w_dgu, w_dm, gains, cos, sin]
    b1 = shape(parts // 2, 2, rows1, 128)
    act, q, k, v, dm, st, da, x, b1 = pl.pallas_call(
        forward_kernel,
        grid=(n_series,),
        in_specs=[whole(series_scale), each(FPAD)] + [whole(a) for a in full] + [hbm],
        out_specs=[each(d)] * 5 + [each(32)] + [each(d)] * 2 + [whole(b1)],
        out_shape=[shape(n_series, d, t)] * 5 + [shape(n_series, 32, t)] + [shape(n_series, d, t)] * 2 + [b1],
        scratch_shapes=[
            pltpu.VMEM((d, t), F32),
            pltpu.VMEM((2 * ff, d), F32),
            pltpu.VMEM((ff, d), F32),
            pltpu.VMEM((d, d), F32),
            pltpu.VMEM((d, 128), F32),
            pltpu.VMEM((2, d, t), F32),
            pltpu.SemaphoreType.DMA((2,)),
        ],
        compiler_params=params,
        name="forward_and_ffn",
    )(series_scale, raw, *full, in_hbm(jnp.transpose(cotangent, (0, 2, 1))))

    ny = parts // 2
    c1, c2 = rows1 // groups, rows2 // groups
    total = shape(groups, c1 + c2, 128)
    full = [w_dqkv, gains, cos, sin, b1]
    copies = ny * groups + groups - 1
    dma = pltpu.SemaphoreType.DMA
    buffers = []
    for rows, chunk in ((rows1, c1), (rows2, c2)):
        buffers += [
            pltpu.VMEM((ny, rows, 128), F32),
            pltpu.VMEM((ny, groups, chunk, 128), F32),
            pltpu.VMEM((ny * groups, chunk, 128), F32),
            dma((copies,)),
            dma((copies,)),
        ]
    dx, total = pl.pallas_call(
        functools.partial(backward_kernel, n_series),
        grid=(n_series,),
        in_specs=[whole(series_scale)] + [each(d)] * 4 + [each(32)] + [each(d)] * 2 + [each(FPAD)] + [whole(a) for a in full],
        out_specs=[each(d), whole(total)],
        out_shape=[shape(n_series, d, t), total],
        scratch_shapes=[
            pltpu.VMEM((3 * d, t), F32),
            pltpu.VMEM((3 * d, d), F32),
            pltpu.VMEM((d, FPAD), F32),
            pltpu.VMEM((d, 128), F32),
            pltpu.VMEM((ny, 2, rows2, 128), F32),
            pltpu.VMEM((groups, c1 + c2, 128), F32),
            *buffers,
        ],
        compiler_params=pltpu.CompilerParams(
            dimension_semantics=("arbitrary",), vmem_limit_bytes=28 * 2**20, collective_id=0, has_side_effects=True
        ),
        name="attention_backward_and_sums",
    )(series_scale, q, k, v, dm, st, da, x, raw, *full)

    grads = [
        shape(ds, nf), shape(ds), shape(ds, d), shape(ds, d), shape(ds, d), shape(ds, d), shape(ds),
        shape(d, fs), shape(d, fs), shape(d, fs),
    ]
    dx, *grads = pl.pallas_call(
        unpack_kernel,
        in_specs=[vmem, vmem],
        out_specs=[hbm] + [vmem] * len(grads),
        out_shape=[shape(n_series, d, t)] + grads,
        scratch_shapes=[dma((n_series,))],
        compiler_params=pltpu.CompilerParams(vmem_limit_bytes=28 * 2**20),
        name="unpack_gradients",
    )(total, dx)
    return (
        jnp.transpose(act, (0, 2, 1)),
        jnp.transpose(dx, (0, 2, 1)),
        grads[0].T,
        *grads[1:9],
        grads[9].T,
    )


def solution(mesh):
    series = P(("group", "narrow"), None)
    return jax.shard_map(
        functools.partial(on_device, mesh.shape["group"], mesh.shape["narrow"]),
        mesh=mesh,
        in_specs=(series, series, P(), P(), P(("group", "narrow"))) + (P(),) * 10 + (P(("group", "narrow"), None, None),),
        out_specs=(
            P(("group", "narrow"), None, None),
            P(("group", "narrow"), None, None),
            P(None, "narrow"),
            P("narrow"),
            P("narrow", None),
            P("narrow", None),
            P("narrow", None),
            P("narrow", None),
            P("narrow"),
            P(None, "narrow"),
            P(None, "narrow"),
            P("narrow", None),
        ),
        check_vma=False,
    )
```
